32 devices in a mesh: dp: 8 (over z, x), seq: 4 (over y, core).
Axes of the slice: x: 2, y: 2, z: 4, core: 2. Of those that a mesh axis runs over, the one named last changes fastest.
Arguments:
- inputs: bfloat16 [8, 1024, 768], P('dp', 'seq'), may hold values from -6 to 6
- w_query: bfloat16 [768, 768], replicated, may hold values from -0.21875 to 0.21875
- query_bias: bfloat16 [768], replicated, may hold values from -4 to 4
- w_key: bfloat16 [768, 768], replicated, may hold values from -0.21875 to 0.21875
- w_value: bfloat16 [768, 768], replicated, may hold values from -0.21875 to 0.21875
- value_bias: bfloat16 [768], replicated, may hold values from -0.75 to 0.75
- w_proj: bfloat16 [768, 768], replicated, may hold values from -3 to 3
- proj_bias: bfloat16 [768], replicated, may hold values from -4 to 4
- ln1_gain: bfloat16 [768], replicated, may hold values from 0.5 to 1.5
- ln1_bias: bfloat16 [768], replicated, may hold values from -4 to 4
- w_up: bfloat16 [768, 3072], replicated, may hold values from -0.21875 to 0.21875
- up_bias: bfloat16 [3072], replicated, may hold values from -4 to 4
- w_down: bfloat16 [3072, 768], replicated, may hold values from -0.109375 to 0.109375
- down_bias: bfloat16 [768], replicated, may hold values from -4 to 4
- ln2_gain: bfloat16 [768], replicated, may hold values from 0.5 to 1.5
- ln2_bias: bfloat16 [768], replicated, may hold values from -4 to 4
- long_group: int32 [8], P('dp'), may hold values from 0 to 1, as said below
- random_blocks: int32 [8, 16, 3], P('dp', 'seq'), may hold values from 1 to 14, as said below
- out_grad: bfloat16 [8, 1024, 768], P('dp', 'seq'), may hold values from -6 to 6
Outputs:
- layer_out: bfloat16 [8, 1024, 768], P('dp', 'seq')
- input_grad: float32 [8, 1024, 768], P('dp', 'seq')
- grad_w_query: float32 [768, 768], P('seq')
- grad_w_key: float32 [768, 768], P('seq')
- grad_w_value: float32 [768, 768], P('seq')
- grad_w_proj: float32 [768, 768], P('seq')
- grad_w_up: float32 [768, 3072], P('seq')
- grad_w_down: float32 [3072, 768], P('seq')
- grad_query_bias: float32 [768], replicated
- grad_value_bias: float32 [768], replicated
- grad_proj_bias: float32 [768], replicated
- grad_ln1_gain: float32 [768], replicated
- grad_ln1_bias: float32 [768], replicated
- grad_up_bias: float32 [3072], replicated
- grad_down_bias: float32 [768], replicated
- grad_ln2_gain: float32 [768], replicated
- grad_ln2_bias: float32 [768], replicated
The draws below stay inside these ranges and needn't reach their ends.
Inputs may be any that keep to these rules, and one draw needn't show every extreme that they name: `long_group`: 1 marks a group holding one sequence of 1024 tokens, 0 a group holding 2 sequences of 512 tokens. `random_blocks`: for a block at relative position p of its sequence of n blocks, the 3 entries are distinct positions of the same sequence, none of them 0, n - 1, p - 1, p or p + 1; the entries of global blocks are not used.
All inputs are finite; a program needn't handle non-finite values.
Results may differ from the reference program's by a relative error of at most 0.018.
Values may be sent and summed in bfloat16 or wider, within the bound.
No kernel may reach another device: no remote copies, remote signals or barrier semaphores. Data moves between devices by JAX's collectives and lax.ppermute only.
A program may use at most 192 MiB of HBM per device.

```python
from functools import partial
import jax
import jax.numpy as jnp
from jax import lax

D = 768
HEADS = 12
HEAD = 64
FF = 3072
BLOCK = 64
RAND = 3
SLOTS = 2
SLOT_TOK = 128
T_DEV = 256
GROUP_TOK = 1024
GROUPS = 8
N_SEQ = 4


def bucket_flags(key):
    shuffled = jax.random.permutation(key, GROUPS)
    return (shuffled % 2).astype(jnp.int32)


def draw_long_group(key, part):
    return bucket_flags(key)


def draw_random_blocks(key, part):
    flags = bucket_flags(key)
    key = jax.random.fold_in(key, 7)
    per_slot = SLOT_TOK // BLOCK
    per_dev = T_DEV // BLOCK
    total_blocks = GROUP_TOK // BLOCK
    blocks = jnp.arange(total_blocks, dtype=jnp.int32)
    device = blocks // per_dev
    within = blocks % per_dev
    long_flag = flags[:, None] == 1
    position = jnp.where(long_flag, blocks[None, :], (device * per_slot + within % per_slot)[None, :])
    seq_blocks = jnp.where(long_flag, total_blocks, total_blocks // SLOTS)
    candidates = jnp.arange(total_blocks, dtype=jnp.int32)[None, None, :]
    position_b = position[:, :, None]
    seq_end = seq_blocks[:, :, None]
    banned = (candidates >= seq_end) | (candidates == 0) | (candidates == seq_end - 1)
    banned = banned | (jnp.abs(candidates - position_b) <= 1)
    random_score = jax.random.randint(key, (GROUPS, total_blocks, total_blocks), 0, 1 << 16) * total_blocks + candidates
    ranked = jnp.where(banned, -1 - candidates, random_score)
    ignored, picked = lax.top_k(ranked, RAND)
    return picked.astype(jnp.int32)


def levels(key, extent, split, smallest, high):
    loudness = 1.0
    for dim, parts in split:
        heights = jax.random.uniform(jax.random.fold_in(jax.random.fold_in(key, 6), dim), (parts,), jnp.float32, smallest / len(split), high / len(split))
        loudness = loudness * jnp.repeat(jnp.exp(heights), extent[dim] // parts).reshape((-1,) + (1,) * (len(extent) - 1 - dim))
    return loudness


def gaussian(stream_key, extent, deviation, limit, shards=(), held_as=jnp.bfloat16):
    entries = deviation * jax.random.normal(stream_key, extent, jnp.float32)
    if shards:
        entries = entries * levels(stream_key, extent, shards, -0.22, 0.18)
    return jnp.clip(entries, -limit, limit).astype(held_as)


def setup_inputs(seed: int = 0) -> dict:
    arg_keys = jax.random.split(jax.random.key(seed), 20)
    inputs = gaussian(arg_keys[0], (GROUPS, GROUP_TOK, D), 1.0, 6.0, ((0, 8), (1, 4)))
    w_query = gaussian(arg_keys[1], (D, D), D ** -0.5, 0.21875)
    query_bias = gaussian(arg_keys[2], (D,), 1.0, 4.0)
    w_key = gaussian(arg_keys[3], (D, D), D ** -0.5, 0.21875)
    w_value = gaussian(arg_keys[4], (D, D), D ** -0.5, 0.21875)
    value_bias = gaussian(arg_keys[5], (D,), 0.05, 0.75)
    w_proj = gaussian(arg_keys[6], (D, D), 4 ** -0.5, 3.0)
    proj_bias = gaussian(arg_keys[7], (D,), 0.5, 4.0)
    ln1_gain = jnp.clip(1.0 + 0.1 * jax.random.normal(arg_keys[8], (D,), jnp.float32), 0.5, 1.5).astype(jnp.bfloat16)
    ln1_bias = gaussian(arg_keys[9], (D,), 0.3, 4.0)
    w_up = gaussian(arg_keys[10], (D, FF), D ** -0.5, 0.21875)
    up_bias = gaussian(arg_keys[11], (FF,), 0.5, 4.0)
    w_down = gaussian(arg_keys[12], (FF, D), FF ** -0.5, 0.109375)
    down_bias = gaussian(arg_keys[13], (D,), 0.5, 4.0)
    ln2_gain = jnp.clip(1.0 + 0.1 * jax.random.normal(arg_keys[14], (D,), jnp.float32), 0.5, 1.5).astype(jnp.bfloat16)
    ln2_bias = gaussian(arg_keys[15], (D,), 0.3, 4.0)
    long_group = draw_long_group(jax.random.fold_in(arg_keys[19], 71), 0)
    random_blocks = draw_random_blocks(jax.random.fold_in(arg_keys[19], 71), 0)
    out_grad = gaussian(arg_keys[18], (GROUPS, GROUP_TOK, D), 1.0, 6.0, ((0, 8), (1, 4)))
    return dict(inputs=inputs, w_query=w_query, query_bias=query_bias, w_key=w_key, w_value=w_value, value_bias=value_bias, w_proj=w_proj, proj_bias=proj_bias, ln1_gain=ln1_gain, ln1_bias=ln1_bias, w_up=w_up, up_bias=up_bias, w_down=w_down, down_bias=down_bias, ln2_gain=ln2_gain, ln2_bias=ln2_bias, long_group=long_group, random_blocks=random_blocks, out_grad=out_grad)


LN_EPS = 1e-05
MASKED = -1e+30
PRECISE = lax.Precision.HIGHEST

@jax.custom_vjp
def low(v):
    return lax.optimization_barrier(v.astype(jnp.bfloat16)).astype(jnp.float32)

@jax.custom_vjp
def low_back(v):
    return v

def low_keep(v):
    return (low(v), None)

def low_pass(kept, grad):
    return (grad,)

def back_keep(v):
    return (v, None)

def back_low(kept, grad):
    return (low(grad),)
low.defvjp(low_keep, low_pass)
low_back.defvjp(back_keep, back_low)

def layer_norm(residual, ln_gain, ln_shift):
    center = residual - lax.optimization_barrier(jnp.mean(residual, axis=-1, keepdims=True))
    variance = lax.optimization_barrier(jnp.mean(center * center, axis=-1, keepdims=True))
    return center * lax.rsqrt(variance + LN_EPS) * ln_gain + ln_shift

def matmul_hi(left, right):
    return jnp.dot(left, right, precision=PRECISE)

def seq_coords(blocks, is_long, per_slot, per_dev):
    device = blocks // per_dev
    within = blocks % per_dev
    slot_id = jnp.where(is_long, 0, within // per_slot).astype(jnp.int32)
    position = jnp.where(is_long, blocks, device * per_slot + within % per_slot).astype(jnp.int32)
    return (slot_id, position)

def to_group(slot_id, position, is_long, per_slot, per_dev):
    placed = position // per_slot * per_dev + slot_id * per_slot + position % per_slot
    return jnp.where(is_long, position, placed).astype(jnp.int32)

def key_plan(blocks, chosen, is_long, per_slot, per_dev, total_blocks):
    slot_id, position = seq_coords(blocks, is_long, per_slot, per_dev)
    last_pos = jnp.where(is_long, total_blocks, total_blocks // SLOTS).astype(jnp.int32) - 1
    first_pos = jnp.zeros_like(position)
    before = jnp.clip(position - 1, 0, last_pos)
    after = jnp.clip(position + 1, 0, last_pos)
    fixed_pos = jnp.stack([first_pos, first_pos + last_pos, before, position, after], axis=-1)
    relative = jnp.concatenate([fixed_pos, chosen.astype(jnp.int32)], axis=-1)
    targets = to_group(slot_id[:, None], relative, is_long, per_slot, per_dev)
    all_true = position >= 0
    fixed_ok = jnp.stack([all_true, all_true, position != 1, all_true, position + 1 != last_pos], axis=-1)
    allowed = jnp.concatenate([fixed_ok, jnp.broadcast_to(all_true[:, None], chosen.shape)], axis=-1)
    is_global = (position == 0) | (position == last_pos)
    return (targets, allowed, is_global)

def global_plan(device, is_long, per_slot, per_dev, seq_devices):
    slot_ids = jnp.arange(SLOTS, dtype=jnp.int32)
    at_end = device == seq_devices - 1
    at_start = device == 0
    cand_rows = (slot_ids * per_slot + jnp.where(at_end, per_slot - 1, 0)).astype(jnp.int32)
    cand_blocks = (device * per_dev + cand_rows).astype(jnp.int32)
    long_flags = at_start & (slot_ids == 0) | at_end & (slot_ids == SLOTS - 1)
    short_flags = (at_start | at_end) & (slot_ids >= 0)
    return (cand_rows, cand_blocks, jnp.where(is_long, long_flags, short_flags))

def softmax_rows(scores):
    row_peak = lax.optimization_barrier(jnp.max(scores, axis=-1, keepdims=True))
    row_exp = jnp.exp(scores - row_peak)
    return row_exp / lax.optimization_barrier(jnp.sum(row_exp, axis=-1, keepdims=True))

def group_forward(params, tok_rows, long_flag, chosen):
    w_query, query_bias, w_key, w_value, value_bias, w_proj, proj_bias, ln1_gain, ln1_bias, w_up, up_bias, w_down, down_bias, ln2_gain, ln2_bias = params
    is_long = long_flag == 1
    per_slot = SLOT_TOK // BLOCK
    per_dev = T_DEV // BLOCK
    total_blocks = GROUP_TOK // BLOCK
    key_width = (5 + RAND) * BLOCK
    query_rows = low_back(low((matmul_hi(tok_rows, w_query) + query_bias) * 0.125))
    key_rows = low_back(low(matmul_hi(tok_rows, w_key)))
    value_rows = low_back(low(matmul_hi(tok_rows, w_value) + value_bias))
    blocks = jnp.arange(total_blocks, dtype=jnp.int32)
    targets, allowed, is_global = key_plan(blocks, chosen, is_long, per_slot, per_dev, total_blocks)
    query_b = query_rows.reshape(total_blocks, BLOCK, HEADS, HEAD)
    key_blocks = key_rows.reshape(total_blocks, BLOCK, D)[targets].reshape(total_blocks, key_width, HEADS, HEAD)
    value_blocks = value_rows.reshape(total_blocks, BLOCK, D)[targets].reshape(total_blocks, key_width, HEADS, HEAD)
    key_mask = jnp.repeat(allowed, BLOCK, axis=1)[:, None, None, :]
    scores = low_back(jnp.einsum('bqhd,bkhd->bhqk', query_b, key_blocks, precision=PRECISE))
    attn_probs = low(softmax_rows(jnp.where(key_mask, scores, MASKED)))
    sparse_out = jnp.einsum('bhqk,bkhd->bqhd', attn_probs, value_blocks, precision=PRECISE)
    first_rows, first_blocks, first_flags = global_plan(jnp.int32(0), is_long, per_slot, per_dev, N_SEQ)
    last_rows, last_blocks, last_flags = global_plan(jnp.int32(N_SEQ - 1), is_long, per_slot, per_dev, N_SEQ)
    cand_blocks = jnp.concatenate([first_blocks, last_blocks])
    cand_flags = jnp.concatenate([first_flags, last_flags])
    slot_all = seq_coords(blocks, is_long, per_slot, per_dev)[0]
    same_seq = jnp.repeat(slot_all[None, :] == slot_all[cand_blocks][:, None], BLOCK, axis=1)[:, None, None, :]
    key_heads = key_rows.reshape(GROUP_TOK, HEADS, HEAD)
    value_heads = value_rows.reshape(GROUP_TOK, HEADS, HEAD)
    glob_scores = low_back(jnp.einsum('cqhd,khd->chqk', query_b[cand_blocks], key_heads, precision=PRECISE))
    glob_probs = low(softmax_rows(jnp.where(same_seq, glob_scores, MASKED)))
    glob_out = jnp.einsum('chqk,khd->cqhd', glob_probs, value_heads, precision=PRECISE)
    picked = jnp.where(cand_flags[:, None, None, None], glob_out, sparse_out[cand_blocks])
    attended = sparse_out.at[cand_blocks].set(picked).reshape(GROUP_TOK, D)
    mixed = low_back(low(attended))
    attn_out = low_back(matmul_hi(mixed, w_proj) + proj_bias)
    normed = layer_norm(tok_rows + attn_out, ln1_gain, ln1_bias)
    hidden_pre = low_back(matmul_hi(low(normed), w_up) + up_bias)
    hidden = low_back(low(jax.nn.gelu(hidden_pre, approximate=True)))
    branch = low_back(matmul_hi(hidden, w_down) + down_bias)
    return layer_norm(normed + branch, ln2_gain, ln2_bias)

def whole_layer(params, rows_all, long_group, random_blocks):

    def one_group(pieces):
        return group_forward(params, pieces[0], pieces[1], pieces[2])
    return lax.map(jax.checkpoint(one_group), (rows_all, long_group, random_blocks))

def reference(inputs, w_query, query_bias, w_key, w_value, value_bias, w_proj, proj_bias, ln1_gain, ln1_bias, w_up, up_bias, w_down, down_bias, ln2_gain, ln2_bias, long_group, random_blocks, out_grad):
    params = tuple((weight_arg.astype(jnp.float32) for weight_arg in (w_query, query_bias, w_key, w_value, value_bias, w_proj, proj_bias, ln1_gain, ln1_bias, w_up, up_bias, w_down, down_bias, ln2_gain, ln2_bias)))
    layer_fn = partial(whole_layer, long_group=long_group, random_blocks=random_blocks)
    final_out, pullback = jax.vjp(layer_fn, params, inputs.astype(jnp.float32))
    param_grads, input_grad = pullback(out_grad.astype(jnp.float32))
    return (final_out.astype(jnp.bfloat16), input_grad, param_grads[0], param_grads[2], param_grads[3], param_grads[5], param_grads[9], param_grads[11], param_grads[1], param_grads[4], param_grads[6], param_grads[7], param_grads[8], param_grads[10], param_grads[12], param_grads[13], param_grads[14])
```

```python
import jax
import jax.numpy as jnp
from jax import lax
from jax.experimental import pallas as pl
from jax.experimental.pallas import tpu as pltpu
from jax.sharding import PartitionSpec as P

D = 768
HEADS = 12
HEAD = 64
FF = 3072
BLOCK = 64
RAND = 3
SLOTS = 2
SLOT_TOK = 128
T_DEV = 256
PER_SLOT = SLOT_TOK // BLOCK
PER_DEV = T_DEV // BLOCK

LN_EPS = 1e-05
MASKED = -1e30
F32 = jnp.float32
BF16 = jnp.bfloat16
MIB = 2**20

NN = (((1,), (0,)), ((), ()))
NT = (((1,), (1,)), ((), ()))
TN = (((0,), (0,)), ((), ()))


def dot(left, right, dims=NN):
    return lax.dot_general(left, right, dims, preferred_element_type=F32)


def layer_norm(residual, ln_gain, ln_shift):
    center = residual - jnp.mean(residual, axis=-1, keepdims=True)
    variance = jnp.mean(center * center, axis=-1, keepdims=True)
    return center * lax.rsqrt(variance + LN_EPS) * ln_gain + ln_shift


def gelu_tanh(pre_act):
    return jax.nn.gelu(pre_act, approximate=True)


def seq_coords(blocks, is_long):
    device = blocks // PER_DEV
    within = blocks % PER_DEV
    slot_id = jnp.where(is_long, 0, within // PER_SLOT)
    position = jnp.where(is_long, blocks, device * PER_SLOT + within % PER_SLOT)
    return (slot_id, position)


def block_bias(device, chosen, is_long, n_seq):
    total_blocks = PER_DEV * n_seq
    last_pos = jnp.where(is_long, total_blocks, total_blocks // SLOTS) - 1
    own_slot, own_pos = seq_coords(device * PER_DEV + jnp.arange(PER_DEV), is_long)
    columns = jnp.arange(total_blocks)
    key_ids = (device ^ (columns // PER_DEV)) * PER_DEV + columns % PER_DEV
    key_slot, key_pos = seq_coords(key_ids, is_long)
    same = own_slot[:, None] == key_slot[None, :]
    ends = (key_pos == 0) | (key_pos == last_pos)
    near = jnp.abs(own_pos[:, None] - key_pos[None, :]) <= 1
    drawn = jnp.any(chosen[:, :, None] == key_pos[None, None, :], axis=1)
    is_global = (own_pos == 0) | (own_pos == last_pos)
    keep = same & (is_global[:, None] | ends[None, :] | near | drawn)
    return jnp.where(keep, 0.0, MASKED).astype(F32)


def attn_fwd_kernel(q_ref, k_ref, v_ref, bias_ref, mixed_ref, lse_ref):
    rows, keys = q_ref.shape[0], k_ref.shape[0]
    query, key, value, bias = q_ref[...], k_ref[...], v_ref[...], bias_ref[...]
    first = lax.broadcasted_iota(jnp.int32, (rows, 2 * HEAD), 1) < HEAD
    outs, lses = [], []
    for head in range(2):
        own = jnp.where(first == (head == 0), query, jnp.zeros_like(query))
        scores = dot(own, key, NT).reshape(PER_DEV, BLOCK, keys) + bias[:, None, :]
        scores = scores.reshape(rows, keys)
        peak = jnp.max(scores, axis=1, keepdims=True)
        weight = jnp.exp(scores - peak)
        total = jnp.sum(weight, axis=1, keepdims=True)
        outs.append(dot((weight * (1.0 / total)).astype(BF16), value))
        lses.append(peak + jnp.log(total))
    mixed_ref[...] = jnp.where(first, outs[0], outs[1]).astype(BF16)
    lse_ref[...] = jnp.where(first, lses[0], lses[1])


def attn_bwd_kernel(q_ref, k_ref, v_ref, bias_ref, g_ref, lse_ref, dq_ref, dk_ref, dv_ref):
    rows, keys = q_ref.shape[0], k_ref.shape[0]
    query, key, value, bias, grad = (
        q_ref[...],
        k_ref[...],
        v_ref[...],
        bias_ref[...],
        g_ref[...],
    )
    first = lax.broadcasted_iota(jnp.int32, (rows, 2 * HEAD), 1) < HEAD
    d_query, d_key, d_value = [], None, None
    for head in range(2):
        mine = first == (head == 0)
        own = jnp.where(mine, query, jnp.zeros_like(query))
        own_grad = jnp.where(mine, grad, jnp.zeros_like(grad))
        scores = dot(own, key, NT).reshape(PER_DEV, BLOCK, keys) + bias[:, None, :]
        probs = jnp.exp(scores.reshape(rows, keys) - lse_ref[:, HEAD * head : HEAD * head + 1])
        d_probs = dot(own_grad, value, NT)
        delta = jnp.sum(probs * d_probs, axis=1, keepdims=True)
        d_scores = (probs * (d_probs - delta)).astype(BF16)
        d_query.append(dot(d_scores, key))
        key_term = dot(d_scores, own, TN)
        value_term = dot(probs.astype(BF16), own_grad, TN)
        d_key = key_term if d_key is None else d_key + key_term
        d_value = value_term if d_value is None else d_value + value_term
    dq_ref[...] = jnp.where(first, d_query[0], d_query[1]).astype(BF16)
    dk_ref[...] = d_key.astype(BF16)
    dv_ref[...] = d_value.astype(BF16)


def head_pair(rows):
    return pl.BlockSpec((rows, 2 * HEAD), lambda i: (0, i))


def whole(shape):
    return pl.BlockSpec(shape, lambda *_: (0,) * len(shape))


def attn_fwd(query, key, value, bias):
    rows, keys = query.shape[0], key.shape[0]
    return pl.pallas_call(
        attn_fwd_kernel,
        grid=(HEADS // 2,),
        in_specs=[head_pair(rows), head_pair(keys), head_pair(keys), whole(bias.shape)],
        out_specs=[head_pair(rows), head_pair(rows)],
        out_shape=[
            jax.ShapeDtypeStruct((rows, D), BF16),
            jax.ShapeDtypeStruct((rows, D), F32),
        ],
        compiler_params=pltpu.CompilerParams(vmem_limit_bytes=40 * MIB),
        name="attn_fwd",
    )(query, key, value, bias)


def attn_bwd(query, key, value, bias, grad, lse):
    rows, keys = query.shape[0], key.shape[0]
    return pl.pallas_call(
        attn_bwd_kernel,
        grid=(HEADS // 2,),
        in_specs=[
            head_pair(rows),
            head_pair(keys),
            head_pair(keys),
            whole(bias.shape),
            head_pair(rows),
            head_pair(rows),
        ],
        out_specs=[head_pair(rows), head_pair(keys), head_pair(keys)],
        out_shape=[
            jax.ShapeDtypeStruct((rows, D), BF16),
            jax.ShapeDtypeStruct((keys, D), BF16),
            jax.ShapeDtypeStruct((keys, D), BF16),
        ],
        compiler_params=pltpu.CompilerParams(vmem_limit_bytes=50 * MIB),
        name="attn_bwd",
    )(query, key, value, bias, grad, lse)


def swap(value, axis, mask):
    size = lax.axis_size(axis)
    return lax.ppermute(value, axis, [(i, i ^ mask) for i in range(size)])


def pick(value, index):
    return lax.dynamic_index_in_dim(value, index, 0, keepdims=False)


def reduce_pieces(grad):
    n_seq, n_dp = lax.axis_size("seq"), lax.axis_size("dp")
    seq, dp = lax.axis_index("seq"), lax.axis_index("dp")
    cols = grad.shape[1]
    share = grad.shape[0] // n_seq
    core = seq % 2
    halves = jnp.swapaxes(grad.reshape(n_seq // 2, 2, share, cols), 0, 1)
    total = pick(halves, core) + swap(pick(halves, 1 - core), "seq", 1)
    step = n_seq // 2
    while step > 1:
        step //= 2
        bit = (seq // (2 * step)) % 2
        halves = total.reshape(2, step, share, cols)
        total = pick(halves, bit) + swap(pick(halves, 1 - bit), "seq", 2 * step)
    bit = dp % 2
    halves = total.reshape(2, share // 2, cols)
    total = pick(halves, bit) + swap(pick(halves, 1 - bit), "dp", 1)
    rest = n_dp // 2
    blocks = total.reshape(rest, share // n_dp, cols)
    place = dp // 2
    piece = pick(blocks, place).astype(F32)
    for other in range(1, rest):
        piece = piece + swap(pick(blocks, place ^ other), "dp", 2 * other).astype(F32)
    return piece.astype(BF16)


def gather_pieces(piece):
    rest = lax.axis_size("dp") // 2
    pieces = [None] * (2 * rest)
    for other in range(rest):
        pieces[2 * other] = piece if other == 0 else swap(piece, "dp", 2 * other)
    for other in range(rest):
        pieces[2 * other + 1] = swap(pieces[2 * other], "dp", 1)
    return pieces


def assemble_kernel(place_ref, *refs, widths):
    outs = refs[len(refs) - len(widths) :]
    for piece_ref, index in zip(refs, range(len(refs) - len(widths))):
        rows = piece_ref.shape[0]
        start = pl.multiple_of(place_ref[index] * rows, 8)
        offset = 0
        for out_ref, width in zip(outs, widths):
            out_ref[pl.ds(start, rows), :] = piece_ref[:, offset : offset + width].astype(F32)
            offset += width


def assemble(pieces, widths):
    n_dp = len(pieces)
    dp = lax.axis_index("dp") ^ jnp.arange(n_dp, dtype=jnp.int32)
    places = dp % 2 * (n_dp // 2) + dp // 2
    rows, cols = pieces[0].shape
    if rows % 8:
        stacked = jnp.zeros((n_dp, rows, cols), F32)
        for i, piece in enumerate(pieces):
            stacked = lax.dynamic_update_slice(stacked, piece.astype(F32)[None], (places[i], 0, 0))
        full = stacked.reshape(n_dp * rows, cols)
        cuts = [sum(widths[:i]) for i in range(len(widths))]
        return [full[:, c : c + w] for c, w in zip(cuts, widths)]
    return pl.pallas_call(
        lambda *refs: assemble_kernel(*refs, widths=widths),
        in_specs=[pl.BlockSpec(memory_space=pltpu.SMEM)]
        + [pl.BlockSpec(memory_space=pltpu.VMEM)] * n_dp,
        out_specs=[pl.BlockSpec(memory_space=pltpu.VMEM)] * len(widths),
        out_shape=[jax.ShapeDtypeStruct((n_dp * rows, w), F32) for w in widths],
        compiler_params=pltpu.CompilerParams(vmem_limit_bytes=24 * MIB),
        name="assemble",
    )(places, *pieces)


def on_device(
    inputs,
    w_query,
    query_bias,
    w_key,
    w_value,
    value_bias,
    w_proj,
    proj_bias,
    ln1_gain,
    ln1_bias,
    w_up,
    up_bias,
    w_down,
    down_bias,
    ln2_gain,
    ln2_bias,
    long_group,
    random_blocks,
    out_grad,
):
    n_seq, n_dp = lax.axis_size("seq"), lax.axis_size("dp")
    device = lax.axis_index("seq")
    tok_rows = inputs.reshape(T_DEV, D)
    parts = [tok_rows] + [None] * (n_seq - 1)
    step = n_seq // 2
    while step > 1:
        for j in range(0, n_seq, 2 * step):
            parts[j + step] = swap(parts[j], "seq", step)
        step //= 2
    for j in range(0, n_seq, 2):
        parts[j + 1] = swap(parts[j], "seq", 1)
    tok_group = jnp.concatenate(parts)
    bias = block_bias(device, random_blocks[0], long_group[0] == 1, n_seq)
    bias = jnp.repeat(bias, BLOCK, axis=1)

    query = ((dot(tok_rows, w_query) + query_bias) * 0.125).astype(BF16)
    key = dot(tok_group, w_key).astype(BF16)
    value = (dot(tok_group, w_value) + value_bias).astype(BF16)
    mixed, lse = attn_fwd(query, key, value, bias)
    attn_out = dot(mixed, w_proj) + proj_bias
    resid_one = tok_rows.astype(F32) + attn_out
    normed, ln1_pull = jax.vjp(
        layer_norm, resid_one, ln1_gain.astype(F32), ln1_bias.astype(F32)
    )
    normed_low = normed.astype(BF16)
    hidden_pre = dot(normed_low, w_up) + up_bias
    activated, gelu_pull = jax.vjp(gelu_tanh, hidden_pre)
    hidden = activated.astype(BF16)
    branch = dot(hidden, w_down) + down_bias
    final_out, ln2_pull = jax.vjp(
        layer_norm, normed + branch, ln2_gain.astype(F32), ln2_bias.astype(F32)
    )
    layer_out = final_out.astype(BF16).reshape(1, T_DEV, D)
    d_resid2, d_gain2, d_bias2 = ln2_pull(out_grad.reshape(T_DEV, D).astype(F32))
    d_branch = d_resid2.astype(BF16)
    piece_down = reduce_pieces(dot(hidden, d_branch, TN).astype(BF16))
    grad_down_b = jnp.sum(d_branch.astype(F32), axis=0)
    d_hidden = dot(d_branch, w_down, NT).astype(BF16)
    (d_pre_raw,) = gelu_pull(d_hidden.astype(F32))
    d_pre = d_pre_raw.astype(BF16)
    piece_up = reduce_pieces(dot(normed_low, d_pre, TN).astype(BF16))
    grad_up_b = jnp.sum(d_pre.astype(F32), axis=0)
    d_normed = d_resid2 + dot(d_pre, w_up, NT)
    d_resid1, d_gain1, d_bias1 = ln1_pull(d_normed)
    d_attn = d_resid1.astype(BF16)
    piece_proj = reduce_pieces(dot(mixed, d_attn, TN).astype(BF16))
    grad_proj_b = jnp.sum(d_attn.astype(F32), axis=0)
    d_mixed = dot(d_attn, w_proj, NT).astype(BF16)

    d_query, d_key, d_value = attn_bwd(query, key, value, bias, d_mixed, lse)
    piece_qkv = reduce_pieces(
        jnp.concatenate(
            [
                (dot(tok_rows, d_query, TN) * 0.125).astype(BF16),
                dot(tok_group, d_key, TN).astype(BF16),
                dot(tok_group, d_value, TN).astype(BF16),
            ],
            axis=1,
        )
    )
    grad_query_b = jnp.sum(d_query.astype(F32), axis=0) * 0.125
    grad_value_b = jnp.sum(d_value.astype(F32), axis=0)

    term = (dot(d_key, w_key, NT) + dot(d_value, w_value, NT)).astype(BF16)
    term = term.reshape(n_seq // 2, 2, T_DEV, D)
    total = term[:, 0].astype(F32) + swap(term[:, 1], "seq", 1).astype(F32)
    step = n_seq // 2
    while step > 1:
        step //= 2
        total = total[:step] + swap(total[step:].astype(BF16), "seq", 2 * step).astype(F32)
    input_grad = d_resid1 + 0.125 * dot(d_query, w_query, NT) + total[0]

    small = jnp.concatenate(
        [
            grad_query_b,
            grad_value_b,
            grad_proj_b,
            d_gain1,
            d_bias1,
            grad_up_b,
            grad_down_b,
            d_gain2,
            d_bias2,
        ]
    )
    for axis, size in (("seq", n_seq), ("dp", n_dp)):
        step = 1
        while step < size:
            small = small + swap(small, axis, step)
            step *= 2

    (grad_down,) = assemble(gather_pieces(piece_down), [D])
    (grad_up,) = assemble(gather_pieces(piece_up), [FF])
    (grad_proj,) = assemble(gather_pieces(piece_proj), [D])
    grad_query, grad_key, grad_value = assemble(gather_pieces(piece_qkv), [D, D, D])
    up_end = 5 * D + FF
    return (
        layer_out,
        input_grad.reshape(1, T_DEV, D),
        grad_query,
        grad_key,
        grad_value,
        grad_proj,
        grad_up,
        grad_down,
        small[0:D],
        small[D : 2 * D],
        small[2 * D : 3 * D],
        small[3 * D : 4 * D],
        small[4 * D : 5 * D],
        small[5 * D : up_end],
        small[up_end : up_end + D],
        small[up_end + D : up_end + 2 * D],
        small[up_end + 2 * D : up_end + 3 * D],
    )


def solution(mesh):
    tokens = P("dp", "seq", None)
    return jax.shard_map(
        on_device,
        mesh=mesh,
        in_specs=(tokens,) + (P(),) * 15 + (P("dp"), tokens, tokens),
        out_specs=(tokens, tokens) + (P("seq", None),) * 6 + (P(),) * 9,
        check_vma=False,
    )
```

```python
import jax
import jax.numpy as jnp
from jax import lax
from jax.experimental import pallas as pl
from jax.experimental.pallas import tpu as pltpu
from jax.sharding import PartitionSpec as P

D = 768
HEADS = 12
HEAD = 64
FF = 3072
BLOCK = 64
RAND = 3
SLOTS = 2
SLOT_TOK = 128
T_DEV = 256
PER_SLOT = SLOT_TOK // BLOCK
PER_DEV = T_DEV // BLOCK

LN_EPS = 1e-05
MASKED = -1e30
F32 = jnp.float32
BF16 = jnp.bfloat16
MIB = 2**20

NN = (((1,), (0,)), ((), ()))
NT = (((1,), (1,)), ((), ()))
TN = (((0,), (0,)), ((), ()))


def dot(left, right, dims=NN):
    return lax.dot_general(left, right, dims, preferred_element_type=F32)


def layer_norm(residual, ln_gain, ln_shift):
    center = residual - jnp.mean(residual, axis=-1, keepdims=True)
    variance = jnp.mean(center * center, axis=-1, keepdims=True)
    return center * lax.rsqrt(variance + LN_EPS) * ln_gain + ln_shift


def gelu_tanh(pre_act):
    return jax.nn.gelu(pre_act, approximate=True)


def seq_coords(blocks, is_long):
    device = blocks // PER_DEV
    within = blocks % PER_DEV
    slot_id = jnp.where(is_long, 0, within // PER_SLOT)
    position = jnp.where(is_long, blocks, device * PER_SLOT + within % PER_SLOT)
    return (slot_id, position)


def block_bias(device, chosen, is_long, n_seq):
    total_blocks = PER_DEV * n_seq
    last_pos = jnp.where(is_long, total_blocks, total_blocks // SLOTS) - 1
    own_slot, own_pos = seq_coords(device * PER_DEV + jnp.arange(PER_DEV), is_long)
    columns = jnp.arange(total_blocks)
    key_ids = (device ^ (columns // PER_DEV)) * PER_DEV + columns % PER_DEV
    key_slot, key_pos = seq_coords(key_ids, is_long)
    same = own_slot[:, None] == key_slot[None, :]
    ends = (key_pos == 0) | (key_pos == last_pos)
    near = jnp.abs(own_pos[:, None] - key_pos[None, :]) <= 1
    drawn = jnp.any(chosen[:, :, None] == key_pos[None, None, :], axis=1)
    is_global = (own_pos == 0) | (own_pos == last_pos)
    keep = same & (is_global[:, None] | ends[None, :] | near | drawn)
    return jnp.where(keep, 0.0, MASKED).astype(F32)


def attn_fwd_kernel(q_ref, k_ref, v_ref, bias_ref, mixed_ref, lse_ref):
    rows, keys = q_ref.shape[0], k_ref.shape[0]
    query, key, value, bias = q_ref[...], k_ref[...], v_ref[...], bias_ref[...]
    first = lax.broadcasted_iota(jnp.int32, (rows, 2 * HEAD), 1) < HEAD
    outs, lses = [], []
    for head in range(2):
        own = jnp.where(first == (head == 0), query, jnp.zeros_like(query))
        scores = dot(own, key, NT).reshape(PER_DEV, BLOCK, keys) + bias[:, None, :]
        scores = scores.reshape(rows, keys)
        peak = jnp.max(scores, axis=1, keepdims=True)
        weight = jnp.exp(scores - peak)
        total = jnp.sum(weight, axis=1, keepdims=True)
        outs.append(dot((weight * (1.0 / total)).astype(BF16), value))
        lses.append(peak + jnp.log(total))
    mixed_ref[...] = jnp.where(first, outs[0], outs[1]).astype(BF16)
    lse_ref[...] = jnp.where(first, lses[0], lses[1])


def attn_bwd_kernel(q_ref, k_ref, v_ref, bias_ref, g_ref, lse_ref, dq_ref, dk_ref, dv_ref):
    rows, keys = q_ref.shape[0], k_ref.shape[0]
    query, key, value, bias, grad = (
        q_ref[...],
        k_ref[...],
        v_ref[...],
        bias_ref[...],
        g_ref[...],
    )
    first = lax.broadcasted_iota(jnp.int32, (rows, 2 * HEAD), 1) < HEAD
    d_query, d_key, d_value = [], None, None
    for head in range(2):
        mine = first == (head == 0)
        own = jnp.where(mine, query, jnp.zeros_like(query))
        own_grad = jnp.where(mine, grad, jnp.zeros_like(grad))
        scores = dot(own, key, NT).reshape(PER_DEV, BLOCK, keys) + bias[:, None, :]
        probs = jnp.exp(scores.reshape(rows, keys) - lse_ref[:, HEAD * head : HEAD * head + 1])
        d_probs = dot(own_grad, value, NT)
        delta = jnp.sum(probs * d_probs, axis=1, keepdims=True)
        d_scores = (probs * (d_probs - delta)).astype(BF16)
        d_query.append(dot(d_scores, key))
        key_term = dot(d_scores, own, TN)
        value_term = dot(probs.astype(BF16), own_grad, TN)
        d_key = key_term if d_key is None else d_key + key_term
        d_value = value_term if d_value is None else d_value + value_term
    dq_ref[...] = jnp.where(first, d_query[0], d_query[1]).astype(BF16)
    dk_ref[...] = d_key.astype(BF16)
    dv_ref[...] = d_value.astype(BF16)


def head_pair(rows):
    return pl.BlockSpec((rows, 2 * HEAD), lambda i: (0, i))


def whole(shape):
    return pl.BlockSpec(shape, lambda *_: (0,) * len(shape))


def attn_fwd(query, key, value, bias):
    rows, keys = query.shape[0], key.shape[0]
    return pl.pallas_call(
        attn_fwd_kernel,
        grid=(HEADS // 2,),
        in_specs=[head_pair(rows), head_pair(keys), head_pair(keys), whole(bias.shape)],
        out_specs=[head_pair(rows), head_pair(rows)],
        out_shape=[
            jax.ShapeDtypeStruct((rows, D), BF16),
            jax.ShapeDtypeStruct((rows, D), F32),
        ],
        compiler_params=pltpu.CompilerParams(vmem_limit_bytes=40 * MIB),
        name="attn_fwd",
    )(query, key, value, bias)


def attn_bwd(query, key, value, bias, grad, lse):
    rows, keys = query.shape[0], key.shape[0]
    return pl.pallas_call(
        attn_bwd_kernel,
        grid=(HEADS // 2,),
        in_specs=[
            head_pair(rows),
            head_pair(keys),
            head_pair(keys),
            whole(bias.shape),
            head_pair(rows),
            head_pair(rows),
        ],
        out_specs=[head_pair(rows), head_pair(keys), head_pair(keys)],
        out_shape=[
            jax.ShapeDtypeStruct((rows, D), BF16),
            jax.ShapeDtypeStruct((keys, D), BF16),
            jax.ShapeDtypeStruct((keys, D), BF16),
        ],
        compiler_params=pltpu.CompilerParams(vmem_limit_bytes=50 * MIB),
        name="attn_bwd",
    )(query, key, value, bias, grad, lse)


LANES = 384
QUARTERS = 4


def quarter_slot(quarter):
    return 2 * (quarter % 2) + quarter // 2


def half_share_kernel(place_ref, *refs, plan, low):
    keep_ref, send_ref, stage, turned = refs[4 * len(plan) :]
    top, low_own, x_own, z_own = (place_ref[i] for i in range(4))
    offset = 0
    for index, (rows, cols) in enumerate(plan):
        sides = (refs[4 * index : 4 * index + 2], refs[4 * index + 2 : 4 * index + 4])
        half = rows // 2
        share = half // low
        strip = min(half, LANES)
        piece_rows = share // QUARTERS
        for start in range(0, half, strip):
            lanes = pl.ds(pl.multiple_of(top * half + start, 128), strip)
            for side, (left, _) in enumerate(sides):
                turned[0:strip, side * T_DEV : (side + 1) * T_DEV] = left[:, lanes].T
            for block in range(cols // D):
                grad = sum(
                    dot(
                        turned[0:strip, side * T_DEV : (side + 1) * T_DEV],
                        right[:, block * D : (block + 1) * D],
                    )
                    for side, (_, right) in enumerate(sides)
                )
                for part in range(D // LANES):
                    column = block * D + part * LANES
                    side_x = column // (cols // 2)
                    slot = offset + (column % (cols // 2)) // LANES * piece_rows
                    for row in range(0, strip, piece_rows):
                        at = start + row
                        low_other = at // share
                        quarter = at % share // piece_rows
                        stage[
                            low_other ^ low_own,
                            side_x ^ x_own,
                            quarter_slot(quarter ^ z_own),
                            slot : slot + piece_rows,
                            :,
                        ] = grad[
                            row : row + piece_rows, part * LANES : (part + 1) * LANES
                        ].astype(BF16)
        offset += piece_rows * (cols // 2 // LANES)
    keep_ref[...] = stage[0 : low // 2]
    send_ref[...] = stage[low // 2 : low]


VMEM_SPEC = pl.BlockSpec(memory_space=pltpu.VMEM)
SMEM_SPEC = pl.BlockSpec(memory_space=pltpu.SMEM)


def half_share_grads(place, weights, n_seq, name):
    low = n_seq // 2
    plan = [(w[0].shape[1], w[1].shape[1]) for w in weights]
    piece_rows = sum(r // n_seq // QUARTERS * (c // 2 // LANES) for r, c in plan)
    shape = (2, QUARTERS, piece_rows, LANES)
    return pl.pallas_call(
        lambda *refs: half_share_kernel(*refs, plan=plan, low=low),
        in_specs=[SMEM_SPEC] + [VMEM_SPEC] * (4 * len(weights)),
        out_specs=[VMEM_SPEC] * 2,
        out_shape=[jax.ShapeDtypeStruct((low // 2, *shape), BF16)] * 2,
        scratch_shapes=[pltpu.VMEM((low, *shape), BF16), pltpu.VMEM((LANES, 2 * T_DEV), BF16)],
        compiler_params=pltpu.CompilerParams(vmem_limit_bytes=48 * MIB),
        name=name,
    )(place, *[array for weight in weights for array in weight])


def full_share_kernel(place_ref, group_ref, dq_ref, dk_ref, dv_ref, keep_ref, send_ref, stage, turned, *, n_seq):
    top, low_own, x_own, z_own = (place_ref[i] for i in range(4))
    seq_own = top * (n_seq // 2) + low_own
    share = D // n_seq
    piece_rows = share // QUARTERS
    tokens = group_ref.shape[0]
    for start in range(0, D, LANES):
        turned[...] = group_ref[:, start : start + LANES].T
        for index, right in enumerate((dq_ref, dk_ref, dv_ref)):
            if index == 0:
                grad = dot(turned[:, 0:T_DEV], right[...]) * 0.125
            else:
                grad = dot(turned[...], right[...])
            for part in range(D // LANES):
                for row in range(0, LANES, piece_rows):
                    at = start + row
                    relative = (at // share) ^ seq_own
                    stage[
                        relative % 2 * (n_seq // 2) + relative // 2,
                        part ^ x_own,
                        quarter_slot(at % share // piece_rows ^ z_own),
                        index * piece_rows : (index + 1) * piece_rows,
                        :,
                    ] = grad[row : row + piece_rows, part * LANES : (part + 1) * LANES].astype(BF16)
    keep_ref[...] = stage[0 : n_seq // 2]
    send_ref[...] = stage[n_seq // 2 : n_seq]


def full_share_grads(place, group, d_query, d_key, d_value, n_seq):
    piece_rows = 3 * (D // n_seq // QUARTERS)
    shape = (2, QUARTERS, piece_rows, LANES)
    return pl.pallas_call(
        lambda *refs: full_share_kernel(*refs, n_seq=n_seq),
        in_specs=[SMEM_SPEC] + [VMEM_SPEC] * 4,
        out_specs=[VMEM_SPEC] * 2,
        out_shape=[jax.ShapeDtypeStruct((n_seq // 2, *shape), BF16)] * 2,
        scratch_shapes=[
            pltpu.VMEM((n_seq, *shape), BF16),
            pltpu.VMEM((LANES, group.shape[0]), BF16),
        ],
        compiler_params=pltpu.CompilerParams(vmem_limit_bytes=48 * MIB),
        name="grads_qkv",
    )(place, group, d_query, d_key, d_value)


def assemble_kernel(place_ref, *refs, plan):
    outs = refs[len(refs) - len(plan) :]
    x_own, z_own = place_ref[2], place_ref[3]
    index = 0
    for ref in refs[: len(refs) - len(plan)]:
        for slot in range(ref.shape[0]):
            relative, column = index % QUARTERS, index // QUARTERS
            quarter = (relative // 2 + relative % 2 * 2) ^ z_own
            offset = 0
            for out, (rows, cols) in zip(outs, plan):
                height = rows // QUARTERS
                at = pl.ds(pl.multiple_of(quarter * height, 8), height)
                for part in range(cols // 2 // LANES):
                    lanes = pl.ds(
                        pl.multiple_of((column ^ x_own) * (cols // 2) + part * LANES, 128), LANES
                    )
                    out[at, lanes] = ref[slot, offset : offset + height, :].astype(F32)
                    offset += height
            index += 1


def assemble(place, pieces, plan, name):
    return pl.pallas_call(
        lambda *refs: assemble_kernel(*refs, plan=plan),
        in_specs=[SMEM_SPEC] + [VMEM_SPEC] * len(pieces),
        out_specs=[VMEM_SPEC] * len(plan),
        out_shape=[jax.ShapeDtypeStruct(shape, F32) for shape in plan],
        compiler_params=pltpu.CompilerParams(vmem_limit_bytes=32 * MIB),
        name=name,
    )(place, *pieces)


def swap(value, axis, mask):
    size = lax.axis_size(axis)
    return lax.ppermute(value, axis, [(i, i ^ mask) for i in range(size)])


def summed(terms):
    total = terms[0].astype(F32)
    for term in terms[1:]:
        total = total + term.astype(F32)
    return total.astype(BF16)


def halve(terms, axis, mask):
    half = terms[0].shape[0] // 2
    got = swap(summed([t[half:] for t in terms]), axis, mask)
    return [t[:half] for t in terms] + [got]


def reduce_and_gather(keep, send, seq_masks):
    n_dp = lax.axis_size("dp")
    terms = [keep, swap(send, "seq", seq_masks[0])]
    for mask in seq_masks[1:]:
        terms = halve(terms, "seq", mask)
    terms = halve([t[0] for t in terms], "dp", 1)
    terms = halve([t[0] for t in terms], "dp", 2)
    terms = halve(terms, "dp", 4)
    piece = summed(terms)
    step = 8
    while step < n_dp:
        piece = summed([piece, swap(piece, "dp", step)])
        step *= 2
    second = swap(piece, "dp", 4)
    pair = jnp.concatenate([piece, second])
    others = swap(pair, "dp", 2)
    return [piece, second, others, swap(jnp.concatenate([pair, others]), "dp", 1)]


def after_attention(tokens, mixed, out_grad, weights):
    w_proj, proj_bias, gain1, bias1, w_up, up_bias, w_down, down_bias, gain2, bias2 = weights
    resid_one = tokens.astype(F32) + dot(mixed, w_proj) + proj_bias
    normed, ln1_pull = jax.vjp(layer_norm, resid_one, gain1, bias1)
    normed_low = normed.astype(BF16)
    hidden_pre = dot(normed_low, w_up) + up_bias
    activated, gelu_pull = jax.vjp(gelu_tanh, hidden_pre)
    hidden = activated.astype(BF16)
    branch = dot(hidden, w_down) + down_bias
    final_out, ln2_pull = jax.vjp(layer_norm, normed + branch, gain2, bias2)
    d_resid2, d_gain2, d_bias2 = ln2_pull(out_grad.astype(F32))
    d_branch = d_resid2.astype(BF16)
    d_hidden = dot(d_branch, w_down, NT).astype(BF16)
    (d_pre_raw,) = gelu_pull(d_hidden.astype(F32))
    d_pre = d_pre_raw.astype(BF16)
    d_normed = d_resid2 + dot(d_pre, w_up, NT)
    d_resid1, d_gain1, d_bias1 = ln1_pull(d_normed)
    d_attn = d_resid1.astype(BF16)
    return dict(
        layer_out=final_out.astype(BF16),
        normed_low=normed_low,
        hidden=hidden,
        d_branch=d_branch,
        d_pre=d_pre,
        d_attn=d_attn,
        d_resid1=d_resid1,
        small=(d_gain1, d_bias1, d_gain2, d_bias2),
    )


def column_sum(array):
    return jnp.sum(array.astype(F32), axis=0)


def on_device(
    inputs,
    w_query,
    query_bias,
    w_key,
    w_value,
    value_bias,
    w_proj,
    proj_bias,
    ln1_gain,
    ln1_bias,
    w_up,
    up_bias,
    w_down,
    down_bias,
    ln2_gain,
    ln2_bias,
    long_group,
    random_blocks,
    out_grad,
):
    n_seq, n_dp = lax.axis_size("seq"), lax.axis_size("dp")
    device, dp = lax.axis_index("seq"), lax.axis_index("dp")
    low = n_seq // 2
    place = jnp.stack([device // low, device % low, dp % 2, dp // 2 % QUARTERS]).astype(jnp.int32)
    tok_rows = inputs.reshape(T_DEV, D)
    cotangent = out_grad.reshape(T_DEV, D)
    parts = [tok_rows] + [None] * (n_seq - 1)
    step = low
    while step > 1:
        for j in range(0, n_seq, 2 * step):
            parts[j + step] = swap(parts[j], "seq", step)
        step //= 2
    for j in range(0, n_seq, 2):
        parts[j + 1] = swap(parts[j], "seq", 1)
    tok_group = jnp.concatenate(parts)
    cotangent_partner = swap(cotangent, "seq", low)
    bias = block_bias(device, random_blocks[0], long_group[0] == 1, n_seq)
    bias = jnp.repeat(bias, BLOCK, axis=1)

    query = ((dot(tok_rows, w_query) + query_bias) * 0.125).astype(BF16)
    key = dot(tok_group, w_key).astype(BF16)
    value = (dot(tok_group, w_value) + value_bias).astype(BF16)
    mixed, lse = attn_fwd(query, key, value, bias)
    mixed_partner = swap(mixed, "seq", low)
    weights = (
        w_proj,
        proj_bias,
        ln1_gain.astype(F32),
        ln1_bias.astype(F32),
        w_up,
        up_bias,
        w_down,
        down_bias,
        ln2_gain.astype(F32),
        ln2_bias.astype(F32),
    )
    own = after_attention(tok_rows, mixed, cotangent, weights)
    other = after_attention(parts[low], mixed_partner, cotangent_partner, weights)
    down_terms = half_share_grads(
        place,
        [(own["hidden"], own["d_branch"], other["hidden"], other["d_branch"])],
        n_seq,
        "grads_down",
    )
    up_terms = half_share_grads(
        place,
        [
            (own["normed_low"], own["d_pre"], other["normed_low"], other["d_pre"]),
            (mixed, own["d_attn"], mixed_partner, other["d_attn"]),
        ],
        n_seq,
        "grads_up_proj",
    )
    low_masks = [1 << i for i in reversed(range(n_seq.bit_length() - 2))]
    pieces_down = reduce_and_gather(*down_terms, low_masks)
    pieces_up = reduce_and_gather(*up_terms, low_masks)

    d_mixed = dot(own["d_attn"], w_proj, NT).astype(BF16)
    d_query, d_key, d_value = attn_bwd(query, key, value, bias, d_mixed, lse)
    qkv_terms = full_share_grads(place, tok_group, d_query, d_key, d_value, n_seq)
    pieces_qkv = reduce_and_gather(
        *qkv_terms, [1] + [1 << i for i in reversed(range(1, n_seq.bit_length() - 1))]
    )

    term = (dot(d_key, w_key, NT) + dot(d_value, w_value, NT)).astype(BF16)
    term = term.reshape(low, 2, T_DEV, D)
    total = [term[:, 0], swap(term[:, 1], "seq", 1)]
    step = low
    while step > 1:
        step //= 2
        total = halve(total, "seq", 2 * step)
    input_grad = own["d_resid1"] + 0.125 * dot(d_query, w_query, NT)
    for part in total:
        input_grad = input_grad + part[0].astype(F32)

    d_gain1, d_bias1, d_gain2, d_bias2 = own["small"]
    small = jnp.concatenate(
        [
            column_sum(d_query) * 0.125,
            column_sum(d_value),
            column_sum(own["d_attn"]),
            d_gain1,
            d_bias1,
            column_sum(own["d_pre"]),
            column_sum(own["d_branch"]),
            d_gain2,
            d_bias2,
        ]
    )
    for axis, size in (("seq", n_seq), ("dp", n_dp)):
        step = 1
        while step < size:
            small = small + swap(small, axis, step)
            step *= 2

    square = (D // n_seq, D)
    (grad_down,) = assemble(place, pieces_down, [(FF // n_seq, D)], "assemble_down")
    grad_up, grad_proj = assemble(place, pieces_up, [(D // n_seq, FF), square], "assemble_up")
    grad_query, grad_key, grad_value = assemble(place, pieces_qkv, [square] * 3, "assemble_qkv")
    up_end = 5 * D + FF
    return (
        own["layer_out"].reshape(1, T_DEV, D),
        input_grad.reshape(1, T_DEV, D),
        grad_query,
        grad_key,
        grad_value,
        grad_proj,
        grad_up,
        grad_down,
        small[0:D],
        small[D : 2 * D],
        small[2 * D : 3 * D],
        small[3 * D : 4 * D],
        small[4 * D : 5 * D],
        small[5 * D : up_end],
        small[up_end : up_end + D],
        small[up_end + D : up_end + 2 * D],
        small[up_end + 2 * D : up_end + 3 * D],
    )


def solution(mesh):
    tokens = P("dp", "seq", None)
    return jax.shard_map(
        on_device,
        mesh=mesh,
        in_specs=(tokens,) + (P(),) * 15 + (P("dp"), tokens, tokens),
        out_specs=(tokens, tokens) + (P("seq", None),) * 6 + (P(),) * 9,
        check_vma=False,
    )
```

```python
import jax
import jax.numpy as jnp
from jax import lax
from jax.experimental import pallas as pl
from jax.experimental.pallas import tpu as pltpu
from jax.sharding import PartitionSpec as P

D = 768
HEADS = 12
HEAD = 64
FF = 3072
BLOCK = 64
RAND = 3
SLOTS = 2
SLOT_TOK = 128
T_DEV = 256
PER_SLOT = SLOT_TOK // BLOCK
PER_DEV = T_DEV // BLOCK

LN_EPS = 1e-05
MASKED = -1e30
F32 = jnp.float32
BF16 = jnp.bfloat16
MIB = 2**20

NN = (((1,), (0,)), ((), ()))
NT = (((1,), (1,)), ((), ()))
TN = (((0,), (0,)), ((), ()))


def dot(left, right, dims=NN):
    return lax.dot_general(left, right, dims, preferred_element_type=F32)


def layer_norm(residual, ln_gain, ln_shift):
    center = residual - jnp.mean(residual, axis=-1, keepdims=True)
    variance = jnp.mean(center * center, axis=-1, keepdims=True)
    return center * lax.rsqrt(variance + LN_EPS) * ln_gain + ln_shift


def gelu_tanh(pre_act):
    return jax.nn.gelu(pre_act, approximate=True)


def seq_coords(blocks, is_long):
    device = blocks // PER_DEV
    within = blocks % PER_DEV
    slot_id = jnp.where(is_long, 0, within // PER_SLOT)
    position = jnp.where(is_long, blocks, device * PER_SLOT + within % PER_SLOT)
    return (slot_id, position)


def block_bias(device, chosen, is_long, n_seq):
    total_blocks = PER_DEV * n_seq
    last_pos = jnp.where(is_long, total_blocks, total_blocks // SLOTS) - 1
    own_slot, own_pos = seq_coords(device * PER_DEV + jnp.arange(PER_DEV), is_long)
    columns = jnp.arange(total_blocks)
    key_ids = (device ^ (columns // PER_DEV)) * PER_DEV + columns % PER_DEV
    key_slot, key_pos = seq_coords(key_ids, is_long)
    same = own_slot[:, None] == key_slot[None, :]
    ends = (key_pos == 0) | (key_pos == last_pos)
    near = jnp.abs(own_pos[:, None] - key_pos[None, :]) <= 1
    drawn = jnp.any(chosen[:, :, None] == key_pos[None, None, :], axis=1)
    is_global = (own_pos == 0) | (own_pos == last_pos)
    keep = same & (is_global[:, None] | ends[None, :] | near | drawn)
    return jnp.where(keep, 0.0, MASKED).astype(F32)


def attn_fwd_kernel(q_ref, k_ref, v_ref, bias_ref, mixed_ref, lse_ref):
    rows, keys = q_ref.shape[0], k_ref.shape[0]
    query, key, value, bias = q_ref[...], k_ref[...], v_ref[...], bias_ref[...]
    first = lax.broadcasted_iota(jnp.int32, (rows, 2 * HEAD), 1) < HEAD
    outs, lses = [], []
    for head in range(2):
        own = jnp.where(first == (head == 0), query, jnp.zeros_like(query))
        scores = dot(own, key, NT).reshape(PER_DEV, BLOCK, keys) + bias[:, None, :]
        scores = scores.reshape(rows, keys)
        peak = jnp.max(scores, axis=1, keepdims=True)
        weight = jnp.exp(scores - peak)
        total = jnp.sum(weight, axis=1, keepdims=True)
        outs.append(dot((weight * (1.0 / total)).astype(BF16), value))
        lses.append(peak + jnp.log(total))
    mixed_ref[...] = jnp.where(first, outs[0], outs[1]).astype(BF16)
    lse_ref[...] = jnp.where(first, lses[0], lses[1])


def attn_bwd_kernel(q_ref, k_ref, v_ref, bias_ref, g_ref, lse_ref, dq_ref, dk_ref, dv_ref):
    rows, keys = q_ref.shape[0], k_ref.shape[0]
    query, key, value, bias, grad = (
        q_ref[...],
        k_ref[...],
        v_ref[...],
        bias_ref[...],
        g_ref[...],
    )
    first = lax.broadcasted_iota(jnp.int32, (rows, 2 * HEAD), 1) < HEAD
    d_query, d_key, d_value = [], None, None
    for head in range(2):
        mine = first == (head == 0)
        own = jnp.where(mine, query, jnp.zeros_like(query))
        own_grad = jnp.where(mine, grad, jnp.zeros_like(grad))
        scores = dot(own, key, NT).reshape(PER_DEV, BLOCK, keys) + bias[:, None, :]
        probs = jnp.exp(scores.reshape(rows, keys) - lse_ref[:, HEAD * head : HEAD * head + 1])
        d_probs = dot(own_grad, value, NT)
        delta = jnp.sum(probs * d_probs, axis=1, keepdims=True)
        d_scores = (probs * (d_probs - delta)).astype(BF16)
        d_query.append(dot(d_scores, key))
        key_term = dot(d_scores, own, TN)
        value_term = dot(probs.astype(BF16), own_grad, TN)
        d_key = key_term if d_key is None else d_key + key_term
        d_value = value_term if d_value is None else d_value + value_term
    dq_ref[...] = jnp.where(first, d_query[0], d_query[1]).astype(BF16)
    dk_ref[...] = d_key.astype(BF16)
    dv_ref[...] = d_value.astype(BF16)


def cost(microseconds):
    return pl.CostEstimate(flops=int(microseconds * 1e3), bytes_accessed=0, transcendentals=0)


def head_pair(rows):
    return pl.BlockSpec((rows, 2 * HEAD), lambda i: (0, i))


def whole(shape):
    return pl.BlockSpec(shape, lambda *_: (0,) * len(shape))


def attn_fwd(query, key, value, bias):
    rows, keys = query.shape[0], key.shape[0]
    return pl.pallas_call(
        attn_fwd_kernel,
        grid=(HEADS // 2,),
        in_specs=[head_pair(rows), head_pair(keys), head_pair(keys), whole(bias.shape)],
        out_specs=[head_pair(rows), head_pair(rows)],
        out_shape=[
            jax.ShapeDtypeStruct((rows, D), BF16),
            jax.ShapeDtypeStruct((rows, D), F32),
        ],
        compiler_params=pltpu.CompilerParams(vmem_limit_bytes=40 * MIB),
        cost_estimate=cost(10),
        name="attn_fwd",
    )(query, key, value, bias)


def attn_bwd(query, key, value, bias, grad, lse):
    rows, keys = query.shape[0], key.shape[0]
    return pl.pallas_call(
        attn_bwd_kernel,
        grid=(HEADS // 2,),
        in_specs=[
            head_pair(rows),
            head_pair(keys),
            head_pair(keys),
            whole(bias.shape),
            head_pair(rows),
            head_pair(rows),
        ],
        out_specs=[head_pair(rows), head_pair(keys), head_pair(keys)],
        out_shape=[
            jax.ShapeDtypeStruct((rows, D), BF16),
            jax.ShapeDtypeStruct((keys, D), BF16),
            jax.ShapeDtypeStruct((keys, D), BF16),
        ],
        compiler_params=pltpu.CompilerParams(vmem_limit_bytes=50 * MIB),
        cost_estimate=cost(14),
        name="attn_bwd",
    )(query, key, value, bias, grad, lse)


LANES = 384
QUARTERS = 4


def slot_of(quarter):
    return 2 * (quarter % 2) + quarter // 2


def half_share_kernel(place_ref, *refs, plan, low):
    keep_ref, send_ref, stage, turned = refs[4 * len(plan) :]
    top, low_own, x_own, z_own = (place_ref[i] for i in range(4))
    offset = 0
    for index, (rows, cols) in enumerate(plan):
        sides = (refs[4 * index : 4 * index + 2], refs[4 * index + 2 : 4 * index + 4])
        half = rows // 2
        share = half // low
        strip = min(half, LANES)
        piece_rows = share // QUARTERS
        for start in range(0, half, strip):
            lanes = pl.ds(pl.multiple_of(top * half + start, 128), strip)
            for side, (left, _) in enumerate(sides):
                turned[0:strip, side * T_DEV : (side + 1) * T_DEV] = left[:, lanes].T
            for block in range(cols // D):
                grad = sum(
                    dot(
                        turned[0:strip, side * T_DEV : (side + 1) * T_DEV],
                        right[:, block * D : (block + 1) * D],
                    )
                    for side, (_, right) in enumerate(sides)
                )
                for part in range(D // LANES):
                    column = block * D + part * LANES
                    side_x = column // (cols // 2)
                    slot = offset + (column % (cols // 2)) // LANES * piece_rows
                    for row in range(0, strip, piece_rows):
                        at = start + row
                        low_other = at // share
                        quarter = at % share // piece_rows
                        stage[
                            low_other ^ low_own,
                            side_x ^ x_own,
                            slot_of(quarter ^ z_own),
                            slot : slot + piece_rows,
                            :,
                        ] = grad[
                            row : row + piece_rows, part * LANES : (part + 1) * LANES
                        ].astype(BF16)
        offset += piece_rows * (cols // 2 // LANES)
    keep_ref[...] = stage[0 : low // 2]
    send_ref[...] = stage[low // 2 : low]


VMEM_SPEC = pl.BlockSpec(memory_space=pltpu.VMEM)
SMEM_SPEC = pl.BlockSpec(memory_space=pltpu.SMEM)


def half_share_grads(place, weights, n_seq, name):
    low = n_seq // 2
    plan = [(w[0].shape[1], w[1].shape[1]) for w in weights]
    piece_rows = sum(r // n_seq // QUARTERS * (c // 2 // LANES) for r, c in plan)
    shape = (2, QUARTERS, piece_rows, LANES)
    return pl.pallas_call(
        lambda *refs: half_share_kernel(*refs, plan=plan, low=low),
        in_specs=[SMEM_SPEC] + [VMEM_SPEC] * (4 * len(weights)),
        out_specs=[VMEM_SPEC] * 2,
        out_shape=[jax.ShapeDtypeStruct((low // 2, *shape), BF16)] * 2,
        scratch_shapes=[pltpu.VMEM((low, *shape), BF16), pltpu.VMEM((LANES, 2 * T_DEV), BF16)],
        compiler_params=pltpu.CompilerParams(vmem_limit_bytes=48 * MIB),
        cost_estimate=cost(4),
        name=name,
    )(place, *[array for weight in weights for array in weight])


def full_share_kernel(place_ref, group_ref, dq_ref, dk_ref, dv_ref, keep_ref, send_ref, stage, turned, *, n_seq):
    top, low_own, x_own, z_own = (place_ref[i] for i in range(4))
    seq_own = top * (n_seq // 2) + low_own
    share = D // n_seq
    piece_rows = share // QUARTERS
    tokens = group_ref.shape[0]
    for start in range(0, D, LANES):
        turned[...] = group_ref[:, start : start + LANES].T
        for index, right in enumerate((dq_ref, dk_ref, dv_ref)):
            if index == 0:
                grad = dot(turned[:, 0:T_DEV], right[...]) * 0.125
            else:
                grad = dot(turned[...], right[...])
            for part in range(D // LANES):
                for row in range(0, LANES, piece_rows):
                    at = start + row
                    relative = (at // share) ^ seq_own
                    stage[
                        relative % 2 * (n_seq // 2) + relative // 2,
                        part ^ x_own,
                        slot_of((at % share // piece_rows) ^ z_own),
                        index * piece_rows : (index + 1) * piece_rows,
                        :,
                    ] = grad[row : row + piece_rows, part * LANES : (part + 1) * LANES].astype(BF16)
    keep_ref[...] = stage[0 : n_seq // 2]
    send_ref[...] = stage[n_seq // 2 : n_seq]


def full_share_grads(place, group, d_query, d_key, d_value, n_seq):
    piece_rows = 3 * (D // n_seq // QUARTERS)
    shape = (2, QUARTERS, piece_rows, LANES)
    return pl.pallas_call(
        lambda *refs: full_share_kernel(*refs, n_seq=n_seq),
        in_specs=[SMEM_SPEC] + [VMEM_SPEC] * 4,
        out_specs=[VMEM_SPEC] * 2,
        out_shape=[jax.ShapeDtypeStruct((n_seq // 2, *shape), BF16)] * 2,
        scratch_shapes=[
            pltpu.VMEM((n_seq, *shape), BF16),
            pltpu.VMEM((LANES, group.shape[0]), BF16),
        ],
        compiler_params=pltpu.CompilerParams(vmem_limit_bytes=48 * MIB),
        cost_estimate=cost(5),
        name="grads_qkv",
    )(place, group, d_query, d_key, d_value)


def assemble_kernel(place_ref, *refs, plan):
    outs = refs[len(refs) - len(plan) :]
    x_own, z_own = place_ref[2], place_ref[3]
    index = 0
    for ref in refs[: len(refs) - len(plan)]:
        for slot in range(ref.shape[0]):
            relative, column = index % QUARTERS, index // QUARTERS
            quarter = slot_of(relative) ^ z_own
            offset = 0
            for out, (rows, cols) in zip(outs, plan):
                height = rows // QUARTERS
                at = pl.ds(pl.multiple_of(quarter * height, 8), height)
                for part in range(cols // 2 // LANES):
                    lanes = pl.ds(
                        pl.multiple_of((column ^ x_own) * (cols // 2) + part * LANES, 128), LANES
                    )
                    out[at, lanes] = ref[slot, offset : offset + height, :].astype(F32)
                    offset += height
            index += 1


def assemble(place, pieces, plan, name):
    return pl.pallas_call(
        lambda *refs: assemble_kernel(*refs, plan=plan),
        in_specs=[SMEM_SPEC] + [VMEM_SPEC] * len(pieces),
        out_specs=[VMEM_SPEC] * len(plan),
        out_shape=[jax.ShapeDtypeStruct(shape, F32) for shape in plan],
        compiler_params=pltpu.CompilerParams(vmem_limit_bytes=32 * MIB),
        cost_estimate=cost(2),
        name=name,
    )(place, *pieces)


def swap(value, axis, mask):
    size = lax.axis_size(axis)
    return lax.ppermute(value, axis, [(i, i ^ mask) for i in range(size)])


def summed(terms):
    total = terms[0].astype(F32)
    for term in terms[1:]:
        total = total + term.astype(F32)
    return total.astype(BF16)


class Order:
    def __init__(self):
        self.last = ()

    def after(self, *arrays):
        return lax.optimization_barrier((*arrays, *self.last))[: len(arrays)]

    def mark(self, *arrays):
        self.last = arrays


def exchange(order, sends, swaps):
    order.mark(*sends)
    return [swap(send, axis, mask) for send, (axis, mask) in zip(sends, swaps)]


def sum_seq(order, keep, send, seq_masks):
    got = exchange(order, [send], [("seq", seq_masks[0])])
    yield
    terms = [keep, *order.after(*got)]
    for mask in seq_masks[1:]:
        half = terms[0].shape[0] // 2
        got = exchange(order, [summed([t[half:] for t in terms])], [("seq", mask)])
        yield
        terms = [t[:half] for t in terms] + list(order.after(*got))
    return [t[0] for t in terms]


def sum_dp_rest(order, piece):
    step = 2 * QUARTERS
    while step < lax.axis_size("dp"):
        got = exchange(order, [piece], [("dp", step)])
        yield
        piece = summed([piece, *order.after(*got)])
        step *= 2
    return piece


def gather_dp(order, own):
    for mask in (4, 2):
        got = exchange(order, [own], [("dp", mask)])
        yield
        own = jnp.concatenate([own, *order.after(*got)])
    got = exchange(order, [own], [("dp", 1)])
    yield
    (other,) = order.after(*got)
    return [own, other]


def columns_first(order, keep, send, seq_masks):
    terms = yield from sum_seq(order, keep, send, seq_masks)
    got = exchange(order, [summed([t[1] for t in terms])], [("dp", 1)])
    yield
    terms = [t[0] for t in terms] + list(order.after(*got))
    for mask in (2, 4):
        half = terms[0].shape[0] // 2
        got = exchange(order, [summed([t[half:] for t in terms])], [("dp", mask)])
        yield
        terms = [t[:half] for t in terms] + list(order.after(*got))
    piece = yield from sum_dp_rest(order, summed(terms))
    return (yield from gather_dp(order, piece))


def quarters_first(order, keep, send, seq_masks):
    terms = yield from sum_seq(order, keep, send, seq_masks)
    others = range(1, QUARTERS)
    sends = [summed([t[:, slot_of(other)] for t in terms]) for other in others]
    got = exchange(order, sends, [("dp", 2 * other) for other in others])
    yield
    terms = [t[:, 0] for t in terms] + list(order.after(*got))
    got = exchange(order, [summed([t[1:] for t in terms])], [("dp", 1)])
    yield
    piece = summed([t[:1] for t in terms] + list(order.after(*got)))
    piece = yield from sum_dp_rest(order, piece)
    return (yield from gather_dp(order, piece))


def token_chain(order, term, small):
    n_seq, n_dp = lax.axis_size("seq"), lax.axis_size("dp")
    terms = [term]
    masks = [1] + [1 << i for i in reversed(range(1, n_seq.bit_length() - 1))]
    for mask in masks:
        half = terms[0].shape[0] // 2
        high = small.astype(BF16)
        rest = (small - high.astype(F32)).astype(BF16)
        send = summed([t[half:] for t in terms]).reshape(half * T_DEV, D)
        send = jnp.concatenate([send, high, rest])
        got = exchange(order, [send], [("seq", mask)])
        yield
        (got,) = order.after(*got)
        count = small.shape[0]
        small = high.astype(F32) + rest.astype(F32) + got[-2 * count : -count].astype(F32) + got[-count:].astype(F32)
        terms = [t[:half] for t in terms] + [got[: half * T_DEV].reshape(half, T_DEV, D)]
    total = sum(t[0].astype(F32) for t in terms)
    step = 1
    while step < n_dp:
        got = exchange(order, [small], [("dp", step)])
        yield
        small = small + order.after(*got)[0]
        step *= 2
    return total, small


def finish(chain):
    try:
        next(chain)
    except StopIteration as stop:
        return stop.value
    raise ValueError("steps left")


def after_attention(tokens, mixed, out_grad, weights):
    w_proj, proj_bias, gain1, bias1, w_up, up_bias, w_down, down_bias, gain2, bias2 = weights
    resid_one = tokens.astype(F32) + dot(mixed, w_proj) + proj_bias
    normed, ln1_pull = jax.vjp(layer_norm, resid_one, gain1, bias1)
    normed_low = normed.astype(BF16)
    hidden_pre = dot(normed_low, w_up) + up_bias
    activated, gelu_pull = jax.vjp(gelu_tanh, hidden_pre)
    hidden = activated.astype(BF16)
    branch = dot(hidden, w_down) + down_bias
    final_out, ln2_pull = jax.vjp(layer_norm, normed + branch, gain2, bias2)
    d_resid2, d_gain2, d_bias2 = ln2_pull(out_grad.astype(F32))
    d_branch = d_resid2.astype(BF16)
    d_hidden = dot(d_branch, w_down, NT).astype(BF16)
    (d_pre_raw,) = gelu_pull(d_hidden.astype(F32))
    d_pre = d_pre_raw.astype(BF16)
    d_normed = d_resid2 + dot(d_pre, w_up, NT)
    d_resid1, d_gain1, d_bias1 = ln1_pull(d_normed)
    d_attn = d_resid1.astype(BF16)
    return dict(
        layer_out=final_out.astype(BF16),
        normed_low=normed_low,
        hidden=hidden,
        d_branch=d_branch,
        d_pre=d_pre,
        d_attn=d_attn,
        d_resid1=d_resid1,
        small=(d_gain1, d_bias1, d_gain2, d_bias2),
    )


def column_sum(array):
    return jnp.sum(array.astype(F32), axis=0)


def on_device(
    inputs,
    w_query,
    query_bias,
    w_key,
    w_value,
    value_bias,
    w_proj,
    proj_bias,
    ln1_gain,
    ln1_bias,
    w_up,
    up_bias,
    w_down,
    down_bias,
    ln2_gain,
    ln2_bias,
    long_group,
    random_blocks,
    out_grad,
):
    n_seq, n_dp = lax.axis_size("seq"), lax.axis_size("dp")
    device, dp = lax.axis_index("seq"), lax.axis_index("dp")
    low = n_seq // 2
    place = jnp.stack([device // low, device % low, dp % 2, dp // 2 % QUARTERS]).astype(jnp.int32)
    tok_rows = inputs.reshape(T_DEV, D)
    cotangent = out_grad.reshape(T_DEV, D)
    parts = [tok_rows] + [None] * (n_seq - 1)
    step = low
    while step > 1:
        for j in range(0, n_seq, 2 * step):
            parts[j + step] = swap(parts[j], "seq", step)
        step //= 2
    for j in range(0, n_seq, 2):
        parts[j + 1] = swap(parts[j], "seq", 1)
    tok_group = jnp.concatenate(parts)
    cotangent_partner = swap(cotangent, "seq", low)
    bias = block_bias(device, random_blocks[0], long_group[0] == 1, n_seq)
    bias = jnp.repeat(bias, BLOCK, axis=1)

    query = ((dot(tok_rows, w_query) + query_bias) * 0.125).astype(BF16)
    key = dot(tok_group, w_key).astype(BF16)
    value = (dot(tok_group, w_value) + value_bias).astype(BF16)
    mixed, lse = attn_fwd(query, key, value, bias)
    mixed_partner = swap(mixed, "seq", low)
    weights = (
        w_proj,
        proj_bias,
        ln1_gain.astype(F32),
        ln1_bias.astype(F32),
        w_up,
        up_bias,
        w_down,
        down_bias,
        ln2_gain.astype(F32),
        ln2_bias.astype(F32),
    )
    own = after_attention(tok_rows, mixed, cotangent, weights)
    mixed_partner, own["d_attn"] = lax.optimization_barrier((mixed_partner, own["d_attn"]))
    other = after_attention(parts[low], mixed_partner, cotangent_partner, weights)
    down_terms = half_share_grads(
        place,
        [(own["hidden"], own["d_branch"], other["hidden"], other["d_branch"])],
        n_seq,
        "grads_down",
    )
    up_terms = half_share_grads(
        place,
        [
            (own["normed_low"], own["d_pre"], other["normed_low"], other["d_pre"]),
            (mixed, own["d_attn"], mixed_partner, other["d_attn"]),
        ],
        n_seq,
        "grads_up_proj",
    )
    order = Order()
    low_masks = [1 << i for i in reversed(range(n_seq.bit_length() - 2))]
    seq_masks = [1] + [1 << i for i in reversed(range(1, n_seq.bit_length() - 1))]
    down = quarters_first(order, *down_terms, low_masks)
    next(down)
    up = columns_first(order, *up_terms, low_masks)
    next(up)
    for _ in low_masks:
        next(up)
        ups = order.last
        next(down)
        order.mark(*order.last, *ups)
    d_mixed = dot(own["d_attn"], w_proj, NT).astype(BF16)
    (d_mixed,) = order.after(d_mixed)
    d_query, d_key, d_value = attn_bwd(query, key, value, bias, d_mixed, lse)
    qkv = columns_first(
        order, *full_share_grads(place, tok_group, d_query, d_key, d_value, n_seq), seq_masks
    )
    next(qkv)

    d_key, d_value = order.after(d_key, d_value)
    term = (dot(d_key, w_key, NT) + dot(d_value, w_value, NT)).astype(BF16)
    term = term.reshape(low, 2, T_DEV, D).swapaxes(0, 1).reshape(n_seq, T_DEV, D)
    d_gain1, d_bias1, d_gain2, d_bias2 = own["small"]
    small = jnp.concatenate(
        [
            column_sum(d_query) * 0.125,
            column_sum(d_value),
            column_sum(own["d_attn"]),
            d_gain1,
            d_bias1,
            column_sum(own["d_pre"]),
            column_sum(own["d_branch"]),
            d_gain2,
            d_bias2,
        ]
    ).reshape(-1, D)
    input_grad = own["d_resid1"] + 0.125 * dot(d_query, w_query, NT)
    tail = token_chain(order, term, small)
    next(tail)
    rest = n_dp.bit_length() - 4

    def advance(chain, more=0):
        for _ in range(1 + more):
            next(chain)

    square = (D // n_seq, D)
    advance(up)
    advance(down, rest)
    for _ in seq_masks[1:]:
        advance(qkv)
    advance(down)
    for _ in seq_masks[1:]:
        advance(tail)
    advance(up)
    advance(down)
    advance(qkv)
    advance(up, rest)
    advance(down)
    advance(tail)
    advance(qkv)
    advance(up)
    advance(tail)
    advance(qkv)
    advance(tail, rest)
    advance(up)
    (grad_down,) = assemble(place, finish(down), [(FF // n_seq, D)], "assemble_down")
    order.mark(grad_down)
    advance(qkv, rest)
    advance(qkv)
    total, small = finish(tail)
    input_grad = input_grad + total
    small = small.reshape(-1)
    advance(qkv)
    grad_up, grad_proj = assemble(place, finish(up), [(D // n_seq, FF), square], "assemble_up")
    grad_query, grad_key, grad_value = assemble(place, finish(qkv), [square] * 3, "assemble_qkv")
    up_end = 5 * D + FF
    return (
        own["layer_out"].reshape(1, T_DEV, D),
        input_grad.reshape(1, T_DEV, D),
        grad_query,
        grad_key,
        grad_value,
        grad_proj,
        grad_up,
        grad_down,
        small[0:D],
        small[D : 2 * D],
        small[2 * D : 3 * D],
        small[3 * D : 4 * D],
        small[4 * D : 5 * D],
        small[5 * D : up_end],
        small[up_end : up_end + D],
        small[up_end + D : up_end + 2 * D],
        small[up_end + 2 * D : up_end + 3 * D],
    )


def solution(mesh):
    tokens = P("dp", "seq", None)
    return jax.shard_map(
        on_device,
        mesh=mesh,
        in_specs=(tokens,) + (P(),) * 15 + (P("dp"), tokens, tokens),
        out_specs=(tokens, tokens) + (P("seq", None),) * 6 + (P(),) * 9,
        check_vma=False,
    )
```

```python
import jax
import jax.numpy as jnp
from jax import lax
from jax.experimental import pallas as pl
from jax.experimental.pallas import tpu as pltpu
from jax.sharding import PartitionSpec as P

D = 768
HEADS = 12
HEAD = 64
FF = 3072
BLOCK = 64
RAND = 3
SLOTS = 2
SLOT_TOK = 128
T_DEV = 256
PER_SLOT = SLOT_TOK // BLOCK
PER_DEV = T_DEV // BLOCK

LN_EPS = 1e-05
MASKED = -1e30
F32 = jnp.float32
BF16 = jnp.bfloat16
MIB = 2**20

NN = (((1,), (0,)), ((), ()))
NT = (((1,), (1,)), ((), ()))
TN = (((0,), (0,)), ((), ()))


def dot(left, right, dims=NN):
    return lax.dot_general(left, right, dims, preferred_element_type=F32)


def seq_coords(blocks, is_long):
    device = blocks // PER_DEV
    within = blocks % PER_DEV
    slot_id = jnp.where(is_long, 0, within // PER_SLOT)
    position = jnp.where(is_long, blocks, device * PER_SLOT + within % PER_SLOT)
    return (slot_id, position)


def block_bias(device, chosen, is_long, n_seq):
    total_blocks = PER_DEV * n_seq
    last_pos = jnp.where(is_long, total_blocks, total_blocks // SLOTS) - 1
    own_slot, own_pos = seq_coords(device * PER_DEV + jnp.arange(PER_DEV), is_long)
    columns = jnp.arange(total_blocks)
    key_ids = (device ^ (columns // PER_DEV)) * PER_DEV + columns % PER_DEV
    key_slot, key_pos = seq_coords(key_ids, is_long)
    same = own_slot[:, None] == key_slot[None, :]
    ends = (key_pos == 0) | (key_pos == last_pos)
    near = jnp.abs(own_pos[:, None] - key_pos[None, :]) <= 1
    drawn = jnp.any(chosen[:, :, None] == key_pos[None, None, :], axis=1)
    is_global = (own_pos == 0) | (own_pos == last_pos)
    keep = same & (is_global[:, None] | ends[None, :] | near | drawn)
    return jnp.where(keep, 0.0, MASKED).astype(F32)


def joined(refs):
    return jnp.concatenate([ref[...] for ref in refs])


def attn_fwd_kernel(q_ref, bias_ref, *refs, parts):
    k_refs, v_refs, (mixed_ref, lse_ref) = refs[:parts], refs[parts : 2 * parts], refs[2 * parts :]
    query, key, value, bias = q_ref[...], joined(k_refs), joined(v_refs), bias_ref[...]
    rows, keys = query.shape[0], key.shape[0]
    first = lax.broadcasted_iota(jnp.int32, (rows, 2 * HEAD), 1) < HEAD
    outs, lses = [], []
    for head in range(2):
        own = jnp.where(first == (head == 0), query, jnp.zeros_like(query))
        scores = dot(own, key, NT).reshape(PER_DEV, BLOCK, keys) + bias[:, None, :]
        scores = scores.reshape(rows, keys)
        peak = jnp.max(scores, axis=1, keepdims=True)
        weight = jnp.exp(scores - peak)
        total = jnp.sum(weight, axis=1, keepdims=True)
        outs.append(dot((weight * (1.0 / total)).astype(BF16), value))
        lses.append(peak + jnp.log(total))
    mixed_ref[...] = jnp.where(first, outs[0], outs[1]).astype(BF16)
    lse_ref[...] = jnp.where(first, lses[0], lses[1])


def attn_bwd_kernel(q_ref, bias_ref, g_ref, lse_ref, *refs, parts):
    k_refs, v_refs, (dq_ref, dk_ref, dv_ref) = (
        refs[:parts],
        refs[parts : 2 * parts],
        refs[2 * parts :],
    )
    query, key, value, bias, grad = (
        q_ref[...],
        joined(k_refs),
        joined(v_refs),
        bias_ref[...],
        g_ref[...],
    )
    rows, keys = query.shape[0], key.shape[0]
    first = lax.broadcasted_iota(jnp.int32, (rows, 2 * HEAD), 1) < HEAD
    d_query, d_key, d_value = [], None, None
    for head in range(2):
        mine = first == (head == 0)
        own = jnp.where(mine, query, jnp.zeros_like(query))
        own_grad = jnp.where(mine, grad, jnp.zeros_like(grad))
        scores = dot(own, key, NT).reshape(PER_DEV, BLOCK, keys) + bias[:, None, :]
        probs = jnp.exp(scores.reshape(rows, keys) - lse_ref[:, HEAD * head : HEAD * head + 1])
        d_probs = dot(own_grad, value, NT)
        delta = jnp.sum(probs * d_probs, axis=1, keepdims=True)
        d_scores = (probs * (d_probs - delta)).astype(BF16)
        d_query.append(dot(d_scores, key))
        key_term = dot(d_scores, own, TN)
        value_term = dot(probs.astype(BF16), own_grad, TN)
        d_key = key_term if d_key is None else d_key + key_term
        d_value = value_term if d_value is None else d_value + value_term
    dq_ref[...] = jnp.where(first, d_query[0], d_query[1]).astype(BF16)
    dk_ref[...] = d_key.astype(BF16)
    dv_ref[...] = d_value.astype(BF16)


def cost(microseconds):
    return pl.CostEstimate(flops=int(microseconds * 1.1e9), bytes_accessed=0, transcendentals=0)


def head_pair(rows):
    return pl.BlockSpec((rows, 2 * HEAD), lambda i: (0, i))


def whole(shape):
    return pl.BlockSpec(shape, lambda *_: (0,) * len(shape))


def attn_fwd(query, bias, keys, values):
    rows = query.shape[0]
    return pl.pallas_call(
        lambda *refs: attn_fwd_kernel(*refs, parts=len(keys)),
        grid=(HEADS // 2,),
        in_specs=[head_pair(rows), whole(bias.shape)] + [head_pair(rows)] * (2 * len(keys)),
        out_specs=[head_pair(rows), head_pair(rows)],
        out_shape=[
            jax.ShapeDtypeStruct((rows, D), BF16),
            jax.ShapeDtypeStruct((rows, D), F32),
        ],
        compiler_params=pltpu.CompilerParams(vmem_limit_bytes=16 * MIB),
        cost_estimate=cost(10),
        name="attn_fwd",
    )(query, bias, *keys, *values)


def attn_bwd(query, bias, keys, values, grad, lse):
    rows = query.shape[0]
    count = rows * len(keys)
    return pl.pallas_call(
        lambda *refs: attn_bwd_kernel(*refs, parts=len(keys)),
        grid=(HEADS // 2,),
        in_specs=[head_pair(rows), whole(bias.shape), head_pair(rows), head_pair(rows)]
        + [head_pair(rows)] * (2 * len(keys)),
        out_specs=[head_pair(rows), head_pair(count), head_pair(count)],
        out_shape=[
            jax.ShapeDtypeStruct((rows, D), BF16),
            jax.ShapeDtypeStruct((count, D), BF16),
            jax.ShapeDtypeStruct((count, D), BF16),
        ],
        compiler_params=pltpu.CompilerParams(vmem_limit_bytes=24 * MIB),
        cost_estimate=cost(0.01),
        name="attn_bwd",
    )(query, bias, grad, lse, *keys, *values)


LANES = 384
QUARTERS = 4


def slot_of(quarter):
    return 2 * (quarter % 2) + quarter // 2


def half_share_kernel(place_ref, *refs, plan, low):
    keep_ref, send_ref, stage, turned = refs[4 * len(plan) :]
    top, low_own, x_own, z_own = (place_ref[i] for i in range(4))
    offset = 0
    for index, (rows, cols) in enumerate(plan):
        sides = (refs[4 * index : 4 * index + 2], refs[4 * index + 2 : 4 * index + 4])
        half = rows // 2
        share = half // low
        strip = min(half, LANES)
        piece_rows = share // QUARTERS
        for start in range(0, half, strip):
            lanes = pl.ds(pl.multiple_of(top * half + start, 128), strip)
            for side, (left, _) in enumerate(sides):
                turned[0:strip, side * T_DEV : (side + 1) * T_DEV] = left[:, lanes].T
            for block in range(cols // D):
                grad = sum(
                    dot(
                        turned[0:strip, side * T_DEV : (side + 1) * T_DEV],
                        right[:, block * D : (block + 1) * D],
                    )
                    for side, (_, right) in enumerate(sides)
                )
                for part in range(D // LANES):
                    column = block * D + part * LANES
                    side_x = column // (cols // 2)
                    slot = offset + (column % (cols // 2)) // LANES * piece_rows
                    for row in range(0, strip, piece_rows):
                        at = start + row
                        low_other = at // share
                        quarter = at % share // piece_rows
                        stage[
                            low_other ^ low_own,
                            side_x ^ x_own,
                            slot_of(quarter ^ z_own),
                            slot : slot + piece_rows,
                            :,
                        ] = grad[
                            row : row + piece_rows, part * LANES : (part + 1) * LANES
                        ].astype(BF16)
        offset += piece_rows * (cols // 2 // LANES)
    keep_ref[...] = stage[0 : low // 2]
    send_ref[...] = stage[low // 2 : low]


VMEM_SPEC = pl.BlockSpec(memory_space=pltpu.VMEM)
SMEM_SPEC = pl.BlockSpec(memory_space=pltpu.SMEM)


def half_share_grads(place, weights, n_seq, name):
    low = n_seq // 2
    plan = [(w[0].shape[1], w[1].shape[1]) for w in weights]
    piece_rows = sum(r // n_seq // QUARTERS * (c // 2 // LANES) for r, c in plan)
    shape = (2, QUARTERS, piece_rows, LANES)
    return pl.pallas_call(
        lambda *refs: half_share_kernel(*refs, plan=plan, low=low),
        in_specs=[SMEM_SPEC] + [VMEM_SPEC] * (4 * len(weights)),
        out_specs=[VMEM_SPEC] * 2,
        out_shape=[jax.ShapeDtypeStruct((low // 2, *shape), BF16)] * 2,
        scratch_shapes=[pltpu.VMEM((low, *shape), BF16), pltpu.VMEM((LANES, 2 * T_DEV), BF16)],
        compiler_params=pltpu.CompilerParams(vmem_limit_bytes=20 * MIB),
        cost_estimate=cost(0.01),
        name=name,
    )(place, *[array for weight in weights for array in weight])


def full_share_kernel(place_ref, dq_ref, dk_ref, dv_ref, sums_ref, *refs, n_seq):
    tokens, (keep_ref, send_ref, small_ref, stage, turned) = refs[:n_seq], refs[n_seq:]
    small_ref[2:, :] = sums_ref[2:, :]
    small_ref[0:1, :] = jnp.sum(dq_ref[...].astype(F32), axis=0, keepdims=True) * 0.125
    small_ref[1:2, :] = jnp.sum(dv_ref[...].astype(F32), axis=0, keepdims=True)
    top, low_own, x_own, z_own = (place_ref[i] for i in range(4))
    seq_own = top * (n_seq // 2) + low_own
    share = D // n_seq
    piece_rows = share // QUARTERS
    for start in range(0, D, LANES):
        for index, part in enumerate(tokens):
            turned[:, index * T_DEV : (index + 1) * T_DEV] = part[:, start : start + LANES].T
        for index, right in enumerate((dq_ref, dk_ref, dv_ref)):
            if index == 0:
                grad = dot(turned[:, 0:T_DEV], right[...]) * 0.125
            else:
                grad = dot(turned[...], right[...])
            for part in range(D // LANES):
                for row in range(0, LANES, piece_rows):
                    at = start + row
                    relative = (at // share) ^ seq_own
                    stage[
                        relative % 2 * (n_seq // 2) + relative // 2,
                        part ^ x_own,
                        slot_of((at % share // piece_rows) ^ z_own),
                        index * piece_rows : (index + 1) * piece_rows,
                        :,
                    ] = grad[row : row + piece_rows, part * LANES : (part + 1) * LANES].astype(BF16)
    keep_ref[...] = stage[0 : n_seq // 2]
    send_ref[...] = stage[n_seq // 2 : n_seq]


def full_share_grads(place, tokens, d_query, d_key, d_value, sums):
    n_seq = len(tokens)
    piece_rows = 3 * (D // n_seq // QUARTERS)
    shape = (2, QUARTERS, piece_rows, LANES)
    return pl.pallas_call(
        lambda *refs: full_share_kernel(*refs, n_seq=n_seq),
        in_specs=[SMEM_SPEC] + [VMEM_SPEC] * (4 + n_seq),
        out_specs=[VMEM_SPEC] * 3,
        out_shape=[jax.ShapeDtypeStruct((n_seq // 2, *shape), BF16)] * 2
        + [jax.ShapeDtypeStruct(sums.shape, F32)],
        scratch_shapes=[
            pltpu.VMEM((n_seq, *shape), BF16),
            pltpu.VMEM((LANES, n_seq * T_DEV), BF16),
        ],
        compiler_params=pltpu.CompilerParams(vmem_limit_bytes=20 * MIB),
        cost_estimate=cost(0.01),
        name="grads_qkv",
    )(place, d_query, d_key, d_value, sums, *tokens)


def assemble_kernel(place_ref, *refs, plan):
    outs = refs[len(refs) - len(plan) :]
    x_own, z_own = place_ref[2], place_ref[3]
    index = 0
    for ref in refs[: len(refs) - len(plan)]:
        for slot in range(ref.shape[0]):
            relative, column = index % QUARTERS, index // QUARTERS
            quarter = slot_of(relative) ^ z_own
            offset = 0
            for out, (rows, cols) in zip(outs, plan):
                height = rows // QUARTERS
                at = pl.ds(pl.multiple_of(quarter * height, 8), height)
                for part in range(cols // 2 // LANES):
                    lanes = pl.ds(
                        pl.multiple_of((column ^ x_own) * (cols // 2) + part * LANES, 128), LANES
                    )
                    out[at, lanes] = ref[slot, offset : offset + height, :].astype(F32)
                    offset += height
            index += 1


def assemble(place, pieces, plan, name):
    return pl.pallas_call(
        lambda *refs: assemble_kernel(*refs, plan=plan),
        in_specs=[SMEM_SPEC] + [VMEM_SPEC] * len(pieces),
        out_specs=[VMEM_SPEC] * len(plan),
        out_shape=[jax.ShapeDtypeStruct(shape, F32) for shape in plan],
        compiler_params=pltpu.CompilerParams(vmem_limit_bytes=12 * MIB),
        cost_estimate=cost(0.01),
        name=name,
    )(place, *pieces)


def swap(value, axis, mask):
    size = lax.axis_size(axis)
    return lax.ppermute(value, axis, [(i, i ^ mask) for i in range(size)])


def summed(terms):
    total = terms[0].astype(F32)
    for term in terms[1:]:
        total = total + term.astype(F32)
    return total.astype(BF16)


class Order:
    def __init__(self):
        self.last = ()

    def after(self, *arrays):
        return lax.optimization_barrier((*arrays, *self.last))[: len(arrays)]

    def mark(self, *arrays):
        self.last = arrays


def exchange(order, sends, swaps):
    order.mark(*sends)
    return [swap(send, axis, mask) for send, (axis, mask) in zip(sends, swaps)]


def sum_seq(order, keep, send, seq_masks):
    got = exchange(order, [send], [("seq", seq_masks[0])])
    yield
    terms = [keep, *order.after(*got)]
    for mask in seq_masks[1:]:
        half = terms[0].shape[0] // 2
        got = exchange(order, [summed([t[half:] for t in terms])], [("seq", mask)])
        yield
        terms = [t[:half] for t in terms] + list(order.after(*got))
    return [t[0] for t in terms]


def sum_dp_rest(order, piece):
    step = 2 * QUARTERS
    while step < lax.axis_size("dp"):
        got = exchange(order, [piece], [("dp", step)])
        yield
        piece = summed([piece, *order.after(*got)])
        step *= 2
    return piece


def gather_dp(order, own):
    for mask in (4, 2):
        got = exchange(order, [own], [("dp", mask)])
        yield
        own = jnp.concatenate([own, *order.after(*got)])
    got = exchange(order, [own], [("dp", 1)])
    yield
    (other,) = order.after(*got)
    return [own, other]


def columns_first(order, keep, send, seq_masks):
    terms = yield from sum_seq(order, keep, send, seq_masks)
    got = exchange(order, [summed([t[1] for t in terms])], [("dp", 1)])
    yield
    terms = [t[0] for t in terms] + list(order.after(*got))
    for mask in (2, 4):
        half = terms[0].shape[0] // 2
        got = exchange(order, [summed([t[half:] for t in terms])], [("dp", mask)])
        yield
        terms = [t[:half] for t in terms] + list(order.after(*got))
    piece = yield from sum_dp_rest(order, summed(terms))
    return (yield from gather_dp(order, piece))


def halves_first(order, keep, send, seq_masks):
    terms = yield from sum_seq(order, keep, send, seq_masks)
    half = QUARTERS // 2
    got = exchange(order, [summed([t[:, half:] for t in terms])], [("dp", 2)])
    yield
    terms = [t[:, :half] for t in terms] + list(order.after(*got))
    got = exchange(order, [summed([t[1] for t in terms])], [("dp", 1)])
    yield
    terms = [t[0] for t in terms] + list(order.after(*got))
    got = exchange(order, [summed([t[1:] for t in terms])], [("dp", 4)])
    yield
    piece = summed([t[:1] for t in terms] + list(order.after(*got)))
    piece = yield from sum_dp_rest(order, piece)
    return (yield from gather_dp(order, piece))


def token_kernel(dk_ref, dv_ref, wk_ref, wv_ref, small_ref, keep_ref, send_ref, *, n_seq):
    for part in range(n_seq):
        rows = slice(part * T_DEV, (part + 1) * T_DEV)
        term = dot(dk_ref[rows, :], wk_ref[...], NT) + dot(dv_ref[rows, :], wv_ref[...], NT)
        out = send_ref if part % 2 else keep_ref
        out[part // 2 * T_DEV : (part // 2 + 1) * T_DEV, :] = term.astype(BF16)
    small = small_ref[...]
    high = small.astype(BF16)
    at = n_seq // 2 * T_DEV
    send_ref[at : at + SMALL_ROWS, :] = high
    send_ref[at + SMALL_ROWS : at + 2 * SMALL_ROWS, :] = (small - high.astype(F32)).astype(BF16)


def token_terms(d_key, d_value, w_key, w_value, small, n_seq):
    rows = n_seq // 2 * T_DEV
    return pl.pallas_call(
        lambda *refs: token_kernel(*refs, n_seq=n_seq),
        in_specs=[VMEM_SPEC] * 5,
        out_specs=[VMEM_SPEC] * 2,
        out_shape=[
            jax.ShapeDtypeStruct((rows, D), BF16),
            jax.ShapeDtypeStruct((rows + 2 * SMALL_ROWS, D), BF16),
        ],
        compiler_params=pltpu.CompilerParams(vmem_limit_bytes=20 * MIB),
        cost_estimate=cost(12),
        name="token_terms",
    )(d_key, d_value, w_key, w_value, small)


def token_chain(order, keep, send, small, masks):
    n_dp = lax.axis_size("dp")
    terms = [keep]
    for step, mask in enumerate(masks):
        half = terms[0].shape[0] // 2
        high = small.astype(BF16)
        rest = (small - high.astype(F32)).astype(BF16)
        if step:
            send = jnp.concatenate([summed([t[half:] for t in terms]), high, rest])
            terms = [t[:half] for t in terms]
        got = exchange(order, [send], [("seq", mask)])
        yield
        (got,) = order.after(*got)
        at = terms[0].shape[0]
        small = high.astype(F32) + rest.astype(F32)
        small = small + got[at : at + SMALL_ROWS].astype(F32) + got[at + SMALL_ROWS :].astype(F32)
        terms = terms + [got[:at]]
    total = sum(t.astype(F32) for t in terms)
    step = 1
    while step < n_dp:
        got = exchange(order, [small], [("dp", step)])
        yield
        small = small + order.after(*got)[0]
        step *= 2
    return total, small


def finish(chain):
    try:
        next(chain)
    except StopIteration as stop:
        return stop.value
    raise ValueError("steps left")


VECTORS = ("proj_bias", "ln1_gain", "ln1_bias", "down_bias", "ln2_gain", "ln2_bias")
FF_CHUNK = 768
PACK = 1024
SMALL_ROWS = 16
GELU_SCALE = 0.7978845608028654
GELU_CUBE = 0.044715


def rows_mean(array):
    return jnp.mean(array, axis=1, keepdims=True)


def rows_sum(array):
    return jnp.sum(array, axis=0, keepdims=True)


def norm_back(grad, xhat, inv, gain):
    scaled = grad * gain
    return inv * (scaled - rows_mean(scaled) - xhat * rows_mean(scaled * xhat))


def layer_kernel(
    x_ref, mixed_ref, grad_ref, proj_ref, up_ref, down_ref, packed_ref, *refs, own
):
    slope = refs[-1]
    normed_ref, hidden_ref, d_branch_ref, d_pre_ref, d_attn_ref = refs[:5]
    chunks = [slice(start, start + FF_CHUNK) for start in range(0, FF, FF_CHUNK)]
    packed = [packed_ref[i * PACK : (i + 1) * PACK].astype(F32)[None, :] for i in range(9)]
    vec = {name: row[:, :D] for name, row in zip(VECTORS, packed)}
    up_bias = jnp.concatenate(packed[len(VECTORS) :], axis=1)
    resid = x_ref[...].astype(F32) + dot(mixed_ref[...], proj_ref[...]) + vec["proj_bias"]
    center = resid - rows_mean(resid)
    inv1 = lax.rsqrt(rows_mean(center * center) + LN_EPS)
    xhat1 = center * inv1
    normed = xhat1 * vec["ln1_gain"] + vec["ln1_bias"]
    normed_low = normed.astype(BF16)
    normed_ref[...] = normed_low
    branch = jnp.zeros_like(normed)
    for cols in chunks:
        pre = dot(normed_low, up_ref[:, cols]) + up_bias[:, cols]
        square = pre * pre
        bent = jnp.tanh(pre * (GELU_SCALE + GELU_SCALE * GELU_CUBE * square))
        half = 0.5 + 0.5 * bent
        slope[:, cols] = half + (0.5 * pre) * (1.0 - bent * bent) * (
            GELU_SCALE + 3.0 * GELU_SCALE * GELU_CUBE * square
        )
        hidden = (pre * half).astype(BF16)
        hidden_ref[:, cols] = hidden
        branch = branch + dot(hidden, down_ref[cols, :])
    resid = normed + (branch + vec["down_bias"])
    center = resid - rows_mean(resid)
    inv2 = lax.rsqrt(rows_mean(center * center) + LN_EPS)
    xhat2 = center * inv2
    grad = grad_ref[...].astype(F32)
    d_resid2 = norm_back(grad, xhat2, inv2, vec["ln2_gain"])
    d_branch = d_resid2.astype(BF16)
    d_branch_ref[...] = d_branch
    d_normed = d_resid2
    for index, cols in enumerate(chunks):
        d_hidden = dot(d_branch, down_ref[cols, :], NT).astype(BF16).astype(F32)
        d_pre = (d_hidden * slope[:, cols]).astype(BF16)
        d_pre_ref[:, cols] = d_pre
        if own:
            refs[7][5 + index : 6 + index, :] = rows_sum(d_pre.astype(F32))
        d_normed = d_normed + dot(d_pre, up_ref[:, cols], NT)
    d_resid1 = norm_back(d_normed, xhat1, inv1, vec["ln1_gain"])
    d_attn = d_resid1.astype(BF16)
    d_attn_ref[...] = d_attn
    if own:
        out_ref, resid_ref, sums_ref, d_mixed_ref = refs[5:9]
        out_ref[...] = (xhat2 * vec["ln2_gain"] + vec["ln2_bias"]).astype(BF16)
        resid_ref[...] = d_resid1
        sums_ref[0:2, :] = jnp.zeros((2, D), F32)
        sums_ref[2:3, :] = rows_sum(d_attn.astype(F32))
        sums_ref[3:4, :] = rows_sum(d_normed * xhat1)
        sums_ref[4:5, :] = rows_sum(d_normed)
        sums_ref[9:10, :] = rows_sum(d_branch.astype(F32))
        sums_ref[10:11, :] = rows_sum(grad * xhat2)
        sums_ref[11:12, :] = rows_sum(grad)
        sums_ref[12:, :] = jnp.zeros((SMALL_ROWS - 12, D), F32)
        d_mixed_ref[...] = dot(d_attn, proj_ref[...], NT).astype(BF16)


def after_attention(tokens, mixed, out_grad, weights, own):
    wide, tall = jax.ShapeDtypeStruct((T_DEV, FF), BF16), jax.ShapeDtypeStruct((T_DEV, D), BF16)
    names = ["normed_low", "hidden", "d_branch", "d_pre", "d_attn"]
    shapes = [tall, wide, tall, wide, tall]
    if own:
        names += ["layer_out", "d_resid1", "sums", "d_mixed"]
        shapes += [
            tall,
            jax.ShapeDtypeStruct((T_DEV, D), F32),
            jax.ShapeDtypeStruct((SMALL_ROWS, D), F32),
            tall,
        ]
    outs = pl.pallas_call(
        lambda *refs: layer_kernel(*refs, own=own),
        in_specs=[VMEM_SPEC] * (3 + len(weights)),
        out_specs=[VMEM_SPEC] * len(shapes),
        out_shape=shapes,
        scratch_shapes=[pltpu.VMEM((T_DEV, FF), F32)],
        compiler_params=pltpu.CompilerParams(vmem_limit_bytes=20 * MIB),
        cost_estimate=cost(9),
        name="layer_own" if own else "layer_other",
    )(tokens, mixed, out_grad, *weights)
    return dict(zip(names, outs))


def on_device(
    inputs,
    w_query,
    query_bias,
    w_key,
    w_value,
    value_bias,
    w_proj,
    proj_bias,
    ln1_gain,
    ln1_bias,
    w_up,
    up_bias,
    w_down,
    down_bias,
    ln2_gain,
    ln2_bias,
    long_group,
    random_blocks,
    out_grad,
):
    n_seq, n_dp = lax.axis_size("seq"), lax.axis_size("dp")
    device, dp = lax.axis_index("seq"), lax.axis_index("dp")
    low = n_seq // 2
    place = jnp.stack([device // low, device % low, dp % 2, dp // 2 % QUARTERS]).astype(jnp.int32)
    tok_rows = inputs.reshape(T_DEV, D)
    cotangent = out_grad.reshape(T_DEV, D)
    parts = [tok_rows] + [None] * (n_seq - 1)
    step = low
    while step > 1:
        for j in range(0, n_seq, 2 * step):
            parts[j + step] = swap(parts[j], "seq", step)
        step //= 2
    for j in range(0, n_seq, 2):
        parts[j + 1] = swap(parts[j], "seq", 1)
    cotangent_partner = swap(cotangent, "seq", low)
    bias = block_bias(device, random_blocks[0], long_group[0] == 1, n_seq)
    bias = jnp.repeat(bias, BLOCK, axis=1)
    vectors = (proj_bias, ln1_gain, ln1_bias, down_bias, ln2_gain, ln2_bias)
    packed = jnp.concatenate([jnp.pad(vector, (0, PACK - D)) for vector in vectors] + [up_bias])
    bias, packed = lax.optimization_barrier((bias, packed))
    weights = (w_proj, w_up, w_down, packed)

    query = ((dot(tok_rows, w_query) + query_bias) * 0.125).astype(BF16)
    keys = [dot(part, w_key).astype(BF16) for part in parts]
    values = [(dot(part, w_value) + value_bias).astype(BF16) for part in parts]
    mixed, lse = attn_fwd(query, bias, keys, values)
    mixed_partner = swap(mixed, "seq", low)
    own = after_attention(tok_rows, mixed, cotangent, weights, True)
    mixed_partner, own["d_attn"] = lax.optimization_barrier((mixed_partner, own["d_attn"]))
    other = after_attention(parts[low], mixed_partner, cotangent_partner, weights, False)
    down_terms = half_share_grads(
        place,
        [(own["hidden"], own["d_branch"], other["hidden"], other["d_branch"])],
        n_seq,
        "grads_down",
    )
    up_terms = half_share_grads(
        place,
        [
            (own["normed_low"], own["d_pre"], other["normed_low"], other["d_pre"]),
            (mixed, own["d_attn"], mixed_partner, other["d_attn"]),
        ],
        n_seq,
        "grads_up_proj",
    )
    order = Order()
    low_masks = [1 << i for i in reversed(range(n_seq.bit_length() - 2))]
    seq_masks = [1] + [1 << i for i in reversed(range(1, n_seq.bit_length() - 1))]
    down = halves_first(order, *down_terms, low_masks)
    next(down)
    up = columns_first(order, *up_terms, low_masks)
    next(up)
    for _ in low_masks:
        next(up)
        ups = order.last
        next(down)
        order.mark(*order.last, *ups)
    (d_mixed,) = order.after(own["d_mixed"])
    d_query, d_key, d_value = attn_bwd(query, bias, keys, values, d_mixed, lse)
    *qkv_terms, small = full_share_grads(place, parts, d_query, d_key, d_value, own["sums"])
    qkv = columns_first(order, *qkv_terms, seq_masks)
    next(qkv)
    next(up)
    next(down)
    d_key, d_value = order.after(d_key, d_value)
    token_parts = token_terms(d_key, d_value, w_key, w_value, small, n_seq)
    input_grad = own["d_resid1"] + 0.125 * dot(d_query, w_query, NT)
    tail = token_chain(order, *token_parts, small, seq_masks)
    next(tail)
    rest = n_dp.bit_length() - 4

    def advance(chain, more=0):
        for _ in range(1 + more):
            next(chain)

    square = (D // n_seq, D)
    for _ in seq_masks[1:]:
        advance(qkv)
    advance(up)
    for _ in seq_masks[1:]:
        advance(tail)
    advance(down)
    advance(up, rest)
    advance(qkv)
    advance(down, rest)
    advance(tail)
    advance(up)
    advance(qkv)
    advance(down)
    advance(tail)
    advance(up)
    advance(qkv)
    advance(down)
    advance(tail, rest)
    advance(qkv, rest)
    total, small = finish(tail)
    input_grad = input_grad + total
    order.mark(input_grad)
    small = small.reshape(-1)
    advance(qkv)
    grad_up, grad_proj = assemble(place, finish(up), [(D // n_seq, FF), square], "assemble_up")
    order.mark(grad_up)
    advance(qkv)
    (grad_down,) = assemble(place, finish(down), [(FF // n_seq, D)], "assemble_down")
    grad_query, grad_key, grad_value = assemble(place, finish(qkv), [square] * 3, "assemble_qkv")
    up_end = 5 * D + FF
    return (
        own["layer_out"].reshape(1, T_DEV, D),
        input_grad.reshape(1, T_DEV, D),
        grad_query,
        grad_key,
        grad_value,
        grad_proj,
        grad_up,
        grad_down,
        small[0:D],
        small[D : 2 * D],
        small[2 * D : 3 * D],
        small[3 * D : 4 * D],
        small[4 * D : 5 * D],
        small[5 * D : up_end],
        small[up_end : up_end + D],
        small[up_end + D : up_end + 2 * D],
        small[up_end + 2 * D : up_end + 3 * D],
    )


def solution(mesh):
    tokens = P("dp", "seq", None)
    return jax.shard_map(
        on_device,
        mesh=mesh,
        in_specs=(tokens,) + (P(),) * 15 + (P("dp"), tokens, tokens),
        out_specs=(tokens, tokens) + (P("seq", None),) * 6 + (P(),) * 9,
        check_vma=False,
    )
```

```python
import jax
import jax.numpy as jnp
from jax import lax
from jax.experimental import pallas as pl
from jax.experimental.pallas import tpu as pltpu
from jax.sharding import PartitionSpec as P

D = 768
HEADS = 12
HEAD = 64
FF = 3072
BLOCK = 64
RAND = 3
SLOTS = 2
SLOT_TOK = 128
T_DEV = 256
PER_SLOT = SLOT_TOK // BLOCK
PER_DEV = T_DEV // BLOCK

LN_EPS = 1e-05
MASKED = -1e30
F32 = jnp.float32
BF16 = jnp.bfloat16
MIB = 2**20

NN = (((1,), (0,)), ((), ()))
NT = (((1,), (1,)), ((), ()))
TN = (((0,), (0,)), ((), ()))


VMEM_SPEC = pl.BlockSpec(memory_space=pltpu.VMEM)
SMEM_SPEC = pl.BlockSpec(memory_space=pltpu.SMEM)


def dot(left, right, dims=NN):
    return lax.dot_general(left, right, dims, preferred_element_type=F32)


def coords(device, within, is_long):
    slot = jnp.where(is_long, 0, within // PER_SLOT)
    position = jnp.where(
        is_long, device * PER_DEV + within, device * PER_SLOT + within % PER_SLOT
    )
    return slot, position


def bias_kernel(place_ref, long_ref, chosen_ref, bias_ref, *, n_seq):
    device = place_ref[0] * (n_seq // 2) + place_ref[1]
    is_long = long_ref[0] == 1
    last = jnp.where(is_long, n_seq * PER_DEV, n_seq * PER_DEV // SLOTS) - 1
    column = lax.broadcasted_iota(jnp.int32, (1, n_seq * T_DEV), 1)
    key_slot, key_pos = coords(
        (column // T_DEV) ^ device, column % T_DEV // BLOCK, is_long
    )
    ends = (key_pos == 0) | (key_pos == last)
    for block in range(PER_DEV):
        slot, position = coords(device, block, is_long)
        keep = ends | (jnp.abs(key_pos - position) <= 1)
        for draw in range(RAND):
            keep = keep | (key_pos == chosen_ref[0, block, draw])
        keep = keep | (position == 0) | (position == last)
        keep = keep & (key_slot == slot)
        bias_ref[block : block + 1, :] = jnp.where(keep, 0.0, MASKED)


def block_bias(place, long_group, random_blocks, n_seq):
    return pl.pallas_call(
        lambda *refs: bias_kernel(*refs, n_seq=n_seq),
        in_specs=[SMEM_SPEC] * 3,
        out_specs=VMEM_SPEC,
        out_shape=jax.ShapeDtypeStruct((PER_DEV, n_seq * T_DEV), F32),
        compiler_params=pltpu.CompilerParams(vmem_limit_bytes=4 * MIB),
        cost_estimate=cost(1),
        name="block_bias",
    )(place, long_group, random_blocks)


def project_kernel(wk_ref, wv_ref, v_bias_ref, *refs, count, with_query):
    parts, refs = refs[:count], refs[count:]
    if with_query:
        wq_ref, q_bias_ref, q_ref, *refs = refs
        query = dot(parts[0][...], wq_ref[...]) + q_bias_ref[...].astype(F32)[None, :]
        q_ref[...] = (query * 0.125).astype(BF16)
    v_bias = v_bias_ref[...].astype(F32)[None, :]
    for index, part in enumerate(parts):
        refs[2 * index][...] = dot(part[...], wk_ref[...]).astype(BF16)
        refs[2 * index + 1][...] = (dot(part[...], wv_ref[...]) + v_bias).astype(BF16)


def project(parts, w_key, w_value, value_bias, *query):
    count = 2 * len(parts) + (1 if query else 0)
    return pl.pallas_call(
        lambda *refs: project_kernel(*refs, count=len(parts), with_query=bool(query)),
        in_specs=[VMEM_SPEC] * (3 + len(parts) + len(query)),
        out_specs=[VMEM_SPEC] * count,
        out_shape=[jax.ShapeDtypeStruct((T_DEV, D), BF16)] * count,
        compiler_params=pltpu.CompilerParams(vmem_limit_bytes=16 * MIB),
        cost_estimate=cost(1),
        name="project_near" if query else "project_far",
    )(w_key, w_value, value_bias, *parts, *query)


def joined(refs):
    return jnp.concatenate([ref[...] for ref in refs])


def attn_fwd_kernel(q_ref, bias_ref, *refs, parts):
    k_refs, v_refs, (mixed_ref, lse_ref) = refs[:parts], refs[parts : 2 * parts], refs[2 * parts :]
    query, key, value, bias = q_ref[...], joined(k_refs), joined(v_refs), bias_ref[...]
    rows, keys = query.shape[0], key.shape[0]
    first = lax.broadcasted_iota(jnp.int32, (rows, 2 * HEAD), 1) < HEAD
    outs, lses = [], []
    for head in range(2):
        own = jnp.where(first == (head == 0), query, jnp.zeros_like(query))
        scores = dot(own, key, NT).reshape(PER_DEV, BLOCK, keys) + bias[:, None, :]
        scores = scores.reshape(rows, keys)
        peak = jnp.max(scores, axis=1, keepdims=True)
        weight = jnp.exp(scores - peak)
        total = jnp.sum(weight, axis=1, keepdims=True)
        outs.append(dot(weight.astype(BF16), value) * (1.0 / total))
        lses.append(peak + jnp.log(total))
    mixed_ref[...] = jnp.where(first, outs[0], outs[1]).astype(BF16)
    lse_ref[...] = jnp.where(first, lses[0], lses[1])


def attn_bwd_kernel(q_ref, bias_ref, g_ref, lse_ref, *refs, parts):
    k_refs, v_refs, (dq_ref, dk_ref, dv_ref) = (
        refs[:parts],
        refs[parts : 2 * parts],
        refs[2 * parts :],
    )
    query, key, value, bias, grad = (
        q_ref[...],
        joined(k_refs),
        joined(v_refs),
        bias_ref[...],
        g_ref[...],
    )
    rows, keys = query.shape[0], key.shape[0]
    first = lax.broadcasted_iota(jnp.int32, (rows, 2 * HEAD), 1) < HEAD
    d_query, d_key, d_value = [], None, None
    for head in range(2):
        mine = first == (head == 0)
        own = jnp.where(mine, query, jnp.zeros_like(query))
        own_grad = jnp.where(mine, grad, jnp.zeros_like(grad))
        scores = dot(own, key, NT).reshape(PER_DEV, BLOCK, keys) + bias[:, None, :]
        probs = jnp.exp(scores.reshape(rows, keys) - lse_ref[:, HEAD * head : HEAD * head + 1])
        d_probs = dot(own_grad, value, NT)
        delta = jnp.sum(probs * d_probs, axis=1, keepdims=True)
        d_scores = (probs * (d_probs - delta)).astype(BF16)
        d_query.append(dot(d_scores, key))
        key_term = dot(d_scores, own, TN)
        value_term = dot(probs.astype(BF16), own_grad, TN)
        d_key = key_term if d_key is None else d_key + key_term
        d_value = value_term if d_value is None else d_value + value_term
    dq_ref[...] = jnp.where(first, d_query[0], d_query[1]).astype(BF16)
    dk_ref[...] = d_key.astype(BF16)
    dv_ref[...] = d_value.astype(BF16)


def cost(microseconds):
    return pl.CostEstimate(flops=int(microseconds * 1.1e9), bytes_accessed=0, transcendentals=0)


def head_pair(rows):
    return pl.BlockSpec((rows, 2 * HEAD), lambda i: (0, i))


def whole(shape):
    return pl.BlockSpec(shape, lambda *_: (0,) * len(shape))


def attn_fwd(query, bias, keys, values):
    rows = query.shape[0]
    return pl.pallas_call(
        lambda *refs: attn_fwd_kernel(*refs, parts=len(keys)),
        grid=(HEADS // 2,),
        in_specs=[head_pair(rows), whole(bias.shape)] + [head_pair(rows)] * (2 * len(keys)),
        out_specs=[head_pair(rows), head_pair(rows)],
        out_shape=[
            jax.ShapeDtypeStruct((rows, D), BF16),
            jax.ShapeDtypeStruct((rows, D), F32),
        ],
        compiler_params=pltpu.CompilerParams(vmem_limit_bytes=16 * MIB),
        cost_estimate=cost(10),
        name="attn_fwd",
    )(query, bias, *keys, *values)


def attn_bwd(query, bias, keys, values, grad, lse):
    rows = query.shape[0]
    count = rows * len(keys)
    return pl.pallas_call(
        lambda *refs: attn_bwd_kernel(*refs, parts=len(keys)),
        grid=(HEADS // 2,),
        in_specs=[head_pair(rows), whole(bias.shape), head_pair(rows), head_pair(rows)]
        + [head_pair(rows)] * (2 * len(keys)),
        out_specs=[head_pair(rows), head_pair(count), head_pair(count)],
        out_shape=[
            jax.ShapeDtypeStruct((rows, D), BF16),
            jax.ShapeDtypeStruct((count, D), BF16),
            jax.ShapeDtypeStruct((count, D), BF16),
        ],
        compiler_params=pltpu.CompilerParams(vmem_limit_bytes=24 * MIB),
        cost_estimate=cost(0.01),
        name="attn_bwd",
    )(query, bias, grad, lse, *keys, *values)


LANES = 384
QUARTERS = 4


def slot_of(quarter):
    return 2 * (quarter % 2) + quarter // 2


def half_share_kernel(place_ref, *refs, plan, low):
    keep_ref, send_ref, stage, turned = refs[4 * len(plan) :]
    top, low_own, x_own, z_own = (place_ref[i] for i in range(4))
    offset = 0
    for index, (rows, cols) in enumerate(plan):
        sides = (refs[4 * index : 4 * index + 2], refs[4 * index + 2 : 4 * index + 4])
        half = rows // 2
        share = half // low
        strip = min(half, LANES)
        piece_rows = share // QUARTERS
        for start in range(0, half, strip):
            lanes = pl.ds(pl.multiple_of(top * half + start, 128), strip)
            for side, (left, _) in enumerate(sides):
                turned[0:strip, side * T_DEV : (side + 1) * T_DEV] = left[:, lanes].T
            for block in range(cols // D):
                grad = sum(
                    dot(
                        turned[0:strip, side * T_DEV : (side + 1) * T_DEV],
                        right[:, block * D : (block + 1) * D],
                    )
                    for side, (_, right) in enumerate(sides)
                )
                for part in range(D // LANES):
                    column = block * D + part * LANES
                    side_x = column // (cols // 2)
                    slot = offset + (column % (cols // 2)) // LANES * piece_rows
                    for row in range(0, strip, piece_rows):
                        at = start + row
                        low_other = at // share
                        quarter = at % share // piece_rows
                        stage[
                            low_other ^ low_own,
                            side_x ^ x_own,
                            slot_of(quarter ^ z_own),
                            slot : slot + piece_rows,
                            :,
                        ] = grad[
                            row : row + piece_rows, part * LANES : (part + 1) * LANES
                        ].astype(BF16)
        offset += piece_rows * (cols // 2 // LANES)
    keep_ref[...] = stage[0 : low // 2]
    send_ref[...] = stage[low // 2 : low]


def half_share_grads(place, weights, n_seq, name):
    low = n_seq // 2
    plan = [(w[0].shape[1], w[1].shape[1]) for w in weights]
    piece_rows = sum(r // n_seq // QUARTERS * (c // 2 // LANES) for r, c in plan)
    shape = (2, QUARTERS, piece_rows, LANES)
    return pl.pallas_call(
        lambda *refs: half_share_kernel(*refs, plan=plan, low=low),
        in_specs=[SMEM_SPEC] + [VMEM_SPEC] * (4 * len(weights)),
        out_specs=[VMEM_SPEC] * 2,
        out_shape=[jax.ShapeDtypeStruct((low // 2, *shape), BF16)] * 2,
        scratch_shapes=[pltpu.VMEM((low, *shape), BF16), pltpu.VMEM((LANES, 2 * T_DEV), BF16)],
        compiler_params=pltpu.CompilerParams(vmem_limit_bytes=20 * MIB),
        cost_estimate=cost(0.01),
        name=name,
    )(place, *[array for weight in weights for array in weight])


def full_share_kernel(place_ref, dq_ref, dk_ref, dv_ref, sums_ref, *refs, n_seq):
    tokens, (keep_ref, send_ref, small_ref, stage, turned) = refs[:n_seq], refs[n_seq:]
    small_ref[2:, :] = sums_ref[2:, :]
    small_ref[0:1, :] = jnp.sum(dq_ref[...].astype(F32), axis=0, keepdims=True) * 0.125
    small_ref[1:2, :] = jnp.sum(dv_ref[...].astype(F32), axis=0, keepdims=True)
    top, low_own, x_own, z_own = (place_ref[i] for i in range(4))
    seq_own = top * (n_seq // 2) + low_own
    share = D // n_seq
    piece_rows = share // QUARTERS
    for start in range(0, D, LANES):
        for index, part in enumerate(tokens):
            turned[:, index * T_DEV : (index + 1) * T_DEV] = part[:, start : start + LANES].T
        for index, right in enumerate((dq_ref, dk_ref, dv_ref)):
            if index == 0:
                grad = dot(turned[:, 0:T_DEV], right[...]) * 0.125
            else:
                grad = dot(turned[...], right[...])
            for part in range(D // LANES):
                for row in range(0, LANES, piece_rows):
                    at = start + row
                    relative = (at // share) ^ seq_own
                    stage[
                        relative % 2 * (n_seq // 2) + relative // 2,
                        part ^ x_own,
                        slot_of((at % share // piece_rows) ^ z_own),
                        index * piece_rows : (index + 1) * piece_rows,
                        :,
                    ] = grad[row : row + piece_rows, part * LANES : (part + 1) * LANES].astype(BF16)
    keep_ref[...] = stage[0 : n_seq // 2]
    send_ref[...] = stage[n_seq // 2 : n_seq]


def full_share_grads(place, tokens, d_query, d_key, d_value, sums):
    n_seq = len(tokens)
    piece_rows = 3 * (D // n_seq // QUARTERS)
    shape = (2, QUARTERS, piece_rows, LANES)
    return pl.pallas_call(
        lambda *refs: full_share_kernel(*refs, n_seq=n_seq),
        in_specs=[SMEM_SPEC] + [VMEM_SPEC] * (4 + n_seq),
        out_specs=[VMEM_SPEC] * 3,
        out_shape=[jax.ShapeDtypeStruct((n_seq // 2, *shape), BF16)] * 2
        + [jax.ShapeDtypeStruct(sums.shape, F32)],
        scratch_shapes=[
            pltpu.VMEM((n_seq, *shape), BF16),
            pltpu.VMEM((LANES, n_seq * T_DEV), BF16),
        ],
        compiler_params=pltpu.CompilerParams(vmem_limit_bytes=20 * MIB),
        cost_estimate=cost(0.01),
        name="grads_qkv",
    )(place, d_query, d_key, d_value, sums, *tokens)


def assemble_kernel(place_ref, *refs, plan):
    outs = refs[len(refs) - len(plan) :]
    x_own, z_own = place_ref[2], place_ref[3]
    index = 0
    for ref in refs[: len(refs) - len(plan)]:
        for slot in range(ref.shape[0]):
            relative, column = index % QUARTERS, index // QUARTERS
            quarter = slot_of(relative) ^ z_own
            offset = 0
            for out, (rows, cols) in zip(outs, plan):
                height = rows // QUARTERS
                at = pl.ds(pl.multiple_of(quarter * height, 8), height)
                for part in range(cols // 2 // LANES):
                    lanes = pl.ds(
                        pl.multiple_of((column ^ x_own) * (cols // 2) + part * LANES, 128), LANES
                    )
                    out[at, lanes] = ref[slot, offset : offset + height, :].astype(F32)
                    offset += height
            index += 1


def assemble(place, pieces, plan, name):
    return pl.pallas_call(
        lambda *refs: assemble_kernel(*refs, plan=plan),
        in_specs=[SMEM_SPEC] + [VMEM_SPEC] * len(pieces),
        out_specs=[VMEM_SPEC] * len(plan),
        out_shape=[jax.ShapeDtypeStruct(shape, F32) for shape in plan],
        compiler_params=pltpu.CompilerParams(vmem_limit_bytes=12 * MIB),
        cost_estimate=cost(0.01),
        name=name,
    )(place, *pieces)


def swap(value, axis, mask):
    size = lax.axis_size(axis)
    return lax.ppermute(value, axis, [(i, i ^ mask) for i in range(size)])


def summed(terms):
    total = terms[0].astype(F32)
    for term in terms[1:]:
        total = total + term.astype(F32)
    return total.astype(BF16)


STEPS = "TUCDUCDCUCDTUCDCTUTDTC"


class Order:
    def __init__(self):
        self.last = ()

    def after(self, *arrays):
        return lax.optimization_barrier((*arrays, *self.last))[: len(arrays)]

    def mark(self, *arrays):
        self.last = arrays


def exchange(order, sends, swaps):
    order.mark(*sends)
    return [swap(send, axis, mask) for send, (axis, mask) in zip(sends, swaps)]


def sum_seq(order, keep, send, seq_masks):
    got = exchange(order, [send], [("seq", seq_masks[0])])
    yield
    terms = [keep, *order.after(*got)]
    for step, mask in enumerate(seq_masks[1:]):
        half = terms[0].shape[0] // 2
        got = exchange(order, [summed([t[half:] for t in terms])], [("seq", mask)])
        if step == 0:
            yield
        terms = [t[:half] for t in terms] + list(order.after(*got))
    return [t[0] for t in terms]


def sum_dp_rest(order, piece):
    step = 2 * QUARTERS
    while step < lax.axis_size("dp"):
        got = exchange(order, [piece], [("dp", step)])
        piece = summed([piece, *order.after(*got)])
        step *= 2
    return piece


def gather_dp(order, piece):
    got = exchange(order, [piece], [("dp", 4)])
    yield
    first = jnp.concatenate([piece, *order.after(*got)])
    got = exchange(order, [first, first], [("dp", 2), ("dp", 1)])
    yield
    second, far_first = order.after(*got)
    got = exchange(order, [second], [("dp", 1)])
    yield
    return [first, second, far_first, *order.after(*got)]


def columns_first(order, keep, send, seq_masks):
    terms = yield from sum_seq(order, keep, send, seq_masks)
    got = exchange(order, [summed([t[1] for t in terms])], [("dp", 1)])
    yield
    terms = [t[0] for t in terms] + list(order.after(*got))
    for mask in (2, 4):
        half = terms[0].shape[0] // 2
        got = exchange(order, [summed([t[half:] for t in terms])], [("dp", mask)])
        yield
        terms = [t[:half] for t in terms] + list(order.after(*got))
    piece = sum_dp_rest(order, summed(terms))
    return (yield from gather_dp(order, piece))


def both_first(order, keep, send, seq_masks):
    got = exchange(order, [send], [("seq", seq_masks[0])])
    yield
    terms = [keep, *order.after(*got)]
    for mask in seq_masks[1:-1]:
        count = terms[0].shape[0] // 2
        got = exchange(order, [summed([t[count:] for t in terms])], [("seq", mask)])
        terms = [t[:count] for t in terms] + list(order.after(*got))
    along_seq, along_dp = ("seq", seq_masks[-1]), ("dp", 1)
    half = QUARTERS // 2
    low, high = [t[:, :, :half] for t in terms], [t[:, :, half:] for t in terms]
    got = exchange(
        order,
        [summed([t[1] for t in low]), summed([t[:, 1] for t in high])],
        [along_seq, along_dp],
    )
    yield
    low_got, high_got = order.after(*got)
    low = [t[0] for t in low] + [low_got]
    high = [t[:, 0] for t in high] + [high_got]
    got = exchange(
        order,
        [summed([t[1] for t in low]), summed([t[1] for t in high])],
        [along_dp, along_seq],
    )
    yield
    low_got, high_got = order.after(*got)
    low = [t[0] for t in low] + [low_got]
    high = [t[0] for t in high] + [high_got]
    got = exchange(order, [summed(high)], [("dp", 2)])
    yield
    terms = low + list(order.after(*got))
    got = exchange(order, [summed([t[1:] for t in terms])], [("dp", 4)])
    yield
    terms = [t[:1] for t in terms] + list(order.after(*got))
    piece = sum_dp_rest(order, summed(terms))
    return (yield from gather_dp(order, piece))


def halves_first(order, keep, send, seq_masks):
    terms = yield from sum_seq(order, keep, send, seq_masks)
    half = QUARTERS // 2
    got = exchange(order, [summed([t[:, half:] for t in terms])], [("dp", 2)])
    yield
    terms = [t[:, :half] for t in terms] + list(order.after(*got))
    got = exchange(order, [summed([t[1] for t in terms])], [("dp", 1)])
    yield
    terms = [t[0] for t in terms] + list(order.after(*got))
    got = exchange(order, [summed([t[1:] for t in terms])], [("dp", 4)])
    yield
    piece = summed([t[:1] for t in terms] + list(order.after(*got)))
    piece = sum_dp_rest(order, piece)
    return (yield from gather_dp(order, piece))


def token_kernel(dk_ref, dv_ref, wk_ref, wv_ref, small_ref, keep_ref, send_ref, *, n_seq):
    for part in range(n_seq):
        rows = slice(part * T_DEV, (part + 1) * T_DEV)
        term = dot(dk_ref[rows, :], wk_ref[...], NT) + dot(dv_ref[rows, :], wv_ref[...], NT)
        out = send_ref if part % 2 else keep_ref
        out[part // 2 * T_DEV : (part // 2 + 1) * T_DEV, :] = term.astype(BF16)
    small = small_ref[...]
    high = small.astype(BF16)
    at = n_seq // 2 * T_DEV
    send_ref[at : at + SMALL_ROWS, :] = high
    send_ref[at + SMALL_ROWS : at + 2 * SMALL_ROWS, :] = (small - high.astype(F32)).astype(BF16)


def token_terms(d_key, d_value, w_key, w_value, small, n_seq):
    rows = n_seq // 2 * T_DEV
    return pl.pallas_call(
        lambda *refs: token_kernel(*refs, n_seq=n_seq),
        in_specs=[VMEM_SPEC] * 5,
        out_specs=[VMEM_SPEC] * 2,
        out_shape=[
            jax.ShapeDtypeStruct((rows, D), BF16),
            jax.ShapeDtypeStruct((rows + 2 * SMALL_ROWS, D), BF16),
        ],
        compiler_params=pltpu.CompilerParams(vmem_limit_bytes=20 * MIB),
        cost_estimate=cost(12),
        name="token_terms",
    )(d_key, d_value, w_key, w_value, small)


def token_chain(order, keep, send, small, masks):
    n_dp = lax.axis_size("dp")
    terms = [keep]
    for step, mask in enumerate(masks):
        half = terms[0].shape[0] // 2
        high = small.astype(BF16)
        rest = (small - high.astype(F32)).astype(BF16)
        if step:
            send = jnp.concatenate([summed([t[half:] for t in terms]), high, rest])
            terms = [t[:half] for t in terms]
        got = exchange(order, [send], [("seq", mask)])
        if step < 2:
            yield
        (got,) = order.after(*got)
        at = terms[0].shape[0]
        small = high.astype(F32) + rest.astype(F32)
        small = small + got[at : at + SMALL_ROWS].astype(F32) + got[at + SMALL_ROWS :].astype(F32)
        terms = terms + [got[:at]]
    total = sum(t.astype(F32) for t in terms)
    step = 1
    while step < n_dp:
        got = exchange(order, [small], [("dp", step)])
        if step < 2 * QUARTERS:
            yield
        small = small + order.after(*got)[0]
        step *= 2
    return total, small


def finish(chain):
    try:
        next(chain)
    except StopIteration as stop:
        return stop.value
    raise ValueError("steps left")


VECTORS = ("proj_bias", "ln1_gain", "ln1_bias", "down_bias", "ln2_gain", "ln2_bias")
FF_CHUNK = 768
PACK = 1024
SMALL_ROWS = 16
GELU_SCALE = 0.7978845608028654
GELU_CUBE = 0.044715


def rows_mean(array):
    return jnp.mean(array, axis=1, keepdims=True)


def rows_sum(array):
    return jnp.sum(array, axis=0, keepdims=True)


def norm_back(grad, xhat, inv, gain):
    scaled = grad * gain
    return inv * (scaled - rows_mean(scaled) - xhat * rows_mean(scaled * xhat))


def layer_kernel(
    x_ref, mixed_ref, grad_ref, proj_ref, up_ref, down_ref, packed_ref, *refs, own
):
    slope = refs[-1]
    normed_ref, hidden_ref, d_branch_ref, d_pre_ref, d_attn_ref = refs[:5]
    chunks = [slice(start, start + FF_CHUNK) for start in range(0, FF, FF_CHUNK)]
    packed = [packed_ref[i * PACK : (i + 1) * PACK].astype(F32)[None, :] for i in range(9)]
    vec = {name: row[:, :D] for name, row in zip(VECTORS, packed)}
    up_bias = jnp.concatenate(packed[len(VECTORS) :], axis=1)
    resid = x_ref[...].astype(F32) + dot(mixed_ref[...], proj_ref[...]) + vec["proj_bias"]
    center = resid - rows_mean(resid)
    inv1 = lax.rsqrt(rows_mean(center * center) + LN_EPS)
    xhat1 = center * inv1
    normed = xhat1 * vec["ln1_gain"] + vec["ln1_bias"]
    normed_low = normed.astype(BF16)
    normed_ref[...] = normed_low
    branch = jnp.zeros_like(normed)
    for cols in chunks:
        pre = dot(normed_low, up_ref[:, cols]) + up_bias[:, cols]
        square = pre * pre
        bent = jnp.tanh(pre * (GELU_SCALE + GELU_SCALE * GELU_CUBE * square))
        half = 0.5 + 0.5 * bent
        slope[:, cols] = half + (0.5 * pre) * (1.0 - bent * bent) * (
            GELU_SCALE + 3.0 * GELU_SCALE * GELU_CUBE * square
        )
        hidden = (pre * half).astype(BF16)
        hidden_ref[:, cols] = hidden
        branch = branch + dot(hidden, down_ref[cols, :])
    resid = normed + (branch + vec["down_bias"])
    center = resid - rows_mean(resid)
    inv2 = lax.rsqrt(rows_mean(center * center) + LN_EPS)
    xhat2 = center * inv2
    grad = grad_ref[...].astype(F32)
    d_resid2 = norm_back(grad, xhat2, inv2, vec["ln2_gain"])
    d_branch = d_resid2.astype(BF16)
    d_branch_ref[...] = d_branch
    d_normed = d_resid2
    for index, cols in enumerate(chunks):
        d_hidden = dot(d_branch, down_ref[cols, :], NT).astype(BF16).astype(F32)
        d_pre = (d_hidden * slope[:, cols]).astype(BF16)
        d_pre_ref[:, cols] = d_pre
        if own:
            refs[7][5 + index : 6 + index, :] = rows_sum(d_pre.astype(F32))
        d_normed = d_normed + dot(d_pre, up_ref[:, cols], NT)
    d_resid1 = norm_back(d_normed, xhat1, inv1, vec["ln1_gain"])
    d_attn = d_resid1.astype(BF16)
    d_attn_ref[...] = d_attn
    if own:
        out_ref, resid_ref, sums_ref, d_mixed_ref = refs[5:9]
        out_ref[...] = (xhat2 * vec["ln2_gain"] + vec["ln2_bias"]).astype(BF16)
        resid_ref[...] = d_resid1
        sums_ref[0:2, :] = jnp.zeros((2, D), F32)
        sums_ref[2:3, :] = rows_sum(d_attn.astype(F32))
        sums_ref[3:4, :] = rows_sum(d_normed * xhat1)
        sums_ref[4:5, :] = rows_sum(d_normed)
        sums_ref[9:10, :] = rows_sum(d_branch.astype(F32))
        sums_ref[10:11, :] = rows_sum(grad * xhat2)
        sums_ref[11:12, :] = rows_sum(grad)
        sums_ref[12:, :] = jnp.zeros((SMALL_ROWS - 12, D), F32)
        d_mixed_ref[...] = dot(d_attn, proj_ref[...], NT).astype(BF16)


def after_attention(tokens, mixed, out_grad, weights, own):
    wide, tall = jax.ShapeDtypeStruct((T_DEV, FF), BF16), jax.ShapeDtypeStruct((T_DEV, D), BF16)
    names = ["normed_low", "hidden", "d_branch", "d_pre", "d_attn"]
    shapes = [tall, wide, tall, wide, tall]
    if own:
        names += ["layer_out", "d_resid1", "sums", "d_mixed"]
        shapes += [
            tall,
            jax.ShapeDtypeStruct((T_DEV, D), F32),
            jax.ShapeDtypeStruct((SMALL_ROWS, D), F32),
            tall,
        ]
    outs = pl.pallas_call(
        lambda *refs: layer_kernel(*refs, own=own),
        in_specs=[VMEM_SPEC] * (3 + len(weights)),
        out_specs=[VMEM_SPEC] * len(shapes),
        out_shape=shapes,
        scratch_shapes=[pltpu.VMEM((T_DEV, FF), F32)],
        compiler_params=pltpu.CompilerParams(vmem_limit_bytes=20 * MIB),
        cost_estimate=cost(9),
        name="layer_own" if own else "layer_other",
    )(tokens, mixed, out_grad, *weights)
    return dict(zip(names, outs))


def on_device(
    inputs,
    w_query,
    query_bias,
    w_key,
    w_value,
    value_bias,
    w_proj,
    proj_bias,
    ln1_gain,
    ln1_bias,
    w_up,
    up_bias,
    w_down,
    down_bias,
    ln2_gain,
    ln2_bias,
    long_group,
    random_blocks,
    out_grad,
):
    n_seq, n_dp = lax.axis_size("seq"), lax.axis_size("dp")
    device, dp = lax.axis_index("seq"), lax.axis_index("dp")
    low = n_seq // 2
    low_bits = low.bit_length() - 1
    place = jnp.stack(
        [device >> low_bits, device & (low - 1), dp & 1, (dp >> 1) & (QUARTERS - 1)]
    ).astype(jnp.int32)
    tok_rows = inputs.reshape(T_DEV, D)
    cotangent = out_grad.reshape(T_DEV, D)
    bias = block_bias(place, long_group, random_blocks, n_seq)
    parts = [tok_rows, swap(tok_rows, "seq", 1)] + [None] * (n_seq - 2)
    step = low
    while step > 1:
        for j in range(0, n_seq, 2 * step):
            parts[j + step] = swap(parts[j], "seq", step)
        step //= 2
    query, *near = project(parts[:2], w_key, w_value, value_bias, w_query, query_bias)
    *parts[2::2], bias, query = lax.optimization_barrier((*parts[2::2], bias, query))
    for j in range(2, n_seq, 2):
        parts[j + 1] = swap(parts[j], "seq", 1)
    cotangent_partner = swap(cotangent, "seq", low)
    vectors = (proj_bias, ln1_gain, ln1_bias, down_bias, ln2_gain, ln2_bias)
    packed = jnp.concatenate([jnp.pad(vector, (0, PACK - D)) for vector in vectors] + [up_bias])
    bias, packed = lax.optimization_barrier((bias, packed))
    weights = (w_proj, w_up, w_down, packed)

    far = [project([part], w_key, w_value, value_bias) for part in parts[2:]]
    keys = [near[0], near[2]] + [pair[0] for pair in far]
    values = [near[1], near[3]] + [pair[1] for pair in far]
    mixed, lse = attn_fwd(query, bias, keys, values)
    mixed_partner = swap(mixed, "seq", low)
    own = after_attention(tok_rows, mixed, cotangent, weights, True)
    mixed_partner, own["d_attn"] = lax.optimization_barrier((mixed_partner, own["d_attn"]))
    other = after_attention(parts[low], mixed_partner, cotangent_partner, weights, False)
    down_terms = half_share_grads(
        place,
        [(own["hidden"], own["d_branch"], other["hidden"], other["d_branch"])],
        n_seq,
        "grads_down",
    )
    up_terms = half_share_grads(
        place,
        [
            (own["normed_low"], own["d_pre"], other["normed_low"], other["d_pre"]),
            (mixed, own["d_attn"], mixed_partner, other["d_attn"]),
        ],
        n_seq,
        "grads_up_proj",
    )
    order = Order()
    low_masks = [1 << i for i in reversed(range(n_seq.bit_length() - 2))]
    seq_masks = [1] + [1 << i for i in reversed(range(1, n_seq.bit_length() - 1))]
    down = halves_first(order, *down_terms, low_masks)
    next(down)
    up = columns_first(order, *up_terms, low_masks)
    next(up)
    for _ in low_masks[:2]:
        next(up)
        ups = order.last
        next(down)
        order.mark(*order.last, *ups)
    (d_mixed,) = order.after(own["d_mixed"])
    d_query, d_key, d_value = attn_bwd(query, bias, keys, values, d_mixed, lse)
    *qkv_terms, small = full_share_grads(place, parts, d_query, d_key, d_value, own["sums"])
    qkv = both_first(order, *qkv_terms, seq_masks)
    next(qkv)
    next(up)
    next(down)
    d_key, d_value = order.after(d_key, d_value)
    token_parts = token_terms(d_key, d_value, w_key, w_value, small, n_seq)
    tail = token_chain(order, *token_parts, small, seq_masks)
    next(tail)
    next(qkv)

    square = (D // n_seq, D)
    chains = dict(D=down, U=up, C=qkv, T=tail)
    plans = dict(D=[(FF // n_seq, D)], U=[(D // n_seq, FF), square], C=[square] * 3)
    results = {}
    for name in STEPS:
        try:
            next(chains[name])
        except StopIteration as stop:
            if name == "T":
                total, small = stop.value
                results[name] = [own["d_resid1"] + 0.125 * dot(d_query, w_query, NT) + total]
            else:
                results[name] = assemble(place, stop.value, plans[name], "assemble_" + name)
            order.mark(*order.last, results[name][0])
    (grad_down,), (grad_up, grad_proj) = results["D"], results["U"]
    grad_query, grad_key, grad_value = results["C"]
    (input_grad,) = results["T"]
    small = small.reshape(-1)
    up_end = 5 * D + FF
    return (
        own["layer_out"].reshape(1, T_DEV, D),
        input_grad.reshape(1, T_DEV, D),
        grad_query,
        grad_key,
        grad_value,
        grad_proj,
        grad_up,
        grad_down,
        small[0:D],
        small[D : 2 * D],
        small[2 * D : 3 * D],
        small[3 * D : 4 * D],
        small[4 * D : 5 * D],
        small[5 * D : up_end],
        small[up_end : up_end + D],
        small[up_end + D : up_end + 2 * D],
        small[up_end + 2 * D : up_end + 3 * D],
    )


def solution(mesh):
    tokens = P("dp", "seq", None)
    return jax.shard_map(
        on_device,
        mesh=mesh,
        in_specs=(tokens,) + (P(),) * 15 + (P("dp"), tokens, tokens),
        out_specs=(tokens, tokens) + (P("seq", None),) * 6 + (P(),) * 9,
        check_vma=False,
    )
```

```python
import jax
import jax.numpy as jnp
from jax import lax
from jax.experimental import pallas as pl
from jax.experimental.pallas import tpu as pltpu
from jax.sharding import PartitionSpec as P

D = 768
HEADS = 12
HEAD = 64
FF = 3072
BLOCK = 64
RAND = 3
SLOTS = 2
SLOT_TOK = 128
T_DEV = 256
PER_SLOT = SLOT_TOK // BLOCK
PER_DEV = T_DEV // BLOCK

LN_EPS = 1e-05
MASKED = -1e30
F32 = jnp.float32
BF16 = jnp.bfloat16
MIB = 2**20

NN = (((1,), (0,)), ((), ()))
NT = (((1,), (1,)), ((), ()))
TN = (((0,), (0,)), ((), ()))


VMEM_SPEC = pl.BlockSpec(memory_space=pltpu.VMEM)
SMEM_SPEC = pl.BlockSpec(memory_space=pltpu.SMEM)


def dot(left, right, dims=NN):
    return lax.dot_general(left, right, dims, preferred_element_type=F32)


def coords(device, within, is_long):
    slot = jnp.where(is_long, 0, within // PER_SLOT)
    position = jnp.where(
        is_long, device * PER_DEV + within, device * PER_SLOT + within % PER_SLOT
    )
    return slot, position


def bias_kernel(place_ref, long_ref, chosen_ref, bias_ref, *, n_seq):
    device = place_ref[0] * (n_seq // 2) + place_ref[1]
    is_long = long_ref[0] == 1
    last = jnp.where(is_long, n_seq * PER_DEV, n_seq * PER_DEV // SLOTS) - 1
    column = lax.broadcasted_iota(jnp.int32, (1, n_seq * T_DEV), 1)
    key_slot, key_pos = coords(
        (column // T_DEV) ^ device, column % T_DEV // BLOCK, is_long
    )
    ends = (key_pos == 0) | (key_pos == last)
    for block in range(PER_DEV):
        slot, position = coords(device, block, is_long)
        keep = ends | (jnp.abs(key_pos - position) <= 1)
        for draw in range(RAND):
            keep = keep | (key_pos == chosen_ref[0, block, draw])
        keep = keep | (position == 0) | (position == last)
        keep = keep & (key_slot == slot)
        bias_ref[block : block + 1, :] = jnp.where(keep, 0.0, MASKED)


def block_bias(place, long_group, random_blocks, n_seq):
    return pl.pallas_call(
        lambda *refs: bias_kernel(*refs, n_seq=n_seq),
        in_specs=[SMEM_SPEC] * 3,
        out_specs=VMEM_SPEC,
        out_shape=jax.ShapeDtypeStruct((PER_DEV, n_seq * T_DEV), F32),
        compiler_params=pltpu.CompilerParams(vmem_limit_bytes=4 * MIB),
        cost_estimate=cost(1),
        name="block_bias",
    )(place, long_group, random_blocks)


def project_kernel(wk_ref, wv_ref, v_bias_ref, *refs, count, with_query):
    parts, refs = refs[:count], refs[count:]
    if with_query:
        wq_ref, q_bias_ref, q_ref, *refs = refs
        query = dot(parts[0][...], wq_ref[...]) + q_bias_ref[...].astype(F32)[None, :]
        q_ref[...] = (query * 0.125).astype(BF16)
    v_bias = v_bias_ref[...].astype(F32)[None, :]
    for index, part in enumerate(parts):
        refs[2 * index][...] = dot(part[...], wk_ref[...]).astype(BF16)
        refs[2 * index + 1][...] = (dot(part[...], wv_ref[...]) + v_bias).astype(BF16)


def project(parts, w_key, w_value, value_bias, *query):
    count = 2 * len(parts) + (1 if query else 0)
    return pl.pallas_call(
        lambda *refs: project_kernel(*refs, count=len(parts), with_query=bool(query)),
        in_specs=[VMEM_SPEC] * (3 + len(parts) + len(query)),
        out_specs=[VMEM_SPEC] * count,
        out_shape=[jax.ShapeDtypeStruct((T_DEV, D), BF16)] * count,
        compiler_params=pltpu.CompilerParams(vmem_limit_bytes=16 * MIB),
        cost_estimate=cost(1),
        name="project_near" if query else "project_far",
    )(w_key, w_value, value_bias, *parts, *query)


def joined(refs):
    return jnp.concatenate([ref[...] for ref in refs])


def attn_fwd_kernel(q_ref, bias_ref, *refs, parts):
    k_refs, v_refs, (mixed_ref, lse_ref) = refs[:parts], refs[parts : 2 * parts], refs[2 * parts :]
    query, key, value, bias = q_ref[...], joined(k_refs), joined(v_refs), bias_ref[...]
    rows, keys = query.shape[0], key.shape[0]
    first = lax.broadcasted_iota(jnp.int32, (rows, 2 * HEAD), 1) < HEAD
    outs, lses = [], []
    for head in range(2):
        own = jnp.where(first == (head == 0), query, jnp.zeros_like(query))
        scores = dot(own, key, NT).reshape(PER_DEV, BLOCK, keys) + bias[:, None, :]
        scores = scores.reshape(rows, keys)
        peak = jnp.max(scores, axis=1, keepdims=True)
        weight = jnp.exp(scores - peak)
        total = jnp.sum(weight, axis=1, keepdims=True)
        outs.append(dot(weight.astype(BF16), value) * (1.0 / total))
        lses.append(peak + jnp.log(total))
    mixed_ref[...] = jnp.where(first, outs[0], outs[1]).astype(BF16)
    lse_ref[...] = jnp.where(first, lses[0], lses[1])


def attn_bwd_kernel(q_ref, bias_ref, g_ref, lse_ref, *refs, parts):
    k_refs, v_refs, (dq_ref, dk_ref, dv_ref) = (
        refs[:parts],
        refs[parts : 2 * parts],
        refs[2 * parts :],
    )
    query, key, value, bias, grad = (
        q_ref[...],
        joined(k_refs),
        joined(v_refs),
        bias_ref[...],
        g_ref[...],
    )
    rows, keys = query.shape[0], key.shape[0]
    first = lax.broadcasted_iota(jnp.int32, (rows, 2 * HEAD), 1) < HEAD
    d_query, d_key, d_value = [], None, None
    for head in range(2):
        mine = first == (head == 0)
        own = jnp.where(mine, query, jnp.zeros_like(query))
        own_grad = jnp.where(mine, grad, jnp.zeros_like(grad))
        scores = dot(own, key, NT).reshape(PER_DEV, BLOCK, keys) + bias[:, None, :]
        probs = jnp.exp(scores.reshape(rows, keys) - lse_ref[:, HEAD * head : HEAD * head + 1])
        d_probs = dot(own_grad, value, NT)
        delta = jnp.sum(probs * d_probs, axis=1, keepdims=True)
        d_scores = (probs * (d_probs - delta)).astype(BF16)
        d_query.append(dot(d_scores, key))
        key_term = dot(d_scores, own, TN)
        value_term = dot(probs.astype(BF16), own_grad, TN)
        d_key = key_term if d_key is None else d_key + key_term
        d_value = value_term if d_value is None else d_value + value_term
    dq_ref[...] = jnp.where(first, d_query[0], d_query[1]).astype(BF16)
    dk_ref[...] = d_key.astype(BF16)
    dv_ref[...] = d_value.astype(BF16)


def cost(microseconds):
    return pl.CostEstimate(flops=int(microseconds * 1.1e9), bytes_accessed=0, transcendentals=0)


def head_pair(rows):
    return pl.BlockSpec((rows, 2 * HEAD), lambda i: (0, i))


def whole(shape):
    return pl.BlockSpec(shape, lambda *_: (0,) * len(shape))


def attn_fwd(query, bias, keys, values):
    rows = query.shape[0]
    return pl.pallas_call(
        lambda *refs: attn_fwd_kernel(*refs, parts=len(keys)),
        grid=(HEADS // 2,),
        in_specs=[head_pair(rows), whole(bias.shape)] + [head_pair(rows)] * (2 * len(keys)),
        out_specs=[head_pair(rows), head_pair(rows)],
        out_shape=[
            jax.ShapeDtypeStruct((rows, D), BF16),
            jax.ShapeDtypeStruct((rows, D), F32),
        ],
        compiler_params=pltpu.CompilerParams(vmem_limit_bytes=16 * MIB),
        cost_estimate=cost(10),
        name="attn_fwd",
    )(query, bias, *keys, *values)


def attn_bwd(query, bias, keys, values, grad, lse):
    rows = query.shape[0]
    count = rows * len(keys)
    return pl.pallas_call(
        lambda *refs: attn_bwd_kernel(*refs, parts=len(keys)),
        grid=(HEADS // 2,),
        in_specs=[head_pair(rows), whole(bias.shape), head_pair(rows), head_pair(rows)]
        + [head_pair(rows)] * (2 * len(keys)),
        out_specs=[head_pair(rows), head_pair(count), head_pair(count)],
        out_shape=[
            jax.ShapeDtypeStruct((rows, D), BF16),
            jax.ShapeDtypeStruct((count, D), BF16),
            jax.ShapeDtypeStruct((count, D), BF16),
        ],
        compiler_params=pltpu.CompilerParams(vmem_limit_bytes=24 * MIB),
        cost_estimate=cost(0.01),
        name="attn_bwd",
    )(query, bias, grad, lse, *keys, *values)


LANES = 384
QUARTERS = 4


def slot_of(quarter):
    return 2 * (quarter % 2) + quarter // 2


def half_share_kernel(place_ref, *refs, plan, low):
    keep_ref, send_ref, stage, turned = refs[4 * len(plan) :]
    top, low_own, x_own, z_own = (place_ref[i] for i in range(4))
    offset = 0
    for index, (rows, cols) in enumerate(plan):
        sides = (refs[4 * index : 4 * index + 2], refs[4 * index + 2 : 4 * index + 4])
        half = rows // 2
        share = half // low
        strip = min(half, LANES)
        piece_rows = share // QUARTERS
        for start in range(0, half, strip):
            lanes = pl.ds(pl.multiple_of(top * half + start, 128), strip)
            for side, (left, _) in enumerate(sides):
                turned[0:strip, side * T_DEV : (side + 1) * T_DEV] = left[:, lanes].T
            for block in range(cols // D):
                grad = sum(
                    dot(
                        turned[0:strip, side * T_DEV : (side + 1) * T_DEV],
                        right[:, block * D : (block + 1) * D],
                    )
                    for side, (_, right) in enumerate(sides)
                )
                for part in range(D // LANES):
                    column = block * D + part * LANES
                    side_x = column // (cols // 2)
                    slot = offset + (column % (cols // 2)) // LANES * piece_rows
                    for row in range(0, strip, piece_rows):
                        at = start + row
                        low_other = at // share
                        quarter = at % share // piece_rows
                        stage[
                            low_other ^ low_own,
                            side_x ^ x_own,
                            slot_of(quarter ^ z_own),
                            slot : slot + piece_rows,
                            :,
                        ] = grad[
                            row : row + piece_rows, part * LANES : (part + 1) * LANES
                        ].astype(BF16)
        offset += piece_rows * (cols // 2 // LANES)
    keep_ref[...] = stage[0 : low // 2]
    send_ref[...] = stage[low // 2 : low]


def half_share_grads(place, weights, n_seq, name):
    low = n_seq // 2
    plan = [(w[0].shape[1], w[1].shape[1]) for w in weights]
    piece_rows = sum(r // n_seq // QUARTERS * (c // 2 // LANES) for r, c in plan)
    shape = (2, QUARTERS, piece_rows, LANES)
    return pl.pallas_call(
        lambda *refs: half_share_kernel(*refs, plan=plan, low=low),
        in_specs=[SMEM_SPEC] + [VMEM_SPEC] * (4 * len(weights)),
        out_specs=[VMEM_SPEC] * 2,
        out_shape=[jax.ShapeDtypeStruct((low // 2, *shape), BF16)] * 2,
        scratch_shapes=[pltpu.VMEM((low, *shape), BF16), pltpu.VMEM((LANES, 2 * T_DEV), BF16)],
        compiler_params=pltpu.CompilerParams(vmem_limit_bytes=20 * MIB),
        cost_estimate=cost(0.01),
        name=name,
    )(place, *[array for weight in weights for array in weight])


def full_share_kernel(place_ref, dq_ref, dk_ref, dv_ref, sums_ref, *refs, n_seq):
    tokens, (keep_ref, send_ref, small_ref, stage, turned) = refs[:n_seq], refs[n_seq:]
    small_ref[2:, :] = sums_ref[2:, :]
    small_ref[0:1, :] = jnp.sum(dq_ref[...].astype(F32), axis=0, keepdims=True) * 0.125
    small_ref[1:2, :] = jnp.sum(dv_ref[...].astype(F32), axis=0, keepdims=True)
    top, low_own, x_own, z_own = (place_ref[i] for i in range(4))
    seq_own = top * (n_seq // 2) + low_own
    share = D // n_seq
    piece_rows = share // QUARTERS
    for start in range(0, D, LANES):
        for index, part in enumerate(tokens):
            turned[:, index * T_DEV : (index + 1) * T_DEV] = part[:, start : start + LANES].T
        for index, right in enumerate((dq_ref, dk_ref, dv_ref)):
            if index == 0:
                grad = dot(turned[:, 0:T_DEV], right[...]) * 0.125
            else:
                grad = dot(turned[...], right[...])
            for part in range(D // LANES):
                for row in range(0, LANES, piece_rows):
                    at = start + row
                    relative = (at // share) ^ seq_own
                    stage[
                        relative % 2 * (n_seq // 2) + relative // 2,
                        part ^ x_own,
                        slot_of((at % share // piece_rows) ^ z_own),
                        index * piece_rows : (index + 1) * piece_rows,
                        :,
                    ] = grad[row : row + piece_rows, part * LANES : (part + 1) * LANES].astype(BF16)
    keep_ref[...] = stage[0 : n_seq // 2]
    send_ref[...] = stage[n_seq // 2 : n_seq]


def full_share_grads(place, tokens, d_query, d_key, d_value, sums):
    n_seq = len(tokens)
    piece_rows = 3 * (D // n_seq // QUARTERS)
    shape = (2, QUARTERS, piece_rows, LANES)
    return pl.pallas_call(
        lambda *refs: full_share_kernel(*refs, n_seq=n_seq),
        in_specs=[SMEM_SPEC] + [VMEM_SPEC] * (4 + n_seq),
        out_specs=[VMEM_SPEC] * 3,
        out_shape=[jax.ShapeDtypeStruct((n_seq // 2, *shape), BF16)] * 2
        + [jax.ShapeDtypeStruct(sums.shape, F32)],
        scratch_shapes=[
            pltpu.VMEM((n_seq, *shape), BF16),
            pltpu.VMEM((LANES, n_seq * T_DEV), BF16),
        ],
        compiler_params=pltpu.CompilerParams(vmem_limit_bytes=20 * MIB),
        cost_estimate=cost(0.01),
        name="grads_qkv",
    )(place, d_query, d_key, d_value, sums, *tokens)


def assemble_kernel(place_ref, *refs, plan, places):
    pieces, outs = refs[: len(places)], refs[len(places) :]
    x_own, z_own = place_ref[2], place_ref[3]
    for ref, indices in zip(pieces, places):
        for at, index in enumerate(indices):
            quarter = slot_of(index % QUARTERS) ^ z_own
            column = (index // QUARTERS) ^ x_own
            offset = 0
            for out, (rows, cols) in zip(outs, plan):
                height = rows // QUARTERS
                row = pl.ds(pl.multiple_of(quarter * height, 8), height)
                for part in range(cols // 2 // LANES):
                    start = pl.multiple_of(column * (cols // 2) + part * LANES, 128)
                    out[row, pl.ds(start, LANES)] = ref[at, offset : offset + height, :].astype(F32)
                    offset += height


def assemble(place, pieces, plan, name):
    places = [indices for _, indices in pieces]
    return pl.pallas_call(
        lambda *refs: assemble_kernel(*refs, plan=plan, places=places),
        in_specs=[SMEM_SPEC] + [VMEM_SPEC] * len(pieces),
        out_specs=[VMEM_SPEC] * len(plan),
        out_shape=[jax.ShapeDtypeStruct(shape, F32) for shape in plan],
        compiler_params=pltpu.CompilerParams(vmem_limit_bytes=12 * MIB),
        cost_estimate=cost(0.01),
        name=name,
    )(place, *[array for array, _ in pieces])


def swap(value, axis, mask):
    size = lax.axis_size(axis)
    return lax.ppermute(value, axis, [(i, i ^ mask) for i in range(size)])


def summed(terms):
    total = terms[0].astype(F32)
    for term in terms[1:]:
        total = total + term.astype(F32)
    return total.astype(BF16)


STEPS = "TUCDUCDTCUTCDTCUDCUTDC"


class Order:
    def __init__(self):
        self.last = ()

    def after(self, *arrays):
        return lax.optimization_barrier((*arrays, *self.last))[: len(arrays)]

    def mark(self, *arrays):
        self.last = arrays


def exchange(order, sends, swaps):
    order.mark(*sends)
    return [swap(send, axis, mask) for send, (axis, mask) in zip(sends, swaps)]


def sum_seq(order, keep, send, seq_masks):
    got = exchange(order, [send], [("seq", seq_masks[0])])
    yield
    terms = [keep, *order.after(*got)]
    for step, mask in enumerate(seq_masks[1:]):
        half = terms[0].shape[0] // 2
        got = exchange(order, [summed([t[half:] for t in terms])], [("seq", mask)])
        if step == 0:
            yield
        terms = [t[:half] for t in terms] + list(order.after(*got))
    return [t[0] for t in terms]


def sum_dp_rest(order, piece):
    step = 2 * QUARTERS
    while step < lax.axis_size("dp"):
        got = exchange(order, [piece], [("dp", step)])
        piece = summed([piece, *order.after(*got)])
        step *= 2
    return piece


def gather_dp(order, piece, mode):
    if mode == "xzz":
        far = exchange(order, [piece], [("dp", 1)])
        yield
        both = jnp.concatenate([piece, *order.after(*far)])
        got = exchange(order, [both], [("dp", 4)])
        yield
        four = jnp.concatenate([both, *order.after(*got)])
        got = exchange(order, [four], [("dp", 2)])
        yield
        return [(four, (0, 4, 1, 5)), (*order.after(*got), (2, 6, 3, 7))]
    got = exchange(order, [piece], [("dp", 4)])
    yield
    first = jnp.concatenate([piece, *order.after(*got)])
    if mode == "zxz":
        far = exchange(order, [first], [("dp", 1)])
        yield
        four = jnp.concatenate([first, *order.after(*far)])
        got = exchange(order, [four], [("dp", 2)])
        yield
        return [(four, (0, 1, 4, 5)), (*order.after(*got), (2, 3, 6, 7))]
    if mode == "zzx split":
        got = exchange(order, [first, first], [("dp", 2), ("dp", 1)])
        yield
        second, far_first = order.after(*got)
        got = exchange(order, [second], [("dp", 1)])
        yield
        return [
            (first, (0, 1)),
            (second, (2, 3)),
            (far_first, (4, 5)),
            (*order.after(*got), (6, 7)),
        ]
    got = exchange(order, [first], [("dp", 2)])
    yield
    own = jnp.concatenate([first, *order.after(*got)])
    got = exchange(order, [own], [("dp", 1)])
    yield
    return [(own, (0, 1, 2, 3)), (*order.after(*got), (4, 5, 6, 7))]


def columns_first(order, keep, send, seq_masks):
    terms = yield from sum_seq(order, keep, send, seq_masks)
    got = exchange(order, [summed([t[1] for t in terms])], [("dp", 1)])
    yield
    terms = [t[0] for t in terms] + list(order.after(*got))
    for mask in (2, 4):
        half = terms[0].shape[0] // 2
        got = exchange(order, [summed([t[half:] for t in terms])], [("dp", mask)])
        yield
        terms = [t[:half] for t in terms] + list(order.after(*got))
    piece = sum_dp_rest(order, summed(terms))
    return (yield from gather_dp(order, piece, "zzx split"))


def both_first(order, keep, send, seq_masks):
    got = exchange(order, [send], [("seq", seq_masks[0])])
    yield
    terms = [keep, *order.after(*got)]
    for mask in seq_masks[1:-1]:
        count = terms[0].shape[0] // 2
        got = exchange(order, [summed([t[count:] for t in terms])], [("seq", mask)])
        terms = [t[:count] for t in terms] + list(order.after(*got))
    along_seq, along_dp = ("seq", seq_masks[-1]), ("dp", 1)
    half = QUARTERS // 2
    low, high = [t[:, :, :half] for t in terms], [t[:, :, half:] for t in terms]
    got = exchange(
        order,
        [summed([t[1] for t in low]), summed([t[:, 1] for t in high])],
        [along_seq, along_dp],
    )
    yield
    low_got, high_got = order.after(*got)
    low = [t[0] for t in low] + [low_got]
    high = [t[:, 0] for t in high] + [high_got]
    got = exchange(
        order,
        [summed([t[1] for t in low]), summed([t[1] for t in high])],
        [along_dp, along_seq],
    )
    yield
    low_got, high_got = order.after(*got)
    low = [t[0] for t in low] + [low_got]
    high = [t[0] for t in high] + [high_got]
    got = exchange(order, [summed(high)], [("dp", 2)])
    yield
    terms = low + list(order.after(*got))
    got = exchange(order, [summed([t[1:] for t in terms])], [("dp", 4)])
    yield
    terms = [t[:1] for t in terms] + list(order.after(*got))
    piece = sum_dp_rest(order, summed(terms))
    return (yield from gather_dp(order, piece, "zzx"))


def halves_first(order, keep, send, seq_masks):
    terms = yield from sum_seq(order, keep, send, seq_masks)
    half = QUARTERS // 2
    got = exchange(order, [summed([t[:, half:] for t in terms])], [("dp", 2)])
    yield
    terms = [t[:, :half] for t in terms] + list(order.after(*got))
    got = exchange(order, [summed([t[1] for t in terms])], [("dp", 1)])
    yield
    terms = [t[0] for t in terms] + list(order.after(*got))
    got = exchange(order, [summed([t[1:] for t in terms])], [("dp", 4)])
    yield
    piece = summed([t[:1] for t in terms] + list(order.after(*got)))
    piece = sum_dp_rest(order, piece)
    return (yield from gather_dp(order, piece, "zxz"))


def token_kernel(dk_ref, dv_ref, wk_ref, wv_ref, small_ref, keep_ref, send_ref, *, n_seq):
    for part in range(n_seq):
        rows = slice(part * T_DEV, (part + 1) * T_DEV)
        term = dot(dk_ref[rows, :], wk_ref[...], NT) + dot(dv_ref[rows, :], wv_ref[...], NT)
        out = send_ref if part % 2 else keep_ref
        out[part // 2 * T_DEV : (part // 2 + 1) * T_DEV, :] = term.astype(BF16)
    small = small_ref[...]
    high = small.astype(BF16)
    at = n_seq // 2 * T_DEV
    send_ref[at : at + SMALL_ROWS, :] = high
    send_ref[at + SMALL_ROWS : at + 2 * SMALL_ROWS, :] = (small - high.astype(F32)).astype(BF16)


def token_terms(d_key, d_value, w_key, w_value, small, n_seq):
    rows = n_seq // 2 * T_DEV
    return pl.pallas_call(
        lambda *refs: token_kernel(*refs, n_seq=n_seq),
        in_specs=[VMEM_SPEC] * 5,
        out_specs=[VMEM_SPEC] * 2,
        out_shape=[
            jax.ShapeDtypeStruct((rows, D), BF16),
            jax.ShapeDtypeStruct((rows + 2 * SMALL_ROWS, D), BF16),
        ],
        compiler_params=pltpu.CompilerParams(vmem_limit_bytes=20 * MIB),
        cost_estimate=cost(12),
        name="token_terms",
    )(d_key, d_value, w_key, w_value, small)


def token_chain(order, keep, send, small, masks):
    n_dp = lax.axis_size("dp")
    terms = [keep]
    for step, mask in enumerate(masks):
        half = terms[0].shape[0] // 2
        high = small.astype(BF16)
        rest = (small - high.astype(F32)).astype(BF16)
        if step:
            send = jnp.concatenate([summed([t[half:] for t in terms]), high, rest])
            terms = [t[:half] for t in terms]
        got = exchange(order, [send], [("seq", mask)])
        if step < 2:
            yield
        (got,) = order.after(*got)
        at = terms[0].shape[0]
        small = high.astype(F32) + rest.astype(F32)
        small = small + got[at : at + SMALL_ROWS].astype(F32) + got[at + SMALL_ROWS :].astype(F32)
        terms = terms + [got[:at]]
    total = sum(t.astype(F32) for t in terms)
    step = 1
    while step < n_dp:
        got = exchange(order, [small], [("dp", step)])
        if step < 2 * QUARTERS:
            yield
        small = small + order.after(*got)[0]
        step *= 2
    return total, small


VECTORS = ("proj_bias", "ln1_gain", "ln1_bias", "down_bias", "ln2_gain", "ln2_bias")
FF_CHUNK = 768
PACK = 1024
SMALL_ROWS = 16
GELU_SCALE = 0.7978845608028654
GELU_CUBE = 0.044715


def rows_mean(array):
    return jnp.mean(array, axis=1, keepdims=True)


def rows_sum(array):
    return jnp.sum(array, axis=0, keepdims=True)


def norm_back(grad, xhat, inv, gain):
    scaled = grad * gain
    return inv * (scaled - rows_mean(scaled) - xhat * rows_mean(scaled * xhat))


def layer_kernel(
    x_ref, mixed_ref, grad_ref, proj_ref, up_ref, down_ref, packed_ref, *refs, own
):
    slope = refs[-1]
    normed_ref, hidden_ref, d_branch_ref, d_pre_ref, d_attn_ref = refs[:5]
    chunks = [slice(start, start + FF_CHUNK) for start in range(0, FF, FF_CHUNK)]
    packed = [packed_ref[i * PACK : (i + 1) * PACK].astype(F32)[None, :] for i in range(9)]
    vec = {name: row[:, :D] for name, row in zip(VECTORS, packed)}
    up_bias = jnp.concatenate(packed[len(VECTORS) :], axis=1)
    resid = x_ref[...].astype(F32) + dot(mixed_ref[...], proj_ref[...]) + vec["proj_bias"]
    center = resid - rows_mean(resid)
    inv1 = lax.rsqrt(rows_mean(center * center) + LN_EPS)
    xhat1 = center * inv1
    normed = xhat1 * vec["ln1_gain"] + vec["ln1_bias"]
    normed_low = normed.astype(BF16)
    normed_ref[...] = normed_low
    branch = jnp.zeros_like(normed)
    for cols in chunks:
        pre = dot(normed_low, up_ref[:, cols]) + up_bias[:, cols]
        square = pre * pre
        bent = jnp.tanh(pre * (GELU_SCALE + GELU_SCALE * GELU_CUBE * square))
        half = 0.5 + 0.5 * bent
        slope[:, cols] = half + (0.5 * pre) * (1.0 - bent * bent) * (
            GELU_SCALE + 3.0 * GELU_SCALE * GELU_CUBE * square
        )
        hidden = (pre * half).astype(BF16)
        hidden_ref[:, cols] = hidden
        branch = branch + dot(hidden, down_ref[cols, :])
    resid = normed + (branch + vec["down_bias"])
    center = resid - rows_mean(resid)
    inv2 = lax.rsqrt(rows_mean(center * center) + LN_EPS)
    xhat2 = center * inv2
    grad = grad_ref[...].astype(F32)
    d_resid2 = norm_back(grad, xhat2, inv2, vec["ln2_gain"])
    d_branch = d_resid2.astype(BF16)
    d_branch_ref[...] = d_branch
    d_normed = d_resid2
    for index, cols in enumerate(chunks):
        d_hidden = dot(d_branch, down_ref[cols, :], NT).astype(BF16).astype(F32)
        d_pre = (d_hidden * slope[:, cols]).astype(BF16)
        d_pre_ref[:, cols] = d_pre
        if own:
            refs[7][5 + index : 6 + index, :] = rows_sum(d_pre.astype(F32))
        d_normed = d_normed + dot(d_pre, up_ref[:, cols], NT)
    d_resid1 = norm_back(d_normed, xhat1, inv1, vec["ln1_gain"])
    d_attn = d_resid1.astype(BF16)
    d_attn_ref[...] = d_attn
    if own:
        out_ref, resid_ref, sums_ref, d_mixed_ref = refs[5:9]
        out_ref[...] = (xhat2 * vec["ln2_gain"] + vec["ln2_bias"]).astype(BF16)
        resid_ref[...] = d_resid1
        sums_ref[0:2, :] = jnp.zeros((2, D), F32)
        sums_ref[2:3, :] = rows_sum(d_attn.astype(F32))
        sums_ref[3:4, :] = rows_sum(d_normed * xhat1)
        sums_ref[4:5, :] = rows_sum(d_normed)
        sums_ref[9:10, :] = rows_sum(d_branch.astype(F32))
        sums_ref[10:11, :] = rows_sum(grad * xhat2)
        sums_ref[11:12, :] = rows_sum(grad)
        sums_ref[12:, :] = jnp.zeros((SMALL_ROWS - 12, D), F32)
        d_mixed_ref[...] = dot(d_attn, proj_ref[...], NT).astype(BF16)


def after_attention(tokens, mixed, out_grad, weights, own):
    wide, tall = jax.ShapeDtypeStruct((T_DEV, FF), BF16), jax.ShapeDtypeStruct((T_DEV, D), BF16)
    names = ["normed_low", "hidden", "d_branch", "d_pre", "d_attn"]
    shapes = [tall, wide, tall, wide, tall]
    if own:
        names += ["layer_out", "d_resid1", "sums", "d_mixed"]
        shapes += [
            tall,
            jax.ShapeDtypeStruct((T_DEV, D), F32),
            jax.ShapeDtypeStruct((SMALL_ROWS, D), F32),
            tall,
        ]
    outs = pl.pallas_call(
        lambda *refs: layer_kernel(*refs, own=own),
        in_specs=[VMEM_SPEC] * (3 + len(weights)),
        out_specs=[VMEM_SPEC] * len(shapes),
        out_shape=shapes,
        scratch_shapes=[pltpu.VMEM((T_DEV, FF), F32)],
        compiler_params=pltpu.CompilerParams(vmem_limit_bytes=20 * MIB),
        cost_estimate=cost(9),
        name="layer_own" if own else "layer_other",
    )(tokens, mixed, out_grad, *weights)
    return dict(zip(names, outs))


def on_device(
    inputs,
    w_query,
    query_bias,
    w_key,
    w_value,
    value_bias,
    w_proj,
    proj_bias,
    ln1_gain,
    ln1_bias,
    w_up,
    up_bias,
    w_down,
    down_bias,
    ln2_gain,
    ln2_bias,
    long_group,
    random_blocks,
    out_grad,
):
    n_seq, n_dp = lax.axis_size("seq"), lax.axis_size("dp")
    device, dp = lax.axis_index("seq"), lax.axis_index("dp")
    low = n_seq // 2
    low_bits = low.bit_length() - 1
    place = jnp.stack(
        [device >> low_bits, device & (low - 1), dp & 1, (dp >> 1) & (QUARTERS - 1)]
    ).astype(jnp.int32)
    tok_rows = inputs.reshape(T_DEV, D)
    cotangent = out_grad.reshape(T_DEV, D)
    bias = block_bias(place, long_group, random_blocks, n_seq)
    parts = [tok_rows, swap(tok_rows, "seq", 1)] + [None] * (n_seq - 2)
    step = low
    while step > 1:
        for j in range(0, n_seq, 2 * step):
            parts[j + step] = swap(parts[j], "seq", step)
        step //= 2
    query, *near = project(parts[:2], w_key, w_value, value_bias, w_query, query_bias)
    *parts[2::2], bias, query = lax.optimization_barrier((*parts[2::2], bias, query))
    for j in range(2, n_seq, 2):
        parts[j + 1] = swap(parts[j], "seq", 1)
    cotangent_partner = swap(cotangent, "seq", low)
    vectors = (proj_bias, ln1_gain, ln1_bias, down_bias, ln2_gain, ln2_bias)
    packed = jnp.concatenate([jnp.pad(vector, (0, PACK - D)) for vector in vectors] + [up_bias])
    bias, packed = lax.optimization_barrier((bias, packed))
    weights = (w_proj, w_up, w_down, packed)

    far = [project([part], w_key, w_value, value_bias) for part in parts[2:]]
    keys = [near[0], near[2]] + [pair[0] for pair in far]
    values = [near[1], near[3]] + [pair[1] for pair in far]
    mixed, lse = attn_fwd(query, bias, keys, values)
    mixed_partner = swap(mixed, "seq", low)
    own = after_attention(tok_rows, mixed, cotangent, weights, True)
    mixed_partner, own["d_attn"] = lax.optimization_barrier((mixed_partner, own["d_attn"]))
    other = after_attention(parts[low], mixed_partner, cotangent_partner, weights, False)
    down_terms = half_share_grads(
        place,
        [(own["hidden"], own["d_branch"], other["hidden"], other["d_branch"])],
        n_seq,
        "grads_down",
    )
    up_terms = half_share_grads(
        place,
        [
            (own["normed_low"], own["d_pre"], other["normed_low"], other["d_pre"]),
            (mixed, own["d_attn"], mixed_partner, other["d_attn"]),
        ],
        n_seq,
        "grads_up_proj",
    )
    order = Order()
    low_masks = [1 << i for i in reversed(range(n_seq.bit_length() - 2))]
    seq_masks = [1] + [1 << i for i in reversed(range(1, n_seq.bit_length() - 1))]
    down = halves_first(order, *down_terms, low_masks)
    next(down)
    up = columns_first(order, *up_terms, low_masks)
    next(up)
    for _ in low_masks[:2]:
        next(up)
        ups = order.last
        next(down)
        order.mark(*order.last, *ups)
    (d_mixed,) = order.after(own["d_mixed"])
    d_query, d_key, d_value = attn_bwd(query, bias, keys, values, d_mixed, lse)
    *qkv_terms, small = full_share_grads(place, parts, d_query, d_key, d_value, own["sums"])
    qkv = both_first(order, *qkv_terms, seq_masks)
    next(qkv)
    next(up)
    next(down)
    d_key, d_value = order.after(d_key, d_value)
    token_parts = token_terms(d_key, d_value, w_key, w_value, small, n_seq)
    tail = token_chain(order, *token_parts, small, seq_masks)
    next(tail)
    next(qkv)

    square = (D // n_seq, D)
    chains = dict(D=down, U=up, C=qkv, T=tail)
    plans = dict(D=[(FF // n_seq, D)], U=[(D // n_seq, FF), square], C=[square] * 3)
    results = {}
    for name in STEPS:
        try:
            next(chains[name])
        except StopIteration as stop:
            if name == "T":
                total, small = stop.value
                results[name] = [own["d_resid1"] + 0.125 * dot(d_query, w_query, NT) + total]
            else:
                results[name] = assemble(place, stop.value, plans[name], "assemble_" + name)
            order.mark(*order.last, results[name][0])
    (grad_down,), (grad_up, grad_proj) = results["D"], results["U"]
    grad_query, grad_key, grad_value = results["C"]
    (input_grad,) = results["T"]
    small = small.reshape(-1)
    up_end = 5 * D + FF
    return (
        own["layer_out"].reshape(1, T_DEV, D),
        input_grad.reshape(1, T_DEV, D),
        grad_query,
        grad_key,
        grad_value,
        grad_proj,
        grad_up,
        grad_down,
        small[0:D],
        small[D : 2 * D],
        small[2 * D : 3 * D],
        small[3 * D : 4 * D],
        small[4 * D : 5 * D],
        small[5 * D : up_end],
        small[up_end : up_end + D],
        small[up_end + D : up_end + 2 * D],
        small[up_end + 2 * D : up_end + 3 * D],
    )


def solution(mesh):
    tokens = P("dp", "seq", None)
    return jax.shard_map(
        on_device,
        mesh=mesh,
        in_specs=(tokens,) + (P(),) * 15 + (P("dp"), tokens, tokens),
        out_specs=(tokens, tokens) + (P("seq", None),) * 6 + (P(),) * 9,
        check_vma=False,
    )
```

```python
import jax
import jax.numpy as jnp
from jax import lax
from jax.experimental import pallas as pl
from jax.experimental.pallas import tpu as pltpu
from jax.sharding import PartitionSpec as P

D = 768
HEADS = 12
HEAD = 64
FF = 3072
BLOCK = 64
RAND = 3
SLOTS = 2
SLOT_TOK = 128
T_DEV = 256
PER_SLOT = SLOT_TOK // BLOCK
PER_DEV = T_DEV // BLOCK

LN_EPS = 1e-05
MASKED = -1e30
F32 = jnp.float32
BF16 = jnp.bfloat16
MIB = 2**20

NN = (((1,), (0,)), ((), ()))
NT = (((1,), (1,)), ((), ()))
TN = (((0,), (0,)), ((), ()))


VMEM_SPEC = pl.BlockSpec(memory_space=pltpu.VMEM)
SMEM_SPEC = pl.BlockSpec(memory_space=pltpu.SMEM)


def dot(left, right, dims=NN):
    return lax.dot_general(left, right, dims, preferred_element_type=F32)


def coords(device, within, is_long):
    slot = jnp.where(is_long, 0, within // PER_SLOT)
    position = jnp.where(
        is_long, device * PER_DEV + within, device * PER_SLOT + within % PER_SLOT
    )
    return slot, position


def bias_kernel(place_ref, long_ref, chosen_ref, bias_ref, *, n_seq):
    device = place_ref[0] * (n_seq // 2) + place_ref[1]
    is_long = long_ref[0] == 1
    last = jnp.where(is_long, n_seq * PER_DEV, n_seq * PER_DEV // SLOTS) - 1
    column = lax.broadcasted_iota(jnp.int32, (1, n_seq * T_DEV), 1)
    key_slot, key_pos = coords(
        (column // T_DEV) ^ device, column % T_DEV // BLOCK, is_long
    )
    ends = (key_pos == 0) | (key_pos == last)
    for block in range(PER_DEV):
        slot, position = coords(device, block, is_long)
        keep = ends | (jnp.abs(key_pos - position) <= 1)
        for draw in range(RAND):
            keep = keep | (key_pos == chosen_ref[0, block, draw])
        keep = keep | (position == 0) | (position == last)
        keep = keep & (key_slot == slot)
        bias_ref[block : block + 1, :] = jnp.where(keep, 0.0, MASKED)


def block_bias(place, long_group, random_blocks, n_seq):
    return pl.pallas_call(
        lambda *refs: bias_kernel(*refs, n_seq=n_seq),
        in_specs=[SMEM_SPEC] * 3,
        out_specs=VMEM_SPEC,
        out_shape=jax.ShapeDtypeStruct((PER_DEV, n_seq * T_DEV), F32),
        compiler_params=pltpu.CompilerParams(vmem_limit_bytes=4 * MIB),
        cost_estimate=cost(1),
        name="block_bias",
    )(place, long_group, random_blocks)


def project_kernel(wk_ref, wv_ref, v_bias_ref, *refs, count, with_query):
    parts, refs = refs[:count], refs[count:]
    if with_query:
        wq_ref, q_bias_ref, q_ref, *refs = refs
        query = dot(parts[0][...], wq_ref[...]) + q_bias_ref[...].astype(F32)[None, :]
        q_ref[...] = (query * 0.125).astype(BF16)
    v_bias = v_bias_ref[...].astype(F32)[None, :]
    for index, part in enumerate(parts):
        refs[2 * index][...] = dot(part[...], wk_ref[...]).astype(BF16)
        refs[2 * index + 1][...] = (dot(part[...], wv_ref[...]) + v_bias).astype(BF16)


def project(parts, w_key, w_value, value_bias, *query):
    count = 2 * len(parts) + (1 if query else 0)
    return pl.pallas_call(
        lambda *refs: project_kernel(*refs, count=len(parts), with_query=bool(query)),
        in_specs=[VMEM_SPEC] * (3 + len(parts) + len(query)),
        out_specs=[VMEM_SPEC] * count,
        out_shape=[jax.ShapeDtypeStruct((T_DEV, D), BF16)] * count,
        compiler_params=pltpu.CompilerParams(vmem_limit_bytes=16 * MIB),
        cost_estimate=cost(1),
        name="project_near" if query else "project_far",
    )(w_key, w_value, value_bias, *parts, *query)


def joined(refs):
    return jnp.concatenate([ref[...] for ref in refs])


def attn_fwd_kernel(q_ref, bias_ref, *refs, parts):
    k_refs, v_refs, (mixed_ref, lse_ref) = refs[:parts], refs[parts : 2 * parts], refs[2 * parts :]
    query, key, value, bias = q_ref[...], joined(k_refs), joined(v_refs), bias_ref[...]
    rows, keys = query.shape[0], key.shape[0]
    first = lax.broadcasted_iota(jnp.int32, (rows, 2 * HEAD), 1) < HEAD
    outs, lses = [], []
    for head in range(2):
        own = jnp.where(first == (head == 0), query, jnp.zeros_like(query))
        scores = dot(own, key, NT).reshape(PER_DEV, BLOCK, keys) + bias[:, None, :]
        scores = scores.reshape(rows, keys)
        peak = jnp.max(scores, axis=1, keepdims=True)
        weight = jnp.exp(scores - peak)
        total = jnp.sum(weight, axis=1, keepdims=True)
        outs.append(dot(weight.astype(BF16), value) * (1.0 / total))
        lses.append(peak + jnp.log(total))
    mixed_ref[...] = jnp.where(first, outs[0], outs[1]).astype(BF16)
    lse_ref[...] = jnp.where(first, lses[0], lses[1])


def attn_bwd_kernel(q_ref, bias_ref, g_ref, lse_ref, *refs, parts):
    k_refs, v_refs, (dq_ref, dk_ref, dv_ref) = (
        refs[:parts],
        refs[parts : 2 * parts],
        refs[2 * parts :],
    )
    query, key, value, bias, grad = (
        q_ref[...],
        joined(k_refs),
        joined(v_refs),
        bias_ref[...],
        g_ref[...],
    )
    rows, keys = query.shape[0], key.shape[0]
    first = lax.broadcasted_iota(jnp.int32, (rows, 2 * HEAD), 1) < HEAD
    d_query, d_key, d_value = [], None, None
    for head in range(2):
        mine = first == (head == 0)
        own = jnp.where(mine, query, jnp.zeros_like(query))
        own_grad = jnp.where(mine, grad, jnp.zeros_like(grad))
        scores = dot(own, key, NT).reshape(PER_DEV, BLOCK, keys) + bias[:, None, :]
        probs = jnp.exp(scores.reshape(rows, keys) - lse_ref[:, HEAD * head : HEAD * head + 1])
        d_probs = dot(own_grad, value, NT)
        delta = jnp.sum(probs * d_probs, axis=1, keepdims=True)
        d_scores = (probs * (d_probs - delta)).astype(BF16)
        d_query.append(dot(d_scores, key))
        key_term = dot(d_scores, own, TN)
        value_term = dot(probs.astype(BF16), own_grad, TN)
        d_key = key_term if d_key is None else d_key + key_term
        d_value = value_term if d_value is None else d_value + value_term
    dq_ref[...] = jnp.where(first, d_query[0], d_query[1]).astype(BF16)
    dk_ref[...] = d_key.astype(BF16)
    dv_ref[...] = d_value.astype(BF16)


def cost(microseconds):
    return pl.CostEstimate(flops=int(microseconds * 1.1e9), bytes_accessed=0, transcendentals=0)


def head_pair(rows):
    return pl.BlockSpec((rows, 2 * HEAD), lambda i: (0, i))


def whole(shape):
    return pl.BlockSpec(shape, lambda *_: (0,) * len(shape))


def attn_fwd(query, bias, keys, values):
    rows = query.shape[0]
    return pl.pallas_call(
        lambda *refs: attn_fwd_kernel(*refs, parts=len(keys)),
        grid=(HEADS // 2,),
        in_specs=[head_pair(rows), whole(bias.shape)] + [head_pair(rows)] * (2 * len(keys)),
        out_specs=[head_pair(rows), head_pair(rows)],
        out_shape=[
            jax.ShapeDtypeStruct((rows, D), BF16),
            jax.ShapeDtypeStruct((rows, D), F32),
        ],
        compiler_params=pltpu.CompilerParams(vmem_limit_bytes=16 * MIB),
        cost_estimate=cost(10),
        name="attn_fwd",
    )(query, bias, *keys, *values)


def attn_bwd(query, bias, keys, values, grad, lse):
    rows = query.shape[0]
    count = rows * len(keys)
    return pl.pallas_call(
        lambda *refs: attn_bwd_kernel(*refs, parts=len(keys)),
        grid=(HEADS // 2,),
        in_specs=[head_pair(rows), whole(bias.shape), head_pair(rows), head_pair(rows)]
        + [head_pair(rows)] * (2 * len(keys)),
        out_specs=[head_pair(rows), head_pair(count), head_pair(count)],
        out_shape=[
            jax.ShapeDtypeStruct((rows, D), BF16),
            jax.ShapeDtypeStruct((count, D), BF16),
            jax.ShapeDtypeStruct((count, D), BF16),
        ],
        compiler_params=pltpu.CompilerParams(vmem_limit_bytes=24 * MIB),
        cost_estimate=cost(0.01),
        name="attn_bwd",
    )(query, bias, grad, lse, *keys, *values)


LANES = 384
QUARTERS = 4


def slot_of(quarter):
    return 2 * (quarter % 2) + quarter // 2


def half_share_kernel(place_ref, *refs, plan, low):
    keep_ref, send_ref, stage, turned = refs[4 * len(plan) :]
    top, low_own, x_own, z_own = (place_ref[i] for i in range(4))
    offset = 0
    for index, (rows, cols) in enumerate(plan):
        sides = (refs[4 * index : 4 * index + 2], refs[4 * index + 2 : 4 * index + 4])
        half = rows // 2
        share = half // low
        strip = min(half, LANES)
        piece_rows = share // QUARTERS
        for start in range(0, half, strip):
            lanes = pl.ds(pl.multiple_of(top * half + start, 128), strip)
            for side, (left, _) in enumerate(sides):
                turned[0:strip, side * T_DEV : (side + 1) * T_DEV] = left[:, lanes].T
            for block in range(cols // D):
                grad = sum(
                    dot(
                        turned[0:strip, side * T_DEV : (side + 1) * T_DEV],
                        right[:, block * D : (block + 1) * D],
                    )
                    for side, (_, right) in enumerate(sides)
                )
                for part in range(D // LANES):
                    column = block * D + part * LANES
                    side_x = column // (cols // 2)
                    slot = offset + (column % (cols // 2)) // LANES * piece_rows
                    for row in range(0, strip, piece_rows):
                        at = start + row
                        low_other = at // share
                        quarter = at % share // piece_rows
                        stage[
                            low_other ^ low_own,
                            side_x ^ x_own,
                            slot_of(quarter ^ z_own),
                            slot : slot + piece_rows,
                            :,
                        ] = grad[
                            row : row + piece_rows, part * LANES : (part + 1) * LANES
                        ].astype(BF16)
        offset += piece_rows * (cols // 2 // LANES)
    keep_ref[...] = stage[0 : low // 2]
    send_ref[...] = stage[low // 2 : low]


def half_share_grads(place, weights, n_seq, name):
    low = n_seq // 2
    plan = [(w[0].shape[1], w[1].shape[1]) for w in weights]
    piece_rows = sum(r // n_seq // QUARTERS * (c // 2 // LANES) for r, c in plan)
    shape = (2, QUARTERS, piece_rows, LANES)
    return pl.pallas_call(
        lambda *refs: half_share_kernel(*refs, plan=plan, low=low),
        in_specs=[SMEM_SPEC] + [VMEM_SPEC] * (4 * len(weights)),
        out_specs=[VMEM_SPEC] * 2,
        out_shape=[jax.ShapeDtypeStruct((low // 2, *shape), BF16)] * 2,
        scratch_shapes=[pltpu.VMEM((low, *shape), BF16), pltpu.VMEM((LANES, 2 * T_DEV), BF16)],
        compiler_params=pltpu.CompilerParams(vmem_limit_bytes=20 * MIB),
        cost_estimate=cost(0.01),
        name=name,
    )(place, *[array for weight in weights for array in weight])


def full_share_kernel(place_ref, dq_ref, dk_ref, dv_ref, sums_ref, *refs, n_seq):
    tokens, (keep_ref, send_ref, small_ref, stage, turned) = refs[:n_seq], refs[n_seq:]
    small_ref[2:, :] = sums_ref[2:, :]
    small_ref[0:1, :] = jnp.sum(dq_ref[...].astype(F32), axis=0, keepdims=True) * 0.125
    small_ref[1:2, :] = jnp.sum(dv_ref[...].astype(F32), axis=0, keepdims=True)
    top, low_own, x_own, z_own = (place_ref[i] for i in range(4))
    seq_own = top * (n_seq // 2) + low_own
    share = D // n_seq
    piece_rows = share // QUARTERS
    for start in range(0, D, LANES):
        for index, part in enumerate(tokens):
            turned[:, index * T_DEV : (index + 1) * T_DEV] = part[:, start : start + LANES].T
        for index, right in enumerate((dq_ref, dk_ref, dv_ref)):
            if index == 0:
                grad = dot(turned[:, 0:T_DEV], right[...]) * 0.125
            else:
                grad = dot(turned[...], right[...])
            for part in range(D // LANES):
                for row in range(0, LANES, piece_rows):
                    at = start + row
                    relative = (at // share) ^ seq_own
                    stage[
                        relative % 2 * (n_seq // 2) + relative // 2,
                        part ^ x_own,
                        slot_of((at % share // piece_rows) ^ z_own),
                        index * piece_rows : (index + 1) * piece_rows,
                        :,
                    ] = grad[row : row + piece_rows, part * LANES : (part + 1) * LANES].astype(BF16)
    keep_ref[...] = stage[0 : n_seq // 2]
    send_ref[...] = stage[n_seq // 2 : n_seq]


def full_share_grads(place, tokens, d_query, d_key, d_value, sums):
    n_seq = len(tokens)
    piece_rows = 3 * (D // n_seq // QUARTERS)
    shape = (2, QUARTERS, piece_rows, LANES)
    return pl.pallas_call(
        lambda *refs: full_share_kernel(*refs, n_seq=n_seq),
        in_specs=[SMEM_SPEC] + [VMEM_SPEC] * (4 + n_seq),
        out_specs=[VMEM_SPEC] * 3,
        out_shape=[jax.ShapeDtypeStruct((n_seq // 2, *shape), BF16)] * 2
        + [jax.ShapeDtypeStruct(sums.shape, F32)],
        scratch_shapes=[
            pltpu.VMEM((n_seq, *shape), BF16),
            pltpu.VMEM((LANES, n_seq * T_DEV), BF16),
        ],
        compiler_params=pltpu.CompilerParams(vmem_limit_bytes=20 * MIB),
        cost_estimate=cost(0.01),
        name="grads_qkv",
    )(place, d_query, d_key, d_value, sums, *tokens)


def assemble_kernel(place_ref, *refs, plan, places):
    pieces, outs = refs[: len(places)], refs[len(places) :]
    x_own, z_own = place_ref[2], place_ref[3]
    for ref, indices in zip(pieces, places):
        for at, index in enumerate(indices):
            quarter = slot_of(index % QUARTERS) ^ z_own
            column = (index // QUARTERS) ^ x_own
            offset = 0
            for out, (rows, cols) in zip(outs, plan):
                height = rows // QUARTERS
                row = pl.ds(pl.multiple_of(quarter * height, 8), height)
                for part in range(cols // 2 // LANES):
                    start = pl.multiple_of(column * (cols // 2) + part * LANES, 128)
                    out[row, pl.ds(start, LANES)] = ref[at, offset : offset + height, :].astype(F32)
                    offset += height


def assemble(place, pieces, plan, name):
    places = [indices for _, indices in pieces]
    return pl.pallas_call(
        lambda *refs: assemble_kernel(*refs, plan=plan, places=places),
        in_specs=[SMEM_SPEC] + [VMEM_SPEC] * len(pieces),
        out_specs=[VMEM_SPEC] * len(plan),
        out_shape=[jax.ShapeDtypeStruct(shape, F32) for shape in plan],
        compiler_params=pltpu.CompilerParams(vmem_limit_bytes=12 * MIB),
        cost_estimate=cost(0.01),
        name=name,
    )(place, *[array for array, _ in pieces])


def swap(value, axis, mask):
    size = lax.axis_size(axis)
    return lax.ppermute(value, axis, [(i, i ^ mask) for i in range(size)])


def summed(terms):
    total = terms[0].astype(F32)
    for term in terms[1:]:
        total = total + term.astype(F32)
    return total.astype(BF16)


STEPS = "TUCDUCDTCUTCDCUDTCUTDC"


class Order:
    def __init__(self):
        self.last = ()

    def after(self, *arrays):
        return lax.optimization_barrier((*arrays, *self.last))[: len(arrays)]

    def mark(self, *arrays):
        self.last = arrays


def exchange(order, sends, swaps):
    order.mark(*sends)
    return [swap(send, axis, mask) for send, (axis, mask) in zip(sends, swaps)]


def sum_seq(order, keep, send, seq_masks):
    got = exchange(order, [send], [("seq", seq_masks[0])])
    yield
    terms = [keep, *order.after(*got)]
    for step, mask in enumerate(seq_masks[1:]):
        half = terms[0].shape[0] // 2
        got = exchange(order, [summed([t[half:] for t in terms])], [("seq", mask)])
        if step == 0:
            yield
        terms = [t[:half] for t in terms] + list(order.after(*got))
    return [t[0] for t in terms]


def sum_dp_rest(order, piece):
    step = 2 * QUARTERS
    while step < lax.axis_size("dp"):
        got = exchange(order, [piece], [("dp", step)])
        piece = summed([piece, *order.after(*got)])
        step *= 2
    return piece


def gather_dp(order, piece, mode):
    if mode == "xzz":
        far = exchange(order, [piece], [("dp", 1)])
        yield
        both = jnp.concatenate([piece, *order.after(*far)])
        got = exchange(order, [both], [("dp", 4)])
        yield
        four = jnp.concatenate([both, *order.after(*got)])
        got = exchange(order, [four], [("dp", 2)])
        yield
        return [(four, (0, 4, 1, 5)), (*order.after(*got), (2, 6, 3, 7))]
    got = exchange(order, [piece], [("dp", 4)])
    yield
    first = jnp.concatenate([piece, *order.after(*got)])
    if mode == "zxz":
        far = exchange(order, [first], [("dp", 1)])
        yield
        four = jnp.concatenate([first, *order.after(*far)])
        got = exchange(order, [four], [("dp", 2)])
        yield
        return [(four, (0, 1, 4, 5)), (*order.after(*got), (2, 3, 6, 7))]
    if mode == "zzx split":
        got = exchange(order, [first, first], [("dp", 2), ("dp", 1)])
        yield
        second, far_first = order.after(*got)
        got = exchange(order, [second], [("dp", 1)])
        yield
        return [
            (first, (0, 1)),
            (second, (2, 3)),
            (far_first, (4, 5)),
            (*order.after(*got), (6, 7)),
        ]
    got = exchange(order, [first], [("dp", 2)])
    yield
    own = jnp.concatenate([first, *order.after(*got)])
    got = exchange(order, [own], [("dp", 1)])
    yield
    return [(own, (0, 1, 2, 3)), (*order.after(*got), (4, 5, 6, 7))]


def columns_first(order, keep, send, seq_masks):
    terms = yield from sum_seq(order, keep, send, seq_masks)
    got = exchange(order, [summed([t[1] for t in terms])], [("dp", 1)])
    yield
    terms = [t[0] for t in terms] + list(order.after(*got))
    for mask in (2, 4):
        half = terms[0].shape[0] // 2
        got = exchange(order, [summed([t[half:] for t in terms])], [("dp", mask)])
        yield
        terms = [t[:half] for t in terms] + list(order.after(*got))
    piece = sum_dp_rest(order, summed(terms))
    return (yield from gather_dp(order, piece, "zzx split"))


def both_first(order, keep, send, seq_masks):
    got = exchange(order, [send], [("seq", seq_masks[0])])
    yield
    terms = [keep, *order.after(*got)]
    for mask in seq_masks[1:-1]:
        count = terms[0].shape[0] // 2
        got = exchange(order, [summed([t[count:] for t in terms])], [("seq", mask)])
        terms = [t[:count] for t in terms] + list(order.after(*got))
    along_seq, along_dp = ("seq", seq_masks[-1]), ("dp", 1)
    half = QUARTERS // 2
    low, high = [t[:, :, :half] for t in terms], [t[:, :, half:] for t in terms]
    got = exchange(
        order,
        [summed([t[1] for t in low]), summed([t[:, 1] for t in high])],
        [along_seq, along_dp],
    )
    yield
    low_got, high_got = order.after(*got)
    low = [t[0] for t in low] + [low_got]
    high = [t[:, 0] for t in high] + [high_got]
    got = exchange(
        order,
        [summed([t[1] for t in low]), summed([t[1] for t in high])],
        [along_dp, along_seq],
    )
    yield
    low_got, high_got = order.after(*got)
    low = [t[0] for t in low] + [low_got]
    high = [t[0] for t in high] + [high_got]
    got = exchange(order, [summed(high)], [("dp", 2)])
    yield
    terms = low + list(order.after(*got))
    got = exchange(order, [summed([t[1:] for t in terms])], [("dp", 4)])
    yield
    terms = [t[:1] for t in terms] + list(order.after(*got))
    piece = sum_dp_rest(order, summed(terms))
    return (yield from gather_dp(order, piece, "zzx"))


def halves_first(order, keep, send, seq_masks):
    terms = yield from sum_seq(order, keep, send, seq_masks)
    half = QUARTERS // 2
    got = exchange(order, [summed([t[:, half:] for t in terms])], [("dp", 2)])
    yield
    terms = [t[:, :half] for t in terms] + list(order.after(*got))
    got = exchange(order, [summed([t[1] for t in terms])], [("dp", 1)])
    yield
    terms = [t[0] for t in terms] + list(order.after(*got))
    got = exchange(order, [summed([t[1:] for t in terms])], [("dp", 4)])
    yield
    piece = summed([t[:1] for t in terms] + list(order.after(*got)))
    piece = sum_dp_rest(order, piece)
    return (yield from gather_dp(order, piece, "zxz"))


def token_kernel(dk_ref, dv_ref, wk_ref, wv_ref, small_ref, keep_ref, send_ref, *, n_seq):
    for part in range(n_seq):
        rows = slice(part * T_DEV, (part + 1) * T_DEV)
        term = dot(dk_ref[rows, :], wk_ref[...], NT) + dot(dv_ref[rows, :], wv_ref[...], NT)
        out = send_ref if part % 2 else keep_ref
        out[part // 2 * T_DEV : (part // 2 + 1) * T_DEV, :] = term.astype(BF16)
    small = small_ref[...]
    high = small.astype(BF16)
    at = n_seq // 2 * T_DEV
    send_ref[at : at + SMALL_ROWS, :] = high
    send_ref[at + SMALL_ROWS : at + 2 * SMALL_ROWS, :] = (small - high.astype(F32)).astype(BF16)


def token_terms(d_key, d_value, w_key, w_value, small, n_seq):
    rows = n_seq // 2 * T_DEV
    return pl.pallas_call(
        lambda *refs: token_kernel(*refs, n_seq=n_seq),
        in_specs=[VMEM_SPEC] * 5,
        out_specs=[VMEM_SPEC] * 2,
        out_shape=[
            jax.ShapeDtypeStruct((rows, D), BF16),
            jax.ShapeDtypeStruct((rows + 2 * SMALL_ROWS, D), BF16),
        ],
        compiler_params=pltpu.CompilerParams(vmem_limit_bytes=20 * MIB),
        cost_estimate=cost(12),
        name="token_terms",
    )(d_key, d_value, w_key, w_value, small)


def token_chain(order, keep, send, small, masks):
    n_dp = lax.axis_size("dp")
    terms = [keep]
    for step, mask in enumerate(masks):
        half = terms[0].shape[0] // 2
        high = small.astype(BF16)
        rest = (small - high.astype(F32)).astype(BF16)
        if step:
            send = jnp.concatenate([summed([t[half:] for t in terms]), high, rest])
            terms = [t[:half] for t in terms]
        got = exchange(order, [send], [("seq", mask)])
        if step < 2:
            yield
        (got,) = order.after(*got)
        at = terms[0].shape[0]
        small = high.astype(F32) + rest.astype(F32)
        small = small + got[at : at + SMALL_ROWS].astype(F32) + got[at + SMALL_ROWS :].astype(F32)
        terms = terms + [got[:at]]
    total = sum(t.astype(F32) for t in terms)
    step = 1
    while step < n_dp:
        got = exchange(order, [small], [("dp", step)])
        if step < 2 * QUARTERS:
            yield
        small = small + order.after(*got)[0]
        step *= 2
    return total, small


VECTORS = ("proj_bias", "ln1_gain", "ln1_bias", "down_bias", "ln2_gain", "ln2_bias")
FF_CHUNK = 768
PACK = 1024
SMALL_ROWS = 16
GELU_SCALE = 0.7978845608028654
GELU_CUBE = 0.044715


def rows_mean(array):
    return jnp.mean(array, axis=1, keepdims=True)


def rows_sum(array):
    return jnp.sum(array, axis=0, keepdims=True)


def norm_back(grad, xhat, inv, gain):
    scaled = grad * gain
    return inv * (scaled - rows_mean(scaled) - xhat * rows_mean(scaled * xhat))


def layer_kernel(
    x_ref, mixed_ref, grad_ref, proj_ref, up_ref, down_ref, packed_ref, *refs, own
):
    slope = refs[-1]
    normed_ref, hidden_ref, d_branch_ref, d_pre_ref, d_attn_ref = refs[:5]
    chunks = [slice(start, start + FF_CHUNK) for start in range(0, FF, FF_CHUNK)]
    packed = [packed_ref[i * PACK : (i + 1) * PACK].astype(F32)[None, :] for i in range(9)]
    vec = {name: row[:, :D] for name, row in zip(VECTORS, packed)}
    up_bias = jnp.concatenate(packed[len(VECTORS) :], axis=1)
    resid = x_ref[...].astype(F32) + dot(mixed_ref[...], proj_ref[...]) + vec["proj_bias"]
    center = resid - rows_mean(resid)
    inv1 = lax.rsqrt(rows_mean(center * center) + LN_EPS)
    xhat1 = center * inv1
    normed = xhat1 * vec["ln1_gain"] + vec["ln1_bias"]
    normed_low = normed.astype(BF16)
    normed_ref[...] = normed_low
    branch = jnp.zeros_like(normed)
    for cols in chunks:
        pre = dot(normed_low, up_ref[:, cols]) + up_bias[:, cols]
        square = pre * pre
        bent = jnp.tanh(pre * (GELU_SCALE + GELU_SCALE * GELU_CUBE * square))
        half = 0.5 + 0.5 * bent
        slope[:, cols] = half + (0.5 * pre) * (1.0 - bent * bent) * (
            GELU_SCALE + 3.0 * GELU_SCALE * GELU_CUBE * square
        )
        hidden = (pre * half).astype(BF16)
        hidden_ref[:, cols] = hidden
        branch = branch + dot(hidden, down_ref[cols, :])
    resid = normed + (branch + vec["down_bias"])
    center = resid - rows_mean(resid)
    inv2 = lax.rsqrt(rows_mean(center * center) + LN_EPS)
    xhat2 = center * inv2
    grad = grad_ref[...].astype(F32)
    d_resid2 = norm_back(grad, xhat2, inv2, vec["ln2_gain"])
    d_branch = d_resid2.astype(BF16)
    d_branch_ref[...] = d_branch
    d_normed = d_resid2
    for index, cols in enumerate(chunks):
        d_hidden = dot(d_branch, down_ref[cols, :], NT).astype(BF16).astype(F32)
        d_pre = (d_hidden * slope[:, cols]).astype(BF16)
        d_pre_ref[:, cols] = d_pre
        if own:
            refs[7][5 + index : 6 + index, :] = rows_sum(d_pre.astype(F32))
        d_normed = d_normed + dot(d_pre, up_ref[:, cols], NT)
    d_resid1 = norm_back(d_normed, xhat1, inv1, vec["ln1_gain"])
    d_attn = d_resid1.astype(BF16)
    d_attn_ref[...] = d_attn
    if own:
        out_ref, resid_ref, sums_ref, d_mixed_ref = refs[5:9]
        out_ref[...] = (xhat2 * vec["ln2_gain"] + vec["ln2_bias"]).astype(BF16)
        resid_ref[...] = d_resid1
        sums_ref[0:2, :] = jnp.zeros((2, D), F32)
        sums_ref[2:3, :] = rows_sum(d_attn.astype(F32))
        sums_ref[3:4, :] = rows_sum(d_normed * xhat1)
        sums_ref[4:5, :] = rows_sum(d_normed)
        sums_ref[9:10, :] = rows_sum(d_branch.astype(F32))
        sums_ref[10:11, :] = rows_sum(grad * xhat2)
        sums_ref[11:12, :] = rows_sum(grad)
        sums_ref[12:, :] = jnp.zeros((SMALL_ROWS - 12, D), F32)
        d_mixed_ref[...] = dot(d_attn, proj_ref[...], NT).astype(BF16)


def after_attention(tokens, mixed, out_grad, weights, own):
    wide, tall = jax.ShapeDtypeStruct((T_DEV, FF), BF16), jax.ShapeDtypeStruct((T_DEV, D), BF16)
    names = ["normed_low", "hidden", "d_branch", "d_pre", "d_attn"]
    shapes = [tall, wide, tall, wide, tall]
    if own:
        names += ["layer_out", "d_resid1", "sums", "d_mixed"]
        shapes += [
            tall,
            jax.ShapeDtypeStruct((T_DEV, D), F32),
            jax.ShapeDtypeStruct((SMALL_ROWS, D), F32),
            tall,
        ]
    outs = pl.pallas_call(
        lambda *refs: layer_kernel(*refs, own=own),
        in_specs=[VMEM_SPEC] * (3 + len(weights)),
        out_specs=[VMEM_SPEC] * len(shapes),
        out_shape=shapes,
        scratch_shapes=[pltpu.VMEM((T_DEV, FF), F32)],
        compiler_params=pltpu.CompilerParams(vmem_limit_bytes=20 * MIB),
        cost_estimate=cost(9),
        name="layer_own" if own else "layer_other",
    )(tokens, mixed, out_grad, *weights)
    return dict(zip(names, outs))


def on_device(
    inputs,
    w_query,
    query_bias,
    w_key,
    w_value,
    value_bias,
    w_proj,
    proj_bias,
    ln1_gain,
    ln1_bias,
    w_up,
    up_bias,
    w_down,
    down_bias,
    ln2_gain,
    ln2_bias,
    long_group,
    random_blocks,
    out_grad,
):
    n_seq, n_dp = lax.axis_size("seq"), lax.axis_size("dp")
    device, dp = lax.axis_index("seq"), lax.axis_index("dp")
    low = n_seq // 2
    low_bits = low.bit_length() - 1
    place = jnp.stack(
        [device >> low_bits, device & (low - 1), dp & 1, (dp >> 1) & (QUARTERS - 1)]
    ).astype(jnp.int32)
    tok_rows = inputs.reshape(T_DEV, D)
    cotangent = out_grad.reshape(T_DEV, D)
    bias = block_bias(place, long_group, random_blocks, n_seq)
    parts = [tok_rows, swap(tok_rows, "seq", 1)] + [None] * (n_seq - 2)
    step = low
    while step > 1:
        for j in range(0, n_seq, 2 * step):
            parts[j + step] = swap(parts[j], "seq", step)
        step //= 2
    query, *near = project(parts[:2], w_key, w_value, value_bias, w_query, query_bias)
    *parts[2::2], bias, query = lax.optimization_barrier((*parts[2::2], bias, query))
    for j in range(2, n_seq, 2):
        parts[j + 1] = swap(parts[j], "seq", 1)
    cotangent_partner = swap(cotangent, "seq", low)
    vectors = (proj_bias, ln1_gain, ln1_bias, down_bias, ln2_gain, ln2_bias)
    packed = jnp.concatenate([jnp.pad(vector, (0, PACK - D)) for vector in vectors] + [up_bias])
    bias, packed = lax.optimization_barrier((bias, packed))
    weights = (w_proj, w_up, w_down, packed)

    far = [project([part], w_key, w_value, value_bias) for part in parts[2:]]
    keys = [near[0], near[2]] + [pair[0] for pair in far]
    values = [near[1], near[3]] + [pair[1] for pair in far]
    mixed, lse = attn_fwd(query, bias, keys, values)
    mixed_partner = swap(mixed, "seq", low)
    own = after_attention(tok_rows, mixed, cotangent, weights, True)
    mixed_partner, own["d_attn"] = lax.optimization_barrier((mixed_partner, own["d_attn"]))
    other = after_attention(parts[low], mixed_partner, cotangent_partner, weights, False)
    down_terms = half_share_grads(
        place,
        [(own["hidden"], own["d_branch"], other["hidden"], other["d_branch"])],
        n_seq,
        "grads_down",
    )
    up_terms = half_share_grads(
        place,
        [
            (own["normed_low"], own["d_pre"], other["normed_low"], other["d_pre"]),
            (mixed, own["d_attn"], mixed_partner, other["d_attn"]),
        ],
        n_seq,
        "grads_up_proj",
    )
    order = Order()
    low_masks = [1 << i for i in reversed(range(n_seq.bit_length() - 2))]
    seq_masks = [1] + [1 << i for i in reversed(range(1, n_seq.bit_length() - 1))]
    down = halves_first(order, *down_terms, low_masks)
    next(down)
    up = columns_first(order, *up_terms, low_masks)
    next(up)
    for _ in low_masks[:2]:
        next(up)
        ups = order.last
        next(down)
        order.mark(*order.last, *ups)
    (d_mixed,) = order.after(own["d_mixed"])
    d_query, d_key, d_value = attn_bwd(query, bias, keys, values, d_mixed, lse)
    *qkv_terms, small = full_share_grads(place, parts, d_query, d_key, d_value, own["sums"])
    qkv = both_first(order, *qkv_terms, seq_masks)
    next(qkv)
    next(up)
    next(down)
    d_key, d_value = order.after(d_key, d_value)
    token_parts = token_terms(d_key, d_value, w_key, w_value, small, n_seq)
    tail = token_chain(order, *token_parts, small, seq_masks)
    next(tail)
    next(qkv)

    square = (D // n_seq, D)
    chains = dict(D=down, U=up, C=qkv, T=tail)
    plans = dict(D=[(FF // n_seq, D)], U=[(D // n_seq, FF), square], C=[square] * 3)
    results = {}
    for name in STEPS:
        try:
            next(chains[name])
        except StopIteration as stop:
            if name == "T":
                total, small = stop.value
                results[name] = [own["d_resid1"] + 0.125 * dot(d_query, w_query, NT) + total]
            else:
                results[name] = assemble(place, stop.value, plans[name], "assemble_" + name)
            order.mark(*order.last, results[name][0])
    (grad_down,), (grad_up, grad_proj) = results["D"], results["U"]
    grad_query, grad_key, grad_value = results["C"]
    (input_grad,) = results["T"]
    small = small.reshape(-1)
    up_end = 5 * D + FF
    return (
        own["layer_out"].reshape(1, T_DEV, D),
        input_grad.reshape(1, T_DEV, D),
        grad_query,
        grad_key,
        grad_value,
        grad_proj,
        grad_up,
        grad_down,
        small[0:D],
        small[D : 2 * D],
        small[2 * D : 3 * D],
        small[3 * D : 4 * D],
        small[4 * D : 5 * D],
        small[5 * D : up_end],
        small[up_end : up_end + D],
        small[up_end + D : up_end + 2 * D],
        small[up_end + 2 * D : up_end + 3 * D],
    )


def solution(mesh):
    tokens = P("dp", "seq", None)
    return jax.shard_map(
        on_device,
        mesh=mesh,
        in_specs=(tokens,) + (P(),) * 15 + (P("dp"), tokens, tokens),
        out_specs=(tokens, tokens) + (P("seq", None),) * 6 + (P(),) * 9,
        check_vma=False,
    )
```
